128 devices in a mesh: fsdp: 8 (over z_hi, y), seq: 16 (over x, z_lo, core).
Axes of the slice: x: 4, y: 4, z: 4 (z_hi: 2, z_lo: 2; z = z_hi * 2 + z_lo), core: 2. Of those that a mesh axis runs over, the one named last changes fastest.
Arguments:
- tokens: bfloat16 [16384, 1024], P(('fsdp', 'seq')), may hold values from -6 to 6
- gain_mix: bfloat16 [1024], P(('fsdp', 'seq')), may hold values from 0.5 to 1.5
- in_weight: bfloat16 [1024, 3072], P(('fsdp', 'seq')), may hold values from -0.1875 to 0.1875
- conv_weight: bfloat16 [3, 1024], P(None, ('fsdp', 'seq')), may hold values from -3 to 3
- out_weight: bfloat16 [1024, 1024], P(('fsdp', 'seq')), may hold values from -0.1875 to 0.1875
- gain_ffn: bfloat16 [1024], P(('fsdp', 'seq')), may hold values from 0.5 to 1.5
- gate_weight: bfloat16 [1024, 4608], P(('fsdp', 'seq')), may hold values from -0.1875 to 0.1875
- up_weight: bfloat16 [1024, 4608], P(('fsdp', 'seq')), may hold values from -0.1875 to 0.1875
- down_weight: bfloat16 [4608, 1024], P(None, ('fsdp', 'seq')), may hold values from -0.09375 to 0.09375
- live_counts: int32 [8, 16], P('fsdp', 'seq'), may hold values from 64 to 128, as said below
- positions: int32 [16384], P(('fsdp', 'seq')), may hold values from 0 to 2, as said below
- cotangent: bfloat16 [16384, 1024], P(('fsdp', 'seq')), may hold values from -24 to 24
Outputs:
- mixed_out: bfloat16 [16384, 1024], P(('fsdp', 'seq'))
- grad_tokens: bfloat16 [16384, 1024], P(('fsdp', 'seq'))
- grad_gain_mix: float32 [1024], P(('fsdp', 'seq'))
- grad_in: float32 [1024, 3072], P(('fsdp', 'seq'))
- grad_conv: float32 [3, 1024], P(None, ('fsdp', 'seq'))
- grad_out: float32 [1024, 1024], P(('fsdp', 'seq'))
- grad_gain_ffn: float32 [1024], P(('fsdp', 'seq'))
- grad_gate: float32 [1024, 4608], P(('fsdp', 'seq'))
- grad_up: float32 [1024, 4608], P(('fsdp', 'seq'))
- grad_down: float32 [4608, 1024], P(None, ('fsdp', 'seq'))
The draws below stay inside these ranges and needn't reach their ends.
Inputs may be any that keep to these rules, and one draw needn't show every extreme that they name: `live_counts`: the live tokens of a device fill the first slots of its block of 128; the other slots are padding. In every draw some device of each fsdp index has all 128 slots live. `positions`: each live token's index within its sequence, capped at 2; 0 at a sequence's first token and on padding slots. Sequences run through the live tokens of one fsdp index in order of seq and slot and never cross fsdp indices. In every draw one sequence of each fsdp index holds tokens of its first and of its last seq device.
All inputs are finite; a program needn't handle non-finite values.
Results may differ from the reference program's by a relative error of at most 0.038.
Values may be sent and summed in bfloat16 or wider, within the bound.
A program may use at most 128 MiB of HBM per device.

```python
import jax
import jax.numpy as jnp
from jax import lax

D = 1024
FF = 4608
CONV = 3
TOK_DEV = 128
TOKENS = 16384
N_FSDP = 8
N_SEQ = 16


def live_table(key):
    key_counts, key_full = jax.random.split(key)
    counts = jax.random.randint(key_counts, (N_FSDP, N_SEQ), TOK_DEV // 2, TOK_DEV + 1)
    full_at = jax.random.randint(key_full, (N_FSDP, 1), 0, N_SEQ)
    columns = jnp.arange(N_SEQ, dtype=jnp.int32)[None, :]
    return jnp.where(columns == full_at, TOK_DEV, counts).astype(jnp.int32)


def draw_live_counts(key, part):
    return live_table(key)


def draw_positions(key, part):
    counts = live_table(key)
    key = jax.random.fold_in(key, 7)
    key_a, key_c, key_b, key_e = jax.random.split(key, 4)
    slots = jnp.arange(TOK_DEV, dtype=jnp.int32)[None, None, :]
    live = slots < counts[:, :, None]
    device_start = jnp.cumsum(counts, axis=1) - counts
    place = device_start[:, :, None] + slots
    total = jnp.sum(counts, axis=1)
    cut_a = jax.random.randint(key_a, (N_FSDP,), 1, counts[:, 0] - 1)
    cut_c = jax.random.randint(key_c, (N_FSDP,), 0, cut_a)
    cut_b = jax.random.randint(key_b, (N_FSDP,), 1, counts[:, -1] - 1)
    finish = total - cut_b
    cut_e = jax.random.randint(key_e, (N_FSDP,), finish, total)
    starts = jnp.stack([jnp.zeros_like(cut_a), cut_c, cut_a, finish, cut_e], axis=1)
    starts = starts[:, None, None, :]
    begin = jnp.max(jnp.where(starts <= place[..., None], starts, 0), axis=-1)
    offset = jnp.where(live, jnp.minimum(place - begin, CONV - 1), 0)
    return offset.reshape(-1).astype(jnp.int32)


def with_spikes(array, key, source, target, shards_of, factor):
    owner, partner = [(jnp.arange(array.shape[dim]) // (array.shape[dim] // shards_of)).reshape([-1 if axis == dim else 1 for axis in range(array.ndim)]) for dim in (source, target)]
    chosen = jax.random.permutation(key, shards_of)[partner]
    strong = (owner == chosen) | (owner == (partner + shards_of // 2) % shards_of)
    return jnp.where(strong, factor * array, array)


def shard_levels(rng, extent, cuts, low, top_value):
    level, own = 1.0, jax.random.fold_in(rng, 6)
    for position, blocks in cuts:
        steps = jnp.exp(jax.random.uniform(jax.random.fold_in(own, position), (blocks,), jnp.float32, low / len(cuts), top_value / len(cuts)))
        level = level * jnp.repeat(steps, extent[position] // blocks).reshape([-1 if axis == position else 1 for axis in range(len(extent))])
    return level


def bell_draw(stream_key, extent, deviation, limit, cuts=(), held_as=jnp.bfloat16):
    array = jax.random.normal(stream_key, extent, jnp.float32) * deviation
    if len(cuts) > 0:
        array = shard_levels(stream_key, extent, cuts, -0.22, 0.18) * array
    return jnp.clip(array, min=-limit, max=limit).astype(held_as)


def noise_with(own_key, shape, scale, most, shards, heavy, kind=jnp.bfloat16):
    drawn = scale * jax.random.normal(own_key, shape, jnp.float32)
    if shards:
        drawn = drawn * shard_levels(own_key, shape, shards, -0.22, 0.18)
    return jnp.clip(with_spikes(drawn, jax.random.fold_in(own_key, 3), *heavy), -most, most).astype(kind)


def setup_inputs(seed: int = 0) -> dict:
    seeds = jax.random.split(jax.random.key(seed), 13)
    return {
        "tokens": bell_draw(seeds[0], (TOKENS, D), 1.0, 6.0, ((0, 128),)),
        "gain_mix": jnp.clip(1.0 + 0.1 * jax.random.normal(seeds[1], (D,), jnp.float32), 0.5, 1.5).astype(jnp.bfloat16),
        "in_weight": bell_draw(seeds[2], (D, 3 * D), D ** -0.5, 0.1875, ((0, 128),)),
        "conv_weight": bell_draw(seeds[3], (CONV, D), 0.6, 3.0, ((1, 128),)),
        "out_weight": bell_draw(seeds[4], (D, D), D ** -0.5, 0.1875, ((0, 128),)),
        "gain_ffn": jnp.clip(1.0 + 0.1 * jax.random.normal(seeds[5], (D,), jnp.float32), 0.5, 1.5).astype(jnp.bfloat16),
        "gate_weight": bell_draw(seeds[6], (D, FF), D ** -0.5, 0.1875, ((0, 128),)),
        "up_weight": bell_draw(seeds[7], (D, FF), D ** -0.5, 0.1875, ((0, 128),)),
        "down_weight": bell_draw(seeds[8], (FF, D), FF ** -0.5, 0.09375, ((1, 128),)),
        "live_counts": draw_live_counts(jax.random.fold_in(seeds[12], 71), 0),
        "positions": draw_positions(jax.random.fold_in(seeds[12], 71), 0),
        "cotangent": noise_with(seeds[11], (TOKENS, D), 1.0, 24.0, ((0, 128),), (0, 1, 128, 5.5)),
    }


EPS = 1e-05

@jax.custom_vjp
def low(v):
    return lax.optimization_barrier(v.astype(jnp.bfloat16)).astype(jnp.float32)

@jax.custom_vjp
def low_back(v):
    return v

def low_keep(v):
    return (low(v), None)

def low_pass(kept, grad):
    return (grad,)

def back_keep(v):
    return (v, None)

def back_low(kept, grad):
    return (low(grad),)
low.defvjp(low_keep, low_pass)
low_back.defvjp(back_keep, back_low)

def matmul_high(left, right):
    return jnp.dot(left, right, precision=lax.Precision.HIGHEST)

def norm_rows(values, gain):
    return values * lax.rsqrt(lax.optimization_barrier(jnp.mean(values * values, axis=-1, keepdims=True)) + EPS) * gain

def stream_block(params, inputs):
    gain_mix, in_weight, conv_weight, out_weight, gain_ffn, gate_weight, up_weight, down_weight = params
    stream, counts, places = inputs
    total_rows = stream.shape[0]
    slots = jnp.arange(total_rows, dtype=jnp.int32)
    owners = slots // TOK_DEV
    keep_rows = (slots % TOK_DEV < counts[owners]).astype(jnp.float32)[:, None]
    normed = low(norm_rows(stream, gain_mix))
    projected = low_back(matmul_high(normed, in_weight))
    b_part = projected[:, :D]
    c_part = projected[:, D:2 * D]
    v_part = projected[:, 2 * D:]
    mixed = b_part * v_part
    blocks = mixed.reshape(N_SEQ, TOK_DEV, D)
    picks = counts[:, None] - 2 + jnp.arange(2, dtype=jnp.int32)[None, :]
    tails = jnp.take_along_axis(blocks, picks[:, :, None], axis=1)
    before = jnp.concatenate([jnp.zeros((1, 2, D), jnp.float32), tails[:-1]], axis=0)
    extended = jnp.concatenate([before, blocks], axis=1)
    one_back = extended[:, 1:-1].reshape(total_rows, D)
    two_back = extended[:, :-2].reshape(total_rows, D)
    first_ok = (places >= 1).astype(jnp.float32)[:, None]
    second_ok = (places >= 2).astype(jnp.float32)[:, None]
    conv = conv_weight[0] * mixed + first_ok * conv_weight[1] * one_back + second_ok * conv_weight[2] * two_back
    gated = low(c_part * conv)
    branch = low_back(matmul_high(gated, out_weight))
    resid = stream + branch
    normed_two = low(norm_rows(resid, gain_ffn))
    gate = low_back(matmul_high(normed_two, gate_weight))
    upper = low_back(matmul_high(normed_two, up_weight))
    active = low(jax.nn.silu(gate) * upper)
    ffn_out = low_back(matmul_high(active, down_weight))
    return keep_rows * (resid + ffn_out)

def reference(tokens, gain_mix, in_weight, conv_weight, out_weight, gain_ffn, gate_weight, up_weight, down_weight, live_counts, positions, cotangent):
    params = (gain_mix.astype(jnp.float32), in_weight.astype(jnp.float32), conv_weight.astype(jnp.float32), out_weight.astype(jnp.float32), gain_ffn.astype(jnp.float32), gate_weight.astype(jnp.float32), up_weight.astype(jnp.float32), down_weight.astype(jnp.float32))
    streams = tokens.astype(jnp.float32).reshape(N_FSDP, N_SEQ * TOK_DEV, D)
    places = positions.reshape(N_FSDP, N_SEQ * TOK_DEV)
    step_block = jax.checkpoint(stream_block)

    def forward(weights, inputs):

        def scan_step(carry, pieces):
            return (carry, step_block(weights, pieces))
        _, results = lax.scan(scan_step, None, (inputs, live_counts, places))
        return results
    outputs, pull = jax.vjp(forward, params, streams)
    grads, grad_streams = pull(cotangent.astype(jnp.float32).reshape(N_FSDP, N_SEQ * TOK_DEV, D))
    return (outputs.reshape(TOKENS, D).astype(jnp.bfloat16), grad_streams.reshape(TOKENS, D).astype(jnp.bfloat16), grads[0], grads[1], grads[2], grads[3], grads[4], grads[5], grads[6], grads[7])
```

```python
import jax
import jax.numpy as jnp
from jax import lax
from jax.experimental import pallas as pl
from jax.experimental.pallas import tpu as pltpu
from jax.sharding import PartitionSpec as P

EPS = 1e-05
FLOAT = jnp.float32
HALF = jnp.bfloat16
MESH = pl.DeviceIdType.MESH
LANE = 128
D = 1024
SLAB = 1152
MIX_COLS = 34 * LANE
FFN_COLS = 28 * LANE
MIX_HALF = MIX_COLS // 2
FFN_HALF = FFN_COLS // 2
OWN_COLS = MIX_HALF + 4 * FFN_HALF
MIX_PARTS = ((0, 9), (9, 4), (13, 4))
MIX_GATHER = (("y", "z", "x"), ("z", "x", "y"), ("x", "y", "z"))
MIX_REDUCE = (("x", "z", "y"), ("y", "x", "z"), ("z", "y", "x"))
FFN_PARTS = ((0, 7), (7, 7))
FFN_GATHER = (("y", "z"), ("z", "y"))
FFN_REDUCE = (("y", "z"), ("z", "y"))
GRID = (2, 4, 4, 2)
MIX_LANDING = 4 * 3 * len(MIX_PARTS)
VMEM_LIMIT = 56 * 2**20


class Here:
    def __init__(self):
        fsdp = lax.axis_index("fsdp")
        seq = lax.axis_index("seq")
        self.fsdp, self.seq = fsdp, seq
        self.at = {
            "x": lax.div(seq, 4),
            "y": lax.rem(fsdp, 4),
            "z": lax.div(fsdp, 4) * 2 + lax.rem(lax.div(seq, 2), 2),
        }
        self.core = lax.rem(seq, 2)

    def device(self, core, **moved):
        at = {**self.at, **moved}
        return (
            lax.div(at["z"], 2) * 4 + at["y"],
            (at["x"] * 2 + lax.rem(at["z"], 2)) * 2 + core,
        )

    def ring(self, axis, step):
        return lax.rem(self.at[axis] + (step + 4) % 4, 4)

    def beside(self, axis, step):
        return self.device(self.core, **{axis: self.ring(axis, step)})

    def twin(self):
        return self.device(1 - self.core)

    def along(self, step):
        return (self.fsdp, lax.rem(self.seq + (step + 16) % 16, 16))


def greet(devices):
    barrier = pltpu.get_barrier_semaphore()
    for device in devices:
        pl.semaphore_signal(barrier, inc=1, device_id=device, device_id_type=MESH)
    pl.semaphore_wait(barrier, len(devices))


class Mail:
    def __init__(self, send, recv):
        self.send, self.recv, self.posted = send, recv, []

    def post(self, src, dst, device):
        place = len(self.posted)
        copy = pltpu.make_async_remote_copy(
            src_ref=src,
            dst_ref=dst,
            send_sem=self.send.at[place],
            recv_sem=self.recv.at[place],
            device_id=device,
            device_id_type=MESH,
        )
        copy.start()
        self.posted.append(copy)
        return copy

    def close(self):
        for copy in self.posted:
            copy.wait_send()


def cut(start, count):
    return pl.ds(pl.multiple_of(start, LANE), count)


def blocks(ref, at, cols):
    whole = slice(None)
    z = at["z"]
    high, low = (whole, whole) if z is None else (lax.div(z, 2), lax.rem(z, 2))
    y = whole if at["y"] is None else at["y"]
    x = whole if at["x"] is None else at["x"]
    return ref.at[high, y, x, low, :, cols]


class RingGather:
    def __init__(self, here, mail, axis, pick):
        self.here, self.mail, self.axis, self.pick = here, mail, axis, pick

    def start(self, source=None):
        here, axis = self.here, self.axis
        own = self.pick(here.at[axis], None)
        source = own if source is None else source
        self.to_up = self.mail.post(source, own, here.beside(axis, 1))
        self.to_down = self.mail.post(source, own, here.beside(axis, -1))

    def relay(self):
        here, axis = self.here, self.axis
        self.to_up.wait_recv()
        first = self.pick(here.ring(axis, -1), 0)
        self.far_up = self.mail.post(first, first, here.beside(axis, 1))
        self.to_down.wait_recv()
        second = self.pick(here.ring(axis, 1), 1)
        self.far_down = self.mail.post(second, second, here.beside(axis, -1))

    def finish(self):
        self.far_up.wait_recv()
        self.far_down.wait_recv()


class RingReduce:
    def __init__(self, here, mail, axis, pick, near, far):
        self.here, self.mail, self.axis, self.pick = here, mail, axis, pick
        self.near, self.far = near, far

    def start(self):
        here, axis = self.here, self.axis
        away = here.ring(axis, 2)
        self.far_up = self.mail.post(self.pick(away, 0), self.far[0], here.beside(axis, 1))
        self.far_down = self.mail.post(self.pick(away, 1), self.far[1], here.beside(axis, -1))

    def relay(self):
        here, axis = self.here, self.axis
        above, below = here.ring(axis, 1), here.ring(axis, -1)
        self.far_up.wait_recv()
        add_into(self.pick(above, 0), self.far[0])
        self.to_up = self.mail.post(self.pick(above, None), self.near[0], here.beside(axis, 1))
        self.far_down.wait_recv()
        add_into(self.pick(below, 1), self.far[1])
        self.to_down = self.mail.post(self.pick(below, None), self.near[1], here.beside(axis, -1))

    def finish(self):
        self.to_up.wait_recv()
        self.to_down.wait_recv()
        own = self.pick(self.here.at[self.axis], None)
        add_into(own, self.near[0], self.near[1])


def add_into(target, *terms):
    total = target[...].astype(FLOAT)
    for term in terms:
        total = total + term[...].astype(FLOAT)
    target[...] = total.astype(target.dtype)


def column_pick(ref, fixed, axis, start, chunks):
    split = (chunks + 1) // 2

    def pick(place, half):
        first, count = {None: (0, chunks), 0: (0, split), 1: (split, chunks - split)}[half]
        return blocks(ref, {**fixed, axis: place}, cut(start + first * LANE, count * LANE))

    return pick


def row_pick(ref):
    def pick(place, half):
        rows = ref.shape[-2]
        part = {None: slice(None), 0: pl.ds(0, rows // 2), 1: pl.ds(rows // 2, rows // 2)}[half]
        return ref.at[place, part]

    return pick


def gather_rings(here, mail, ref, base, parts, orders, stage):
    rings = []
    for (first, chunks), order in zip(parts, orders):
        fixed = dict(here.at)
        for axis in ("x", "y", "z"):
            if axis not in order or axis in order[:stage]:
                fixed[axis] = None
        pick = column_pick(ref, fixed, order[stage], base + first * LANE, chunks)
        rings.append(RingGather(here, mail, order[stage], pick))
    return rings


def run_rings(rings):
    for ring in rings:
        ring.start()
    for ring in rings:
        ring.relay()
    for ring in rings:
        ring.finish()


def run_last(here, mail, rings):
    def swap(ring, step):
        piece = ring.pick(here.ring(ring.axis, step), None)
        return mail.post(piece, piece, here.twin())

    swaps = []
    for ring in rings:
        ring.start()
    for ring in rings:
        swaps.append(swap(ring, 0))
    for ring in rings:
        ring.relay()
    for ring in rings:
        swaps += [swap(ring, 1), swap(ring, -1)]
    for ring in rings:
        ring.finish()
        swaps.append(swap(ring, 2))
    for copy in swaps:
        copy.wait_recv()


def near_list(here, axes):
    return [here.beside(axis, step) for axis in axes for step in (1, -1)]


def gather_kernel(own, tail, back, mix, ffn, backs, halo, mate, full, send, recv, local_sem):
    here = Here()
    mail = Mail(send, recv)
    x = here.at["x"]
    keep_back = pltpu.make_async_copy(back, backs.at[x], local_sem.at[0])
    keep_back.start()
    greet(
        near_list(here, ("x", "y", "z"))
        + [here.beside("x", 2), here.twin(), here.along(1), here.along(-1)]
    )
    rows = mail.post(own.at[1 - here.core], mate, here.twin())
    stream = RingGather(here, mail, "x", row_pick(backs))
    stream.start(back)
    halo_in = mail.post(tail, halo, here.along(1))
    rows.wait_recv()
    mine = lax.broadcasted_iota(jnp.int32, (16, OWN_COLS), 0) // 8 == here.core
    full[...] = jnp.where(mine, own[here.core].astype(FLOAT), mate[...].astype(FLOAT)).astype(HALF)

    mix_base, ffn_base = here.core * MIX_HALF, here.core * FFN_HALF
    ffn_own = blocks(ffn, here.at, cut(ffn_base, FFN_HALF))

    def slab(place):
        return full.at[:, cut(MIX_HALF + place * FFN_HALF, FFN_HALF)]

    rings = gather_rings(here, mail, mix, mix_base, MIX_PARTS, MIX_GATHER, 0)
    for ring, (first, chunks) in zip(rings, MIX_PARTS):
        ring.start(full.at[:, first * LANE : (first + chunks) * LANE])
    slabs = [
        mail.post(slab(here.ring("x", step)), ffn_own, here.beside("x", step)) for step in (1, 3, 2)
    ]
    keeps = [
        pltpu.make_async_copy(
            full.at[:, 0:MIX_HALF], blocks(mix, here.at, cut(mix_base, MIX_HALF)), local_sem.at[1]
        ),
        pltpu.make_async_copy(slab(x), ffn_own, local_sem.at[2]),
    ]
    for copy in keeps:
        copy.start()
    for ring in rings:
        ring.relay()
    for ring in rings:
        ring.finish()
    for copy in keeps:
        copy.wait()
    for copy in slabs:
        copy.wait_recv()
    rings = gather_rings(here, mail, mix, mix_base, MIX_PARTS, MIX_GATHER, 1)
    rings += gather_rings(here, mail, ffn, ffn_base, FFN_PARTS, FFN_GATHER, 0)
    run_rings(rings)
    stream.relay()
    rings = gather_rings(here, mail, mix, mix_base, MIX_PARTS, MIX_GATHER, 2)
    rings += gather_rings(here, mail, ffn, ffn_base, FFN_PARTS, FFN_GATHER, 1)
    run_last(here, mail, rings)
    stream.finish()
    keep_back.wait()
    halo_in.wait_recv()
    mail.close()


def gather_stream_kernel(rows, stream, send, recv):
    here = Here()
    mail = Mail(send, recv)
    greet(near_list(here, ("x",)))
    ring = RingGather(here, mail, "x", row_pick(stream))
    ring.start(rows)
    stream[here.at["x"]] = rows[...]
    ring.relay()
    ring.finish()
    mail.close()


def reduce_stream_kernel(sums, owned, work, near_a, near_b, far_a, far_b, send, recv, local_sem):
    here = Here()
    mail = Mail(send, recv)
    load = pltpu.make_async_copy(sums, work, local_sem.at[0])
    load.start()
    greet(near_list(here, ("x",)))
    load.wait()
    ring = RingReduce(here, mail, "x", row_pick(work), (near_a, near_b), (far_a, far_b))
    ring.start()
    ring.relay()
    ring.finish()
    owned[...] = work[here.at["x"]].astype(FLOAT)
    mail.close()


def reduce_rings(here, mail, ref, parts, orders, near, far, stage):
    rings = []
    for number, ((first, chunks), order) in enumerate(zip(parts, orders)):
        fixed = {"x": None, "y": None, "z": None}
        for axis in order[:stage]:
            fixed[axis] = here.at[axis]
        pick = column_pick(ref, fixed, order[stage], first * LANE, chunks)
        rings.append(
            RingReduce(here, mail, order[stage], pick, near[number][stage], far[number][stage])
        )
    return rings


def landing_shapes(parts, orders):
    shapes = []
    for (_, chunks), order in zip(parts, orders):
        split = (chunks + 1) // 2
        done = []
        for stage in range(len(order)):
            gone = order[: stage + 1]
            lead = ()
            if "z" not in gone:
                lead += (2,)
            if "y" not in gone:
                lead += (4,)
            if "x" not in gone:
                lead += (4,)
            if "z" not in gone:
                lead += (2,)
            for count, copies in ((chunks, 2), (split, 1), (chunks - split, 1)):
                done += [lead + (16, count * LANE)] * copies
        shapes.append(done)
    return shapes


def landing_refs(orders, refs):
    near, far = [], []
    place = 0
    for order in orders:
        near.append([])
        far.append([])
        for _ in order:
            near[-1].append(refs[place : place + 2])
            far[-1].append(refs[place + 2 : place + 4])
            place += 4
    return near, far


def twin_send(here, mail, grads, half, landed):
    other = (1 - here.core) * half
    return mail.post(grads.at[:, :, :, :, :, cut(other, half)], landed, here.twin())


def twin_sum(here, grads, half, landed, total):
    base = here.core * half

    @pl.loop(0, 32)
    def _(index):
        high, y = lax.div(index, 16), lax.rem(lax.div(index, 4), 4)
        x = lax.rem(index, 4)
        for low in range(2):
            total[high, y, x, low] = (
                grads[high, y, x, low, :, cut(base, half)].astype(FLOAT)
                + landed[high, y, x, low].astype(FLOAT)
            ).astype(HALF)


def reduce_kernel(mix, ffn, sums, tail, mix_owned, ffn_owned, tokens, halo, *scratch):
    mix_landed, mix_total, mix_mate, ffn_landed, ffn_total, ffn_rest, ffn_mate, work = scratch[:8]
    *landing, near_a, near_b, far_a, far_b, send, recv, local_sem = scratch[8:]
    mix_near, mix_far = landing_refs(MIX_REDUCE, landing[:MIX_LANDING])
    ffn_near, ffn_far = landing_refs(FFN_REDUCE, landing[MIX_LANDING:])
    here = Here()
    mail = Mail(send, recv)
    x = here.at["x"]
    load = pltpu.make_async_copy(sums, work, local_sem.at[0])
    load.start()
    greet(
        near_list(here, ("x", "y", "z"))
        + [here.beside("x", 2), here.twin(), here.along(1), here.along(-1)]
    )
    mix_twin = twin_send(here, mail, mix, MIX_HALF, mix_landed)
    ffn_twin = twin_send(here, mail, ffn, FFN_HALF, ffn_landed)
    halo_in = mail.post(tail, halo, here.along(-1))
    load.wait()
    stream = RingReduce(here, mail, "x", row_pick(work), (near_a, near_b), (far_a, far_b))
    stream.start()
    mix_twin.wait_recv()
    twin_sum(here, mix, MIX_HALF, mix_landed, mix_total)
    mix_rings = reduce_rings(here, mail, mix_total, MIX_PARTS, MIX_REDUCE, mix_near, mix_far, 0)
    for ring in mix_rings:
        ring.start()
    stream.relay()
    ffn_twin.wait_recv()
    twin_sum(here, ffn, FFN_HALF, ffn_landed, ffn_total)
    ffn_rings = reduce_rings(here, mail, ffn_total, FFN_PARTS, FFN_REDUCE, ffn_near, ffn_far, 0)
    for ring in ffn_rings:
        ring.start()
    for ring in mix_rings + ffn_rings:
        ring.relay()
    for ring in mix_rings + ffn_rings + [stream]:
        ring.finish()
    tokens[...] = work[x].astype(FLOAT)
    run_rings(
        reduce_rings(here, mail, mix_total, MIX_PARTS, MIX_REDUCE, mix_near, mix_far, 1)
        + reduce_rings(here, mail, ffn_total, FFN_PARTS, FFN_REDUCE, ffn_near, ffn_far, 1)
    )
    copies = []
    for step in (1, 3, 2):
        there = here.ring("x", step)
        copies.append(
            mail.post(
                blocks(ffn_total, {**here.at, "x": there}, slice(None)),
                ffn_rest.at[x],
                here.beside("x", step),
            )
        )
    ffn_rest[x] = blocks(ffn_total, here.at, slice(None))[...]
    run_rings(reduce_rings(here, mail, mix_total, MIX_PARTS, MIX_REDUCE, mix_near, mix_far, 2))
    own = blocks(mix_total, here.at, slice(None))
    mix_swap = mail.post(own, mix_mate, here.twin())
    for copy in copies:
        copy.wait_recv()
    ffn_swap = mail.post(ffn_rest, ffn_mate, here.twin())
    mix_owned[:, cut(here.core * MIX_HALF, MIX_HALF)] = own[...].astype(FLOAT)
    ffn_owned[:, :, cut(here.core * FFN_HALF, FFN_HALF)] = ffn_rest[...].astype(FLOAT)
    mix_swap.wait_recv()
    mix_owned[:, cut((1 - here.core) * MIX_HALF, MIX_HALF)] = mix_mate[...].astype(FLOAT)
    ffn_swap.wait_recv()
    ffn_owned[:, :, cut((1 - here.core) * FFN_HALF, FFN_HALF)] = ffn_mate[...].astype(FLOAT)
    halo_in.wait_recv()
    mail.close()


def vmem():
    return pl.BlockSpec(memory_space=pltpu.VMEM)


def anywhere():
    return pl.BlockSpec(memory_space=pl.ANY)


def sems(count):
    return pltpu.SemaphoreType.DMA((count,))


def params(number):
    return pltpu.CompilerParams(
        collective_id=number, has_side_effects=True, vmem_limit_bytes=VMEM_LIMIT
    )


def shape(dims, dtype):
    return jax.ShapeDtypeStruct(dims, dtype)


def gather(own, tail, back):
    return pl.pallas_call(
        gather_kernel,
        out_shape=(
            shape(GRID + (16, MIX_COLS), HALF),
            shape(GRID + (16, FFN_COLS), HALF),
            shape((4, 128, D), HALF),
            shape((16, D), HALF),
        ),
        in_specs=[vmem()] * 3,
        out_specs=(anywhere(), anywhere(), anywhere(), vmem()),
        scratch_shapes=[
            pltpu.VMEM((16, OWN_COLS), HALF),
            pltpu.VMEM((16, OWN_COLS), HALF),
            sems(88),
            sems(88),
            sems(3),
        ],
        compiler_params=params(0),
        name="gather",
    )(own, tail, back)


def gather_stream(rows):
    return pl.pallas_call(
        gather_stream_kernel,
        out_shape=shape((4, 128, D), HALF),
        in_specs=[vmem()],
        out_specs=vmem(),
        scratch_shapes=[sems(4), sems(4)],
        compiler_params=params(1),
        name="gather_stream",
    )(rows)


def reduce_stream(sums):
    return pl.pallas_call(
        reduce_stream_kernel,
        out_shape=shape((128, D), FLOAT),
        in_specs=[anywhere()],
        out_specs=vmem(),
        scratch_shapes=[pltpu.VMEM((4, 128, D), HALF)]
        + [pltpu.VMEM((128, D), HALF)] * 2
        + [pltpu.VMEM((64, D), HALF)] * 2
        + [sems(4), sems(4), sems(1)],
        compiler_params=params(2),
        name="reduce_stream",
    )(sums)


def reduce(mix, ffn, sums, tail):
    landing = [
        pltpu.VMEM(dims, HALF)
        for part in landing_shapes(MIX_PARTS, MIX_REDUCE) + landing_shapes(FFN_PARTS, FFN_REDUCE)
        for dims in part
    ]
    return pl.pallas_call(
        reduce_kernel,
        out_shape=(
            shape((16, MIX_COLS), FLOAT),
            shape((4, 16, FFN_COLS), FLOAT),
            shape((128, D), FLOAT),
            shape((8, D), FLOAT),
        ),
        in_specs=[vmem(), vmem(), anywhere(), vmem()],
        out_specs=(vmem(),) * 4,
        scratch_shapes=[
            pltpu.VMEM(GRID + (16, MIX_HALF), HALF),
            pltpu.VMEM(GRID + (16, MIX_HALF), HALF),
            pltpu.VMEM((16, MIX_HALF), HALF),
            pltpu.VMEM(GRID + (16, FFN_HALF), HALF),
            pltpu.VMEM(GRID + (16, FFN_HALF), HALF),
            pltpu.VMEM((4, 16, FFN_HALF), HALF),
            pltpu.VMEM((4, 16, FFN_HALF), HALF),
            pltpu.VMEM((4, 128, D), HALF),
        ]
        + landing
        + [pltpu.VMEM((128, D), HALF)] * 2
        + [pltpu.VMEM((64, D), HALF)] * 2
        + [sems(72), sems(72), sems(1)],
        compiler_params=params(3),
        name="reduce",
    )(mix, ffn, sums, tail)


def norm_scale(values):
    return lax.rsqrt(jnp.mean(values * values, axis=-1, keepdims=True) + EPS)


def dot(left, right):
    return jnp.dot(left, right, preferred_element_type=FLOAT)


def dot_nt(left, right):
    return jnp.einsum("ta,ba->tb", left, right, preferred_element_type=FLOAT)


def dot_tn(left, right):
    return jnp.einsum("ta,tb->ab", left, right, preferred_element_type=FLOAT)


def norm_back(normal, row_scale, gain_row, upstream):
    weighted = upstream * gain_row
    return row_scale * (
        weighted - normal * jnp.mean(weighted * normal, axis=-1, keepdims=True)
    )


def local(
    tokens,
    gain_mix,
    in_weight,
    conv_weight,
    out_weight,
    gain_ffn,
    gate_weight,
    up_weight,
    down_weight,
    live_counts,
    positions,
    cotangent,
):
    seq = lax.axis_index("seq")
    core = lax.rem(seq, 2)
    count = live_counts[0, 0]
    small = jnp.stack([gain_mix, gain_ffn, conv_weight[0], conv_weight[1], conv_weight[2]], axis=1)
    ffn_rows = [
        weight.reshape(8, 4, SLAB) for weight in (gate_weight, up_weight, jnp.transpose(down_weight))
    ]
    ffn_rows = jnp.concatenate(ffn_rows + [jnp.zeros((8, 4, FFN_COLS - 3 * SLAB), HALF)], axis=2)
    ffn_rows = ffn_rows.reshape(8, 4, 2, FFN_HALF).transpose(2, 0, 1, 3)
    mix_rows = jnp.concatenate(
        [in_weight, out_weight, jnp.pad(small, ((0, 0), (0, MIX_COLS - 4 * D - 5)))], axis=1
    )
    mix_rows = mix_rows.reshape(8, 2, MIX_HALF).transpose(1, 0, 2)
    own = jnp.concatenate([mix_rows, ffn_rows.reshape(2, 8, 4 * FFN_HALF)], axis=2)
    own = jnp.concatenate([own, own], axis=1)
    tail = jnp.pad(lax.dynamic_slice(tokens, (count - 2, 0), (2, D)), ((0, 14), (0, 0)))
    follows = (seq > 0).astype(FLOAT)
    keep = (jnp.arange(128, dtype=jnp.int32) < count).astype(FLOAT)[:, None]
    d_out = keep * cotangent.astype(FLOAT)
    first_ok = (positions >= 1).astype(FLOAT)[:, None]
    second_ok = (positions >= 2).astype(FLOAT)[:, None]

    mix, ffn, backs, halo = gather(own, tail, d_out.astype(HALF))
    mix = mix.reshape(D, MIX_COLS)
    w_in = mix[:, : 3 * D]
    w_out = mix[:, 3 * D : 4 * D]
    small_rows = jnp.transpose(mix[:, 4 * D : 4 * D + 8]).astype(FLOAT)
    gain_one, gain_two = small_rows[0], small_rows[1]
    taps = small_rows[2:5]

    x_all = jnp.concatenate([tokens, halo], axis=0).astype(FLOAT)
    scale_all = norm_scale(x_all)
    unit_all = x_all * scale_all
    normed = (unit_all * gain_one).astype(HALF)
    projected = dot(normed, w_in)
    b_all = projected[:, :D]
    c_part = projected[:128, D : 2 * D]
    v_all = projected[:, 2 * D :]
    mixed_all = b_all * v_all
    mixed = mixed_all[:128]
    extended = jnp.concatenate([follows * mixed_all[128:130], mixed], axis=0)
    one_back = extended[1:129]
    two_back = extended[:128]
    conv = taps[0] * mixed + first_ok * taps[1] * one_back + second_ok * taps[2] * two_back
    gated = (c_part * conv).astype(HALF)
    x_own = tokens.astype(FLOAT)
    resid = x_own + dot(gated, w_out)
    scale_two = norm_scale(resid)
    unit_two = resid * scale_two
    normed_two = (unit_two * gain_two).astype(HALF)

    twos = gather_stream(normed_two)
    ffn = ffn.reshape(D, FFN_COLS)
    w_gate, w_up, w_down = ffn[:, :SLAB], ffn[:, SLAB : 2 * SLAB], ffn[:, 2 * SLAB : 3 * SLAB]
    twos = twos.reshape(512, D)
    backs = backs.reshape(512, D)
    gate = dot(twos, w_gate)
    upper = dot(twos, w_up)
    sig = jax.nn.sigmoid(gate)
    swish = gate * sig
    active = (swish * upper).astype(HALF)
    d_active = dot(backs, w_down)
    d_gate = (d_active * upper * (sig * (1.0 + gate * (1.0 - sig)))).astype(HALF)
    d_upper = (d_active * swish).astype(HALF)
    ffn_sum = dot_nt(active, w_down).astype(HALF)
    two_sum = (dot_nt(d_gate, w_gate) + dot_nt(d_upper, w_up)).astype(HALF)
    ffn_grads = jnp.concatenate(
        [
            dot_tn(twos, d_gate).astype(HALF),
            dot_tn(twos, d_upper).astype(HALF),
            dot_tn(backs, active).astype(HALF),
            jnp.zeros((D, FFN_COLS - 3 * SLAB), HALF),
        ],
        axis=1,
    )
    d_two = reduce_stream(two_sum.reshape(4, 128, D))

    grad_gain_two = jnp.sum(d_two * unit_two, axis=0)
    d_resid = d_out + norm_back(unit_two, scale_two, gain_two, d_two)
    d_branch = d_resid.astype(HALF)
    grad_out = dot_tn(gated, d_branch).astype(HALF)
    d_gated = dot_nt(d_branch, w_out)
    d_c = d_gated * conv
    d_conv = d_gated * c_part
    grad_taps = [
        jnp.sum(d_conv * mixed, axis=0),
        jnp.sum(d_conv * first_ok * one_back, axis=0),
        jnp.sum(d_conv * second_ok * two_back, axis=0),
    ]
    term_one = first_ok * taps[1] * d_conv
    term_two = second_ok * taps[2] * d_conv
    d_ext = jnp.pad(term_one, ((1, 1), (0, 0))) + jnp.pad(term_two, ((0, 2), (0, 0)))
    d_mixed = d_ext[2:] + taps[0] * d_conv
    d_mixed_all = jnp.concatenate(
        [d_mixed, jnp.pad(follows * d_ext[:2], ((0, 14), (0, 0)))], axis=0
    )
    d_projected = jnp.concatenate(
        [d_mixed_all * v_all, jnp.pad(d_c, ((0, 16), (0, 0))), d_mixed_all * b_all], axis=1
    ).astype(HALF)
    grad_in = dot_tn(normed, d_projected).astype(HALF)
    d_normed_all = dot_nt(d_projected, w_in)
    grad_gain_one = jnp.sum(d_normed_all * unit_all, axis=0)
    small_grads = jnp.stack([grad_gain_one, grad_gain_two] + grad_taps, axis=1).astype(HALF)
    mix_grads = jnp.concatenate(
        [grad_in, grad_out, jnp.pad(small_grads, ((0, 0), (0, MIX_COLS - 4 * D - 5)))], axis=1
    )
    owned_mix, owned_ffn, ffn_out, back_rows = reduce(
        mix_grads.reshape(GRID + (16, MIX_COLS)),
        ffn_grads.reshape(GRID + (16, FFN_COLS)),
        ffn_sum.reshape(4, 128, D),
        d_normed_all[128:136],
    )
    mixed_out = (keep * (resid + ffn_out)).astype(HALF)
    slots = jnp.arange(128, dtype=jnp.int32)[:, None]
    d_normed = (
        d_normed_all[:128]
        + (slots == count - 2).astype(FLOAT) * back_rows[0]
        + (slots == count - 1).astype(FLOAT) * back_rows[1]
    )
    d_norm_one = norm_back(unit_all[:128], scale_all[:128], gain_one, d_normed)
    grad_tokens = (d_resid + d_norm_one).astype(HALF)

    mine = lax.dynamic_slice(owned_mix, (8 * core, 0), (8, MIX_COLS))
    ffn_mine = lax.dynamic_slice(owned_ffn, (0, 8 * core, 0), (4, 8, FFN_COLS))
    ffn_mine = jnp.transpose(ffn_mine, (1, 0, 2))
    small_mine = jnp.transpose(mine[:, 4 * D : 4 * D + 5])
    return (
        mixed_out,
        grad_tokens,
        small_mine[0],
        mine[:, : 3 * D],
        small_mine[2:5],
        mine[:, 3 * D : 4 * D],
        small_mine[1],
        ffn_mine[:, :, :SLAB].reshape(8, 4 * SLAB),
        ffn_mine[:, :, SLAB : 2 * SLAB].reshape(8, 4 * SLAB),
        jnp.transpose(ffn_mine[:, :, 2 * SLAB : 3 * SLAB].reshape(8, 4 * SLAB)),
    )


def solution(mesh):
    rows = P(("fsdp", "seq"), None)
    flat = P(("fsdp", "seq"))
    cols = P(None, ("fsdp", "seq"))
    return jax.shard_map(
        local,
        mesh=mesh,
        in_specs=(rows, flat, rows, cols, rows, flat, rows, rows, cols, P("fsdp", "seq"), flat, rows),
        out_specs=(rows, rows, flat, rows, cols, rows, flat, rows, rows, cols),
        check_vma=False,
    )
```

```python
import jax
import jax.numpy as jnp
from jax import lax
from jax.experimental import pallas as pl
from jax.experimental.pallas import tpu as pltpu
from jax.sharding import PartitionSpec as P

EPS = 1e-05
FLOAT = jnp.float32
HALF = jnp.bfloat16
MESH = pl.DeviceIdType.MESH
LANE = 128
D = 1024
SLAB = 1152
MIX_COLS = 34 * LANE
FFN_COLS = 28 * LANE
MIX_HALF = MIX_COLS // 2
FFN_HALF = FFN_COLS // 2
OWN_COLS = MIX_HALF + 4 * FFN_HALF
HALF_D = D // 2
OUT_AT = 3 * HALF_D
SMALL_AT = 4 * HALF_D
TILE = 256
TOK = 128
ALL = TOK + 16
MIX_PARTS = ((0, 9), (9, 4), (13, 4))
MIX_GATHER = (("y", "z", "x"), ("z", "x", "y"), ("x", "y", "z"))
MIX_REDUCE = (("x", "z", "y"), ("y", "x", "z"), ("z", "y", "x"))
FFN_PARTS = ((0, 7), (7, 7))
FFN_GATHER = (("y", "z"), ("z", "y"))
FFN_REDUCE = (("y", "z"), ("z", "y"))
GRID = (2, 4, 4, 2)
MIX_LANDING = 4 * 3 * len(MIX_PARTS)
VMEM_LIMIT = 60 * 2**20


class Here:
    def __init__(self):
        fsdp = lax.axis_index("fsdp")
        seq = lax.axis_index("seq")
        self.fsdp, self.seq = fsdp, seq
        self.at = {
            "x": lax.div(seq, 4),
            "y": lax.rem(fsdp, 4),
            "z": lax.div(fsdp, 4) * 2 + lax.rem(lax.div(seq, 2), 2),
        }
        self.core = lax.rem(seq, 2)

    def device(self, core, **moved):
        at = {**self.at, **moved}
        return (
            lax.div(at["z"], 2) * 4 + at["y"],
            (at["x"] * 2 + lax.rem(at["z"], 2)) * 2 + core,
        )

    def ring(self, axis, step):
        return lax.rem(self.at[axis] + (step + 4) % 4, 4)

    def beside(self, axis, step):
        return self.device(self.core, **{axis: self.ring(axis, step)})

    def twin(self):
        return self.device(1 - self.core)

    def along(self, step):
        return (self.fsdp, lax.rem(self.seq + (step + 16) % 16, 16))


def greet(devices):
    barrier = pltpu.get_barrier_semaphore()
    for device in devices:
        pl.semaphore_signal(barrier, inc=1, device_id=device, device_id_type=MESH)
    pl.semaphore_wait(barrier, len(devices))


class Mail:
    def __init__(self, send, recv):
        self.send, self.recv, self.posted = send, recv, []

    def post(self, src, dst, device):
        place = len(self.posted)
        copy = pltpu.make_async_remote_copy(
            src_ref=src,
            dst_ref=dst,
            send_sem=self.send.at[place],
            recv_sem=self.recv.at[place],
            device_id=device,
            device_id_type=MESH,
        )
        copy.start()
        self.posted.append(copy)
        return copy

    def close(self):
        for copy in self.posted:
            copy.wait_send()


def cut(start, count):
    return pl.ds(pl.multiple_of(start, LANE), count)


def blocks(ref, at, cols):
    whole = slice(None)
    z = at["z"]
    high, low = (whole, whole) if z is None else (lax.div(z, 2), lax.rem(z, 2))
    y = whole if at["y"] is None else at["y"]
    x = whole if at["x"] is None else at["x"]
    return ref.at[high, y, x, low, :, cols]


class RingGather:
    def __init__(self, here, mail, axis, pick):
        self.here, self.mail, self.axis, self.pick = here, mail, axis, pick

    def start(self, source=None):
        here, axis = self.here, self.axis
        own = self.pick(here.at[axis], None)
        source = own if source is None else source
        self.to_up = self.mail.post(source, own, here.beside(axis, 1))
        self.to_down = self.mail.post(source, own, here.beside(axis, -1))

    def relay(self):
        here, axis = self.here, self.axis
        self.to_up.wait_recv()
        first = self.pick(here.ring(axis, -1), 0)
        self.far_up = self.mail.post(first, first, here.beside(axis, 1))
        self.to_down.wait_recv()
        second = self.pick(here.ring(axis, 1), 1)
        self.far_down = self.mail.post(second, second, here.beside(axis, -1))

    def finish(self):
        self.far_up.wait_recv()
        self.far_down.wait_recv()


class RingReduce:
    def __init__(self, here, mail, axis, pick, near, far):
        self.here, self.mail, self.axis, self.pick = here, mail, axis, pick
        self.near, self.far = near, far

    def start(self):
        here, axis = self.here, self.axis
        away = here.ring(axis, 2)
        self.far_up = self.mail.post(self.pick(away, 0), self.far[0], here.beside(axis, 1))
        self.far_down = self.mail.post(self.pick(away, 1), self.far[1], here.beside(axis, -1))

    def relay(self):
        here, axis = self.here, self.axis
        above, below = here.ring(axis, 1), here.ring(axis, -1)
        self.far_up.wait_recv()
        add_into(self.pick(above, 0), self.far[0])
        self.to_up = self.mail.post(self.pick(above, None), self.near[0], here.beside(axis, 1))
        self.far_down.wait_recv()
        add_into(self.pick(below, 1), self.far[1])
        self.to_down = self.mail.post(self.pick(below, None), self.near[1], here.beside(axis, -1))

    def finish(self):
        self.to_up.wait_recv()
        self.to_down.wait_recv()
        own = self.pick(self.here.at[self.axis], None)
        add_into(own, self.near[0], self.near[1])


def add_into(target, *terms):
    total = target[...].astype(FLOAT)
    for term in terms:
        total = total + term[...].astype(FLOAT)
    target[...] = total.astype(target.dtype)


def column_pick(ref, fixed, axis, start, chunks):
    split = (chunks + 1) // 2

    def pick(place, half):
        first, count = {None: (0, chunks), 0: (0, split), 1: (split, chunks - split)}[half]
        return blocks(ref, {**fixed, axis: place}, cut(start + first * LANE, count * LANE))

    return pick


def row_pick(ref):
    def pick(place, half):
        rows = ref.shape[-2]
        part = {None: slice(None), 0: pl.ds(0, rows // 2), 1: pl.ds(rows // 2, rows // 2)}[half]
        return ref.at[place, part]

    return pick


def gather_rings(here, mail, ref, base, parts, orders, stage):
    rings = []
    for (first, chunks), order in zip(parts, orders):
        fixed = dict(here.at)
        for axis in ("x", "y", "z"):
            if axis not in order or axis in order[:stage]:
                fixed[axis] = None
        pick = column_pick(ref, fixed, order[stage], base + first * LANE, chunks)
        rings.append(RingGather(here, mail, order[stage], pick))
    return rings


def start_all(rings):
    for ring in rings:
        ring.start()


def relay_all(rings):
    for ring in rings:
        ring.relay()


def finish_all(rings):
    for ring in rings:
        ring.finish()


def run_rings(rings):
    start_all(rings)
    relay_all(rings)
    finish_all(rings)


def swap_pieces(here, mail, rings, steps):
    copies = []
    for ring in rings:
        for step in steps:
            piece = ring.pick(here.ring(ring.axis, step), None)
            copies.append(mail.post(piece, piece, here.twin()))
    return copies


def wait_all(copies):
    for copy in copies:
        copy.wait_recv()


def near_list(here, axes):
    return [here.beside(axis, step) for axis in axes for step in (1, -1)]


def mat(ref, cols):
    block = ref[:, :, :, :, :, cols]
    return block.reshape(D, block.shape[-1])


def mat_rows(ref, tile, cols):
    block = ref[lax.div(tile, 2), pl.ds(lax.rem(tile, 2) * 2, 2), :, :, :, cols]
    return block.reshape(TILE, block.shape[-1])


def mix_cols(tile, which):
    return cut(lax.div(tile, 2) * MIX_HALF + which * HALF_D + lax.rem(tile, 2) * TILE, TILE)


def dot(left, right):
    return jnp.dot(left, right, preferred_element_type=FLOAT)


def dot_nt(left, right):
    return lax.dot_general(
        left, right, (((1,), (1,)), ((), ())), preferred_element_type=FLOAT
    )


def norm_scale(values):
    return lax.rsqrt(jnp.mean(values * values, axis=-1, keepdims=True) + EPS)


def norm_back(normal, row_scale, gain_row, upstream):
    weighted = upstream * gain_row
    return row_scale * (
        weighted - normal * jnp.mean(weighted * normal, axis=-1, keepdims=True)
    )


def row_index(rows, cols):
    return lax.broadcasted_iota(jnp.int32, (rows, cols), 0)


def conv_terms(mixed, halo):
    rows = row_index(TOK, mixed.shape[1])
    one = pltpu.roll(mixed, 1, 0)
    two = pltpu.roll(mixed, 2, 0)
    one = jnp.where(rows == 0, halo[1:2], one)
    two = jnp.where(rows == 0, halo[0:1], jnp.where(rows == 1, halo[1:2], two))
    return one, two


def follows_of(here):
    return jnp.minimum(here.seq, 1).astype(FLOAT)


def mixer_forward(here, tokens, halo, flags, mix, proj, normed, gated, resid, rows, two):
    small = jnp.transpose(mat(mix, slice(SMALL_AT, SMALL_AT + LANE)).astype(FLOAT))
    rows[...] = small[0:8]
    gain = rows[0:1]
    x = tokens[...].astype(FLOAT)
    normed[0:TOK] = (x * norm_scale(x) * gain).astype(HALF)
    before = halo[...].astype(FLOAT)
    normed[TOK:ALL] = (before * norm_scale(before) * gain).astype(HALF)
    follows = follows_of(here)
    first_ok, second_ok = flags[:, 0:1], flags[:, 1:2]

    @pl.loop(0, D // TILE)
    def _(tile):
        feats = cut(tile * TILE, TILE)
        parts = [dot(normed[...], mat(mix, mix_cols(tile, which))) for which in range(3)]
        for which in range(3):
            proj[which, :, feats] = parts[which]
        mixed = parts[0] * parts[2]
        own = mixed[0:TOK]
        one, second = conv_terms(own, mixed[TOK:ALL] * follows)
        conv = (
            rows[2:3, feats] * own
            + first_ok * rows[3:4, feats] * one
            + second_ok * rows[4:5, feats] * second
        )
        gated[:, feats] = (parts[1][0:TOK] * conv).astype(HALF)

    @pl.loop(0, D // TILE)
    def _(tile):
        feats = cut(tile * TILE, TILE)
        branch = dot(gated[...], mat(mix, mix_cols(tile, 3)))
        resid[:, feats] = tokens[:, feats].astype(FLOAT) + branch

    value = resid[...]
    two[...] = (value * norm_scale(value) * rows[1:2]).astype(HALF)


def forward_kernel(
    own, tail, back, tokens, flags,
    mix_out, ffn, backs, twos, proj, normed, gated, resid, rows, halo,
    mate, full, mix, two, send, recv, local_sem,
):
    here = Here()
    mail = Mail(send, recv)
    x = here.at["x"]
    keep_back = pltpu.make_async_copy(back, backs.at[x], local_sem.at[0])
    keep_back.start()
    greet(
        near_list(here, ("x", "y", "z"))
        + [here.beside("x", 2), here.twin(), here.along(1), here.along(-1)]
    )
    rows_in = mail.post(own.at[1 - here.core], mate, here.twin())
    halo_in = mail.post(tail, halo, here.along(1))
    rows_in.wait_recv()
    mine = lax.broadcasted_iota(jnp.int32, (16, OWN_COLS), 0) // 8 == here.core
    full[...] = jnp.where(mine, own[here.core].astype(FLOAT), mate[...].astype(FLOAT)).astype(HALF)

    mix_base, ffn_base = here.core * MIX_HALF, here.core * FFN_HALF
    ffn_own = blocks(ffn, here.at, cut(ffn_base, FFN_HALF))

    def slab(place):
        return full.at[:, cut(MIX_HALF + place * FFN_HALF, FFN_HALF)]

    rings = gather_rings(here, mail, mix, mix_base, MIX_PARTS, MIX_GATHER, 0)
    for ring, (first, chunks) in zip(rings, MIX_PARTS):
        ring.start(full.at[:, first * LANE : (first + chunks) * LANE])
    slabs = [
        mail.post(slab(here.ring("x", step)), ffn_own, here.beside("x", step)) for step in (1, 3, 2)
    ]
    keep_mix = pltpu.make_async_copy(
        full.at[:, 0:MIX_HALF], blocks(mix, here.at, cut(mix_base, MIX_HALF)), local_sem.at[1]
    )
    keep_slab = pltpu.make_async_copy(slab(x), ffn_own, local_sem.at[2])
    keep_mix.start()
    keep_slab.start()
    relay_all(rings)
    finish_all(rings)
    keep_mix.wait()
    keep_slab.wait()
    wait_all(slabs)
    mix_rings = gather_rings(here, mail, mix, mix_base, MIX_PARTS, MIX_GATHER, 1)
    ffn_rings = gather_rings(here, mail, ffn, ffn_base, FFN_PARTS, FFN_GATHER, 0)
    run_rings(mix_rings + ffn_rings)
    mix_rings = gather_rings(here, mail, mix, mix_base, MIX_PARTS, MIX_GATHER, 2)
    ffn_rings = gather_rings(here, mail, ffn, ffn_base, FFN_PARTS, FFN_GATHER, 1)
    start_all(mix_rings)
    swaps = swap_pieces(here, mail, mix_rings, (0,))
    relay_all(mix_rings)
    swaps += swap_pieces(here, mail, mix_rings, (1, -1))
    start_all(ffn_rings)
    stream = RingGather(here, mail, "x", row_pick(backs))
    stream.start(back)
    finish_all(mix_rings)
    swaps += swap_pieces(here, mail, mix_rings, (2,))
    ffn_swaps = swap_pieces(here, mail, ffn_rings, (0,))
    wait_all(swaps)
    halo_in.wait_recv()
    keep_all = pltpu.make_async_copy(mix, mix_out, local_sem.at[1])
    keep_all.start()
    mixer_forward(here, tokens, halo, flags, mix, proj, normed, gated, resid, rows, two)
    two_ring = RingGather(here, mail, "x", row_pick(twos))
    two_ring.start(two)
    keep_two = pltpu.make_async_copy(two, twos.at[x], local_sem.at[2])
    keep_two.start()
    relay_all(ffn_rings)
    stream.relay()
    ffn_swaps += swap_pieces(here, mail, ffn_rings, (1, -1))
    two_ring.relay()
    finish_all(ffn_rings)
    ffn_swaps += swap_pieces(here, mail, ffn_rings, (2,))
    stream.finish()
    two_ring.finish()
    wait_all(ffn_swaps)
    keep_back.wait()
    keep_two.wait()
    keep_all.wait()
    mail.close()


def reduce_rings(here, mail, ref, parts, orders, near, far, stage):
    rings = []
    for number, ((first, chunks), order) in enumerate(zip(parts, orders)):
        fixed = {"x": None, "y": None, "z": None}
        for axis in order[:stage]:
            fixed[axis] = here.at[axis]
        pick = column_pick(ref, fixed, order[stage], first * LANE, chunks)
        rings.append(
            RingReduce(here, mail, order[stage], pick, near[number][stage], far[number][stage])
        )
    return rings


def landing_shapes(parts, orders):
    shapes = []
    for (_, chunks), order in zip(parts, orders):
        split = (chunks + 1) // 2
        done = []
        for stage in range(len(order)):
            gone = order[: stage + 1]
            lead = ()
            if "z" not in gone:
                lead += (2,)
            if "y" not in gone:
                lead += (4,)
            if "x" not in gone:
                lead += (4,)
            if "z" not in gone:
                lead += (2,)
            for count, copies in ((chunks, 2), (split, 1), (chunks - split, 1)):
                done += [lead + (16, count * LANE)] * copies
        shapes.append(done)
    return shapes


def landing_refs(orders, refs):
    near, far = [], []
    place = 0
    for order in orders:
        near.append([])
        far.append([])
        for _ in order:
            near[-1].append(refs[place : place + 2])
            far[-1].append(refs[place + 2 : place + 4])
            place += 4
    return near, far


def twin_send(here, mail, grads, half, landed):
    other = (1 - here.core) * half
    return mail.post(grads.at[:, :, :, :, :, cut(other, half)], landed, here.twin())


def twin_sum(here, grads, half, landed, total):
    base = here.core * half

    @pl.loop(0, 32)
    def _(index):
        high, y = lax.div(index, 16), lax.rem(lax.div(index, 4), 4)
        x = lax.rem(index, 4)
        for low in range(2):
            total[high, y, x, low] = (
                grads[high, y, x, low, :, cut(base, half)].astype(FLOAT)
                + landed[high, y, x, low].astype(FLOAT)
            ).astype(HALF)


def mixer_backward(here, flags, mix, proj, rows, branch, grads, small):
    follows = follows_of(here)
    first_ok, second_ok = flags[:, 0:1], flags[:, 1:2]

    @pl.loop(0, D // TILE)
    def _(tile):
        feats = cut(tile * TILE, TILE)
        gated = dot_nt(branch[0], mat_rows(mix, tile, slice(OUT_AT, OUT_AT + HALF_D)))
        gated += dot_nt(
            branch[1], mat_rows(mix, tile, slice(MIX_HALF + OUT_AT, MIX_HALF + OUT_AT + HALF_D))
        )
        b_all, c_all, v_all = (proj[which, :, feats] for which in range(3))
        mixed = b_all * v_all
        own = mixed[0:TOK]
        one, second = conv_terms(own, mixed[TOK:ALL] * follows)
        tap_one, tap_two = rows[3:4, feats], rows[4:5, feats]
        conv = rows[2:3, feats] * own + first_ok * tap_one * one + second_ok * tap_two * second
        d_c = gated * conv
        d_conv = gated * c_all[0:TOK]
        small[2:3, feats] = jnp.sum(d_conv * own, axis=0, keepdims=True)
        small[3:4, feats] = jnp.sum(d_conv * first_ok * one, axis=0, keepdims=True)
        small[4:5, feats] = jnp.sum(d_conv * second_ok * second, axis=0, keepdims=True)
        term_one = first_ok * tap_one * d_conv
        term_two = second_ok * tap_two * d_conv
        lines = row_index(TOK, TILE)
        zero = jnp.zeros((TOK, TILE), FLOAT)
        d_mixed = (
            rows[2:3, feats] * d_conv
            + jnp.where(lines < TOK - 1, pltpu.roll(term_one, TOK - 1, 0), zero)
            + jnp.where(lines < TOK - 2, pltpu.roll(term_two, TOK - 2, 0), zero)
        )
        lines = row_index(16, TILE)
        zero = jnp.zeros((16, TILE), FLOAT)
        d_halo = follows * (
            jnp.where(lines < 2, term_two[0:16], zero)
            + jnp.where(lines == 1, pltpu.roll(term_one[0:16], 1, 0), zero)
        )
        half, place = lax.div(tile, 2), lax.rem(tile, 2) * TILE
        for which, (main, edge) in enumerate(
            (
                (d_mixed * v_all[0:TOK], d_halo * v_all[TOK:ALL]),
                (d_c, zero),
                (d_mixed * b_all[0:TOK], d_halo * b_all[TOK:ALL]),
            )
        ):
            cols = cut(which * HALF_D + place, TILE)
            grads[half, 0:TOK, cols] = main.astype(HALF)
            grads[half, TOK:ALL, cols] = edge.astype(HALF)


def projection_back(mix, grads, normed_grad):
    @pl.loop(0, D // TILE)
    def _(tile):
        total = dot_nt(grads[0], mat_rows(mix, tile, slice(0, OUT_AT)))
        total += dot_nt(grads[1], mat_rows(mix, tile, slice(MIX_HALF, MIX_HALF + OUT_AT)))
        normed_grad[:, cut(tile * TILE, TILE)] = total


def mixer_weight_grads(here, grads, branch, turned, grads_in, branch_in, total):
    def put(cols, value):
        total[:, :, :, :, :, cols] = value.astype(HALF).reshape(GRID + (16, TILE))

    @pl.loop(0, OUT_AT // TILE)
    def _(tile):
        cols = cut(tile * TILE, TILE)
        put(cols, dot(turned[0], grads[here.core, :, cols]) + dot(turned[1], grads_in[:, cols]))

    @pl.loop(0, HALF_D // TILE)
    def _(tile):
        cols = cut(tile * TILE, TILE)
        value = dot(turned[2, :, 0:TOK], branch[here.core, :, cols])
        value += dot(turned[3, :, 0:TOK], branch_in[:, cols])
        put(cut(OUT_AT + tile * TILE, TILE), value)


def backward_kernel(
    mix_in, proj, normed, gated, resid, rows, tokens, halo, flags, cotangent, two_sum, ffn_sum, ffn,
    mixed_out, grad_tokens, mix_owned, ffn_owned,
    mix, total, mix_mate, ffn_landed, ffn_total, ffn_rest, ffn_mate, work, ffn_work,
    branch, grads, d_normed, small, turned, normed_in, gated_in, branch_in, grads_in, small_in,
    edge_in, d_resid, *scratch,
):
    two_near, two_far = scratch[0:2], scratch[2:4]
    out_near, out_far = scratch[4:6], scratch[6:8]
    *landing, send, recv, local_sem = scratch[8:]
    mix_near, mix_far = landing_refs(MIX_REDUCE, landing[:MIX_LANDING])
    ffn_near, ffn_far = landing_refs(FFN_REDUCE, landing[MIX_LANDING:])
    here = Here()
    mail = Mail(send, recv)
    x, core = here.at["x"], here.core
    twin = here.twin()
    loads = [
        pltpu.make_async_copy(two_sum, work, local_sem.at[0]),
        pltpu.make_async_copy(mix_in, mix, local_sem.at[1]),
        pltpu.make_async_copy(ffn_sum, ffn_work, local_sem.at[2]),
    ]
    for load in loads:
        load.start()
    greet(
        near_list(here, ("x", "y", "z"))
        + [here.beside("x", 2), twin, here.along(1), here.along(-1)]
    )
    loads[0].wait()
    two_ring = RingReduce(here, mail, "x", row_pick(work), two_near, two_far)
    two_ring.start()
    early = [mail.post(normed, normed_in, twin), mail.post(gated, gated_in, twin)]
    ffn_twin = twin_send(here, mail, ffn, FFN_HALF, ffn_landed)
    turned[0, :, 0:ALL] = jnp.transpose(normed[...].astype(FLOAT)).astype(HALF)
    turned[2, :, 0:TOK] = jnp.transpose(gated[...].astype(FLOAT)).astype(HALF)
    two_ring.relay()
    ffn_twin.wait_recv()
    twin_sum(here, ffn, FFN_HALF, ffn_landed, ffn_total)
    ffn_rings = reduce_rings(here, mail, ffn_total, FFN_PARTS, FFN_REDUCE, ffn_near, ffn_far, 0)
    start_all(ffn_rings)
    two_ring.finish()

    value = resid[...]
    scale = norm_scale(value)
    unit = value * scale
    d_two = work[x].astype(FLOAT)
    small[...] = jnp.zeros_like(small)
    small[1:2] = jnp.sum(d_two * unit, axis=0, keepdims=True)
    d_value = flags[:, 2:3] * cotangent[...].astype(FLOAT) + norm_back(unit, scale, rows[1:2], d_two)
    d_resid[...] = d_value
    branch[0] = d_value[:, 0:HALF_D].astype(HALF)
    branch[1] = d_value[:, HALF_D:D].astype(HALF)
    late = [mail.post(branch.at[1 - core], branch_in, twin)]
    loads[1].wait()
    mixer_backward(here, flags, mix, proj, rows, branch, grads, small)
    late.append(mail.post(grads.at[1 - core], grads_in, twin))
    relay_all(ffn_rings)
    projection_back(mix, grads, d_normed)
    x_own, x_edge = tokens[...].astype(FLOAT), halo[...].astype(FLOAT)
    scale = norm_scale(x_own)
    unit = x_own * scale
    small[0:1] = jnp.sum(d_normed[0:TOK] * unit, axis=0, keepdims=True) + jnp.sum(
        d_normed[TOK:ALL] * x_edge * norm_scale(x_edge), axis=0, keepdims=True
    )
    late.append(mail.post(small, small_in, twin))
    edge = mail.post(d_normed.at[pl.ds(TOK, 8)], edge_in, here.along(-1))
    wait_all(early)
    turned[1, :, 0:ALL] = jnp.transpose(normed_in[...].astype(FLOAT)).astype(HALF)
    turned[3, :, 0:TOK] = jnp.transpose(gated_in[...].astype(FLOAT)).astype(HALF)
    wait_all(late)
    mixer_weight_grads(here, grads, branch, turned, grads_in, branch_in, total)
    small_sum = small[...] + small_in[...]
    total[:, :, :, :, :, SMALL_AT:MIX_HALF] = (
        jnp.transpose(small_sum).astype(HALF).reshape(GRID + (16, LANE))
    )
    mix_rings = reduce_rings(here, mail, total, MIX_PARTS, MIX_REDUCE, mix_near, mix_far, 0)
    start_all(mix_rings)
    loads[2].wait()
    out_ring = RingReduce(here, mail, "x", row_pick(ffn_work), out_near, out_far)
    out_ring.start()
    finish_all(ffn_rings)
    ffn_rings = reduce_rings(here, mail, ffn_total, FFN_PARTS, FFN_REDUCE, ffn_near, ffn_far, 1)
    start_all(ffn_rings)
    relay_all(mix_rings)
    out_ring.relay()
    relay_all(ffn_rings)
    edge.wait_recv()
    d_first = (
        d_normed[0:TOK] + flags[:, 3:4] * edge_in[0:1] + flags[:, 4:5] * edge_in[1:2]
    )
    grad_tokens[...] = (d_resid[...] + norm_back(unit, scale, rows[0:1], d_first)).astype(HALF)
    finish_all(mix_rings)
    mix_rings = reduce_rings(here, mail, total, MIX_PARTS, MIX_REDUCE, mix_near, mix_far, 1)
    start_all(mix_rings)
    finish_all(ffn_rings)
    copies = []
    for step in (1, 3, 2):
        there = here.ring("x", step)
        copies.append(
            mail.post(
                blocks(ffn_total, {**here.at, "x": there}, slice(None)),
                ffn_rest.at[x],
                here.beside("x", step),
            )
        )
    ffn_rest[x] = blocks(ffn_total, here.at, slice(None))[...]
    relay_all(mix_rings)
    out_ring.finish()
    mixed_out[...] = (flags[:, 2:3] * (resid[...] + ffn_work[x].astype(FLOAT))).astype(HALF)
    finish_all(mix_rings)
    mix_rings = reduce_rings(here, mail, total, MIX_PARTS, MIX_REDUCE, mix_near, mix_far, 2)
    start_all(mix_rings)
    wait_all(copies)
    ffn_swap = mail.post(ffn_rest, ffn_mate, twin)
    ffn_owned[:, :, cut(core * FFN_HALF, FFN_HALF)] = ffn_rest[...].astype(FLOAT)
    relay_all(mix_rings)
    ffn_swap.wait_recv()
    ffn_owned[:, :, cut((1 - core) * FFN_HALF, FFN_HALF)] = ffn_mate[...].astype(FLOAT)
    finish_all(mix_rings)
    own = blocks(total, here.at, slice(None))
    mix_swap = mail.post(own, mix_mate, twin)
    mix_owned[:, cut(core * MIX_HALF, MIX_HALF)] = own[...].astype(FLOAT)
    mix_swap.wait_recv()
    mix_owned[:, cut((1 - core) * MIX_HALF, MIX_HALF)] = mix_mate[...].astype(FLOAT)
    mail.close()


def vmem():
    return pl.BlockSpec(memory_space=pltpu.VMEM)


def anywhere():
    return pl.BlockSpec(memory_space=pl.ANY)


def sems(count):
    return pltpu.SemaphoreType.DMA((count,))


def params(number):
    return pltpu.CompilerParams(
        collective_id=number, has_side_effects=True, vmem_limit_bytes=VMEM_LIMIT
    )


def shape(dims, dtype):
    return jax.ShapeDtypeStruct(dims, dtype)


def forward(own, tail, back, tokens, flags):
    return pl.pallas_call(
        forward_kernel,
        out_shape=(
            shape(GRID + (16, MIX_COLS), HALF),
            shape(GRID + (16, FFN_COLS), HALF),
            shape((4, TOK, D), HALF),
            shape((4, TOK, D), HALF),
            shape((3, ALL, D), FLOAT),
            shape((ALL, D), HALF),
            shape((TOK, D), HALF),
            shape((TOK, D), FLOAT),
            shape((8, D), FLOAT),
            shape((16, D), HALF),
        ),
        in_specs=[vmem()] * 5,
        out_specs=(anywhere(),) * 4 + (vmem(),) * 6,
        scratch_shapes=[
            pltpu.VMEM((16, OWN_COLS), HALF),
            pltpu.VMEM((16, OWN_COLS), HALF),
            pltpu.VMEM(GRID + (16, MIX_COLS), HALF),
            pltpu.VMEM((TOK, D), HALF),
            sems(96),
            sems(96),
            sems(3),
        ],
        compiler_params=params(0),
        name="forward",
    )(own, tail, back, tokens, flags)


def backward(mix, proj, normed, gated, resid, rows, tokens, halo, flags, cotangent, two_sum, ffn_sum, ffn):
    landing = [
        pltpu.VMEM(dims, HALF)
        for part in landing_shapes(MIX_PARTS, MIX_REDUCE) + landing_shapes(FFN_PARTS, FFN_REDUCE)
        for dims in part
    ]
    stream_landing = [pltpu.VMEM((TOK, D), HALF)] * 2 + [pltpu.VMEM((TOK // 2, D), HALF)] * 2
    return pl.pallas_call(
        backward_kernel,
        out_shape=(
            shape((TOK, D), HALF),
            shape((TOK, D), HALF),
            shape((16, MIX_COLS), FLOAT),
            shape((4, 16, FFN_COLS), FLOAT),
        ),
        in_specs=[anywhere()] + [vmem()] * 9 + [anywhere()] * 2 + [vmem()],
        out_specs=(vmem(),) * 4,
        scratch_shapes=[
            pltpu.VMEM(GRID + (16, MIX_COLS), HALF),
            pltpu.VMEM(GRID + (16, MIX_HALF), HALF),
            pltpu.VMEM((16, MIX_HALF), HALF),
            pltpu.VMEM(GRID + (16, FFN_HALF), HALF),
            pltpu.VMEM(GRID + (16, FFN_HALF), HALF),
            pltpu.VMEM((4, 16, FFN_HALF), HALF),
            pltpu.VMEM((4, 16, FFN_HALF), HALF),
            pltpu.VMEM((4, TOK, D), HALF),
            pltpu.VMEM((4, TOK, D), HALF),
            pltpu.VMEM((2, TOK, HALF_D), HALF),
            pltpu.VMEM((2, ALL, OUT_AT), HALF),
            pltpu.VMEM((ALL, D), FLOAT),
            pltpu.VMEM((LANE, D), FLOAT),
            pltpu.VMEM((4, D, ALL), HALF),
            pltpu.VMEM((ALL, D), HALF),
            pltpu.VMEM((TOK, D), HALF),
            pltpu.VMEM((TOK, HALF_D), HALF),
            pltpu.VMEM((ALL, OUT_AT), HALF),
            pltpu.VMEM((LANE, D), FLOAT),
            pltpu.VMEM((8, D), FLOAT),
            pltpu.VMEM((TOK, D), FLOAT),
        ]
        + stream_landing * 2
        + landing
        + [sems(96), sems(96), sems(3)],
        compiler_params=params(1),
        name="backward",
    )(mix, proj, normed, gated, resid, rows, tokens, halo, flags, cotangent, two_sum, ffn_sum, ffn)


def dot_tn(left, right):
    return jnp.einsum("ta,tb->ab", left, right, preferred_element_type=FLOAT)


def local(
    tokens,
    gain_mix,
    in_weight,
    conv_weight,
    out_weight,
    gain_ffn,
    gate_weight,
    up_weight,
    down_weight,
    live_counts,
    positions,
    cotangent,
):
    core = lax.rem(lax.axis_index("seq"), 2)
    count = live_counts[0, 0]
    small = jnp.stack([gain_mix, gain_ffn, conv_weight[0], conv_weight[1], conv_weight[2]], axis=1)
    small = jnp.pad(small, ((0, 0), (0, LANE - 5)))
    mix_rows = jnp.concatenate(
        [
            in_weight.reshape(8, 3, 2, HALF_D).transpose(0, 2, 1, 3).reshape(8, 2, OUT_AT),
            out_weight.reshape(8, 2, HALF_D),
            jnp.stack([small, small], axis=1),
        ],
        axis=2,
    )
    ffn_rows = [
        weight.reshape(8, 4, SLAB) for weight in (gate_weight, up_weight, jnp.transpose(down_weight))
    ]
    ffn_rows = jnp.concatenate(ffn_rows + [jnp.zeros((8, 4, FFN_COLS - 3 * SLAB), HALF)], axis=2)
    ffn_rows = ffn_rows.reshape(8, 4, 2, FFN_HALF).transpose(0, 2, 1, 3).reshape(8, 2, 4 * FFN_HALF)
    own = jnp.concatenate([mix_rows, ffn_rows], axis=2).transpose(1, 0, 2)
    own = jnp.concatenate([own, own], axis=1)
    tail = jnp.pad(lax.dynamic_slice(tokens, (count - 2, 0), (2, D)), ((0, 14), (0, 0)))
    slots = jnp.arange(TOK, dtype=jnp.int32)
    flags = jnp.stack(
        [positions >= 1, positions >= 2, slots < count, slots == count - 2, slots == count - 1], axis=1
    )
    flags = jnp.pad(flags.astype(FLOAT), ((0, 0), (0, LANE - 5)))
    d_ffn = jnp.where(flags[:, 2:3] > 0, cotangent, jnp.zeros_like(cotangent))

    mix, ffn, backs, twos, proj, normed, gated, resid, rows, halo = forward(
        own, tail, d_ffn, tokens, flags
    )
    ffn = ffn.reshape(D, FFN_COLS)
    w_gate, w_up, w_down = ffn[:, :SLAB], ffn[:, SLAB : 2 * SLAB], ffn[:, 2 * SLAB : 3 * SLAB]
    twos = twos.reshape(4 * TOK, D)
    backs = backs.reshape(4 * TOK, D)
    gate = dot(twos, w_gate)
    upper = dot(twos, w_up)
    sig = jax.nn.sigmoid(gate)
    swish = gate * sig
    active = (swish * upper).astype(HALF)
    d_active = dot(backs, w_down)
    d_gate = (d_active * upper * (sig * (1.0 + gate * (1.0 - sig)))).astype(HALF)
    d_upper = (d_active * swish).astype(HALF)
    ffn_sum = dot_nt(active, w_down).astype(HALF)
    two_sum = (dot_nt(d_gate, w_gate) + dot_nt(d_upper, w_up)).astype(HALF)
    ffn_grads = jnp.concatenate(
        [
            dot_tn(twos, d_gate).astype(HALF),
            dot_tn(twos, d_upper).astype(HALF),
            dot_tn(backs, active).astype(HALF),
            jnp.zeros((D, FFN_COLS - 3 * SLAB), HALF),
        ],
        axis=1,
    )
    mixed_out, grad_tokens, owned_mix, owned_ffn = backward(
        mix, proj, normed, gated, resid, rows, tokens, halo, flags, cotangent,
        two_sum.reshape(4, TOK, D), ffn_sum.reshape(4, TOK, D), ffn_grads.reshape(GRID + (16, FFN_COLS)),
    )
    mine = lax.dynamic_slice(owned_mix, (8 * core, 0), (8, MIX_COLS)).reshape(8, 2, MIX_HALF)
    ffn_mine = lax.dynamic_slice(owned_ffn, (0, 8 * core, 0), (4, 8, FFN_COLS))
    ffn_mine = jnp.transpose(ffn_mine, (1, 0, 2))
    small_mine = jnp.transpose(mine[:, 0, SMALL_AT : SMALL_AT + 8])
    grad_in = mine[:, :, :OUT_AT].reshape(8, 2, 3, HALF_D).transpose(0, 2, 1, 3).reshape(8, 3 * D)
    return (
        mixed_out,
        grad_tokens,
        small_mine[0],
        grad_in,
        small_mine[2:5],
        mine[:, :, OUT_AT:SMALL_AT].reshape(8, D),
        small_mine[1],
        ffn_mine[:, :, :SLAB].reshape(8, 4 * SLAB),
        ffn_mine[:, :, SLAB : 2 * SLAB].reshape(8, 4 * SLAB),
        jnp.transpose(ffn_mine[:, :, 2 * SLAB : 3 * SLAB].reshape(8, 4 * SLAB)),
    )


def solution(mesh):
    rows = P(("fsdp", "seq"), None)
    flat = P(("fsdp", "seq"))
    cols = P(None, ("fsdp", "seq"))
    return jax.shard_map(
        local,
        mesh=mesh,
        in_specs=(rows, flat, rows, cols, rows, flat, rows, rows, cols, P("fsdp", "seq"), flat, rows),
        out_specs=(rows, rows, flat, rows, cols, rows, flat, rows, rows, cols),
        check_vma=False,
    )
```

```python
import jax
import jax.numpy as jnp
from jax import lax
from jax.experimental import pallas as pl
from jax.experimental.pallas import tpu as pltpu
from jax.sharding import PartitionSpec as P

EPS = 1e-05
FLOAT = jnp.float32
HALF = jnp.bfloat16
MESH = pl.DeviceIdType.MESH
LANE = 128
D = 1024
SLAB = 1152
MIX_COLS = 34 * LANE
FFN_COLS = 28 * LANE
MIX_HALF = MIX_COLS // 2
FFN_HALF = FFN_COLS // 2
OWN_COLS = MIX_HALF + 4 * FFN_HALF
HALF_D = D // 2
OUT_AT = 3 * HALF_D
SMALL_AT = 4 * HALF_D
TILE = 256
TOK = 128
ALL = TOK + 16
MIX_PARTS = ((0, 6), (6, 6), (12, 5))
MIX_GATHER = (("y", "z", "x"), ("z", "x", "y"), ("x", "y", "z"))
MIX_REDUCE = (("x", "z", "y"), ("y", "x", "z"), ("z", "y", "x"))
FFN_PARTS = ((0, 7), (7, 7))
FFN_GATHER = (("y", "z"), ("z", "y"))
FFN_REDUCE = (("y", "z"), ("z", "y"))
GRID = (2, 4, 4, 2)
MIX_LANDING = 4 * 3 * len(MIX_PARTS)
VMEM_LIMIT = 60 * 2**20


class Here:
    def __init__(self):
        fsdp = lax.axis_index("fsdp")
        seq = lax.axis_index("seq")
        self.fsdp, self.seq = fsdp, seq
        self.at = {
            "x": lax.div(seq, 4),
            "y": lax.rem(fsdp, 4),
            "z": lax.div(fsdp, 4) * 2 + lax.rem(lax.div(seq, 2), 2),
        }
        self.core = lax.rem(seq, 2)

    def device(self, core, **moved):
        at = {**self.at, **moved}
        return (
            lax.div(at["z"], 2) * 4 + at["y"],
            (at["x"] * 2 + lax.rem(at["z"], 2)) * 2 + core,
        )

    def ring(self, axis, step):
        return lax.rem(self.at[axis] + (step + 4) % 4, 4)

    def beside(self, axis, step):
        return self.device(self.core, **{axis: self.ring(axis, step)})

    def twin(self):
        return self.device(1 - self.core)

    def along(self, step):
        return (self.fsdp, lax.rem(self.seq + (step + 16) % 16, 16))


def greet(devices):
    barrier = pltpu.get_barrier_semaphore()
    for device in devices:
        pl.semaphore_signal(barrier, inc=1, device_id=device, device_id_type=MESH)
    pl.semaphore_wait(barrier, len(devices))


class Mail:
    def __init__(self, send, recv):
        self.send, self.recv, self.posted, self.settled = send, recv, [], 0

    def post(self, src, dst, device):
        place = len(self.posted)
        copy = pltpu.make_async_remote_copy(
            src_ref=src,
            dst_ref=dst,
            send_sem=self.send.at[place],
            recv_sem=self.recv.at[place],
            device_id=device,
            device_id_type=MESH,
        )
        copy.start()
        self.posted.append(copy)
        return copy

    def settle(self, count):
        for copy in self.posted[self.settled : count]:
            copy.wait_send()
        self.settled = count


def cut(start, count):
    return pl.ds(pl.multiple_of(start, LANE), count)


def blocks(ref, at, cols):
    whole = slice(None)
    z = at["z"]
    high, low = (whole, whole) if z is None else (lax.div(z, 2), lax.rem(z, 2))
    y = whole if at["y"] is None else at["y"]
    x = whole if at["x"] is None else at["x"]
    return ref.at[high, y, x, low, :, cols]


class RingGather:
    def __init__(self, here, mail, axis, pick):
        self.here, self.mail, self.axis, self.pick = here, mail, axis, pick

    def start(self, source=None):
        here, axis = self.here, self.axis
        own = self.pick(here.at[axis], None)
        source = own if source is None else source
        self.to_up = self.mail.post(source, own, here.beside(axis, 1))
        self.to_down = self.mail.post(source, own, here.beside(axis, -1))

    def relay(self):
        here, axis = self.here, self.axis
        self.to_up.wait_recv()
        first = self.pick(here.ring(axis, -1), 0)
        self.far_up = self.mail.post(first, first, here.beside(axis, 1))
        self.to_down.wait_recv()
        second = self.pick(here.ring(axis, 1), 1)
        self.far_down = self.mail.post(second, second, here.beside(axis, -1))

    def finish(self):
        self.far_up.wait_recv()
        self.far_down.wait_recv()


class RingReduce:
    def __init__(self, here, mail, axis, pick, near, far):
        self.here, self.mail, self.axis, self.pick = here, mail, axis, pick
        self.near, self.far = near, far

    def start(self):
        here, axis = self.here, self.axis
        away = here.ring(axis, 2)
        self.far_up = self.mail.post(self.pick(away, 0), self.far[0], here.beside(axis, 1))
        self.far_down = self.mail.post(self.pick(away, 1), self.far[1], here.beside(axis, -1))

    def relay(self):
        here, axis = self.here, self.axis
        above, below = here.ring(axis, 1), here.ring(axis, -1)
        self.far_up.wait_recv()
        add_into(self.pick(above, 0), self.far[0])
        self.to_up = self.mail.post(self.pick(above, None), self.near[0], here.beside(axis, 1))
        self.far_down.wait_recv()
        add_into(self.pick(below, 1), self.far[1])
        self.to_down = self.mail.post(self.pick(below, None), self.near[1], here.beside(axis, -1))

    def finish(self):
        self.to_up.wait_recv()
        self.to_down.wait_recv()
        own = self.pick(self.here.at[self.axis], None)
        add_into(own, self.near[0], self.near[1])


def add_into(target, *terms):
    total = target[...].astype(FLOAT)
    for term in terms:
        total = total + term[...].astype(FLOAT)
    target[...] = total.astype(target.dtype)


def column_pick(ref, fixed, axis, start, chunks):
    split = (chunks + 1) // 2

    def pick(place, half):
        first, count = {None: (0, chunks), 0: (0, split), 1: (split, chunks - split)}[half]
        return blocks(ref, {**fixed, axis: place}, cut(start + first * LANE, count * LANE))

    return pick


def row_pick(ref):
    def pick(place, half):
        rows = ref.shape[-2]
        part = {None: slice(None), 0: pl.ds(0, rows // 2), 1: pl.ds(rows // 2, rows // 2)}[half]
        return ref.at[place, part]

    return pick


def gather_rings(here, mail, ref, base, parts, orders, stage):
    rings = []
    for (first, chunks), order in zip(parts, orders):
        fixed = dict(here.at)
        for axis in ("x", "y", "z"):
            if axis not in order or axis in order[:stage]:
                fixed[axis] = None
        pick = column_pick(ref, fixed, order[stage], base + first * LANE, chunks)
        rings.append(RingGather(here, mail, order[stage], pick))
    return rings


def start_all(rings):
    for ring in rings:
        ring.start()


def relay_all(rings):
    for ring in rings:
        ring.relay()


def finish_all(rings):
    for ring in rings:
        ring.finish()


def run_rings(rings):
    start_all(rings)
    relay_all(rings)
    finish_all(rings)


def swap_pieces(here, mail, rings, steps):
    copies = []
    for ring in rings:
        for step in steps:
            piece = ring.pick(here.ring(ring.axis, step), None)
            copies.append(mail.post(piece, piece, here.twin()))
    return copies


def wait_all(copies):
    for copy in copies:
        copy.wait_recv()


def near_list(here, axes):
    return [here.beside(axis, step) for axis in axes for step in (1, -1)]


def mat(ref, cols):
    block = ref[:, :, :, :, :, cols]
    return block.reshape(D, block.shape[-1])


def mat_rows(ref, tile, cols):
    block = ref[lax.div(tile, 2), pl.ds(lax.rem(tile, 2) * 2, 2), :, :, :, cols]
    return block.reshape(TILE, block.shape[-1])


def mix_cols(tile, which):
    return cut(lax.div(tile, 2) * MIX_HALF + which * HALF_D + lax.rem(tile, 2) * TILE, TILE)


def dot(left, right):
    return jnp.dot(left, right, preferred_element_type=FLOAT)


def dot_nt(left, right):
    return lax.dot_general(
        left, right, (((1,), (1,)), ((), ())), preferred_element_type=FLOAT
    )


def norm_scale(values):
    return lax.rsqrt(jnp.mean(values * values, axis=-1, keepdims=True) + EPS)


def norm_back(normal, row_scale, gain_row, upstream):
    weighted = upstream * gain_row
    return row_scale * (
        weighted - normal * jnp.mean(weighted * normal, axis=-1, keepdims=True)
    )


def row_index(rows, cols):
    return lax.broadcasted_iota(jnp.int32, (rows, cols), 0)


def conv_terms(mixed, halo):
    rows = row_index(TOK, mixed.shape[1])
    one = pltpu.roll(mixed, 1, 0)
    two = pltpu.roll(mixed, 2, 0)
    one = jnp.where(rows == 0, halo[1:2], one)
    two = jnp.where(rows == 0, halo[0:1], jnp.where(rows == 1, halo[1:2], two))
    return one, two


def follows_of(here):
    return jnp.minimum(here.seq, 1).astype(FLOAT)


def mixer_forward(here, tokens, halo, flags, mix, proj, normed, gated, resid, rows, two):
    small = jnp.transpose(mat(mix, slice(SMALL_AT, SMALL_AT + LANE)).astype(FLOAT))
    rows[...] = small[0:8]
    gain = rows[0:1]
    x = tokens[...].astype(FLOAT)
    normed[0:TOK] = (x * norm_scale(x) * gain).astype(HALF)
    before = halo[...].astype(FLOAT)
    normed[TOK:ALL] = (before * norm_scale(before) * gain).astype(HALF)
    follows = follows_of(here)
    first_ok, second_ok = flags[:, 0:1], flags[:, 1:2]

    @pl.loop(0, D // TILE)
    def _(tile):
        feats = cut(tile * TILE, TILE)
        parts = [dot(normed[...], mat(mix, mix_cols(tile, which))) for which in range(3)]
        for which in range(3):
            proj[which, :, feats] = parts[which]
        mixed = parts[0] * parts[2]
        own = mixed[0:TOK]
        one, second = conv_terms(own, mixed[TOK:ALL] * follows)
        conv = (
            rows[2:3, feats] * own
            + first_ok * rows[3:4, feats] * one
            + second_ok * rows[4:5, feats] * second
        )
        gated[:, feats] = (parts[1][0:TOK] * conv).astype(HALF)

    @pl.loop(0, D // TILE)
    def _(tile):
        feats = cut(tile * TILE, TILE)
        branch = dot(gated[...], mat(mix, mix_cols(tile, 3)))
        resid[:, feats] = tokens[:, feats].astype(FLOAT) + branch

    value = resid[...]
    two[...] = (value * norm_scale(value) * rows[1:2]).astype(HALF)


def reduce_rings(here, mail, ref, base, parts, orders, near, far, stage):
    rings = []
    for number, ((first, chunks), order) in enumerate(zip(parts, orders)):
        fixed = {"x": None, "y": None, "z": None}
        for axis in order[:stage]:
            fixed[axis] = here.at[axis]
        pick = column_pick(ref, fixed, order[stage], base + first * LANE, chunks)
        rings.append(
            RingReduce(here, mail, order[stage], pick, near[number][stage], far[number][stage])
        )
    return rings


def landing_shapes(parts, orders):
    shapes = []
    for (_, chunks), order in zip(parts, orders):
        split = (chunks + 1) // 2
        done = []
        for stage in range(len(order)):
            gone = order[: stage + 1]
            lead = ()
            if "z" not in gone:
                lead += (2,)
            if "y" not in gone:
                lead += (4,)
            if "x" not in gone:
                lead += (4,)
            if "z" not in gone:
                lead += (2,)
            for count, copies in ((chunks, 2), (split, 1), (chunks - split, 1)):
                done += [lead + (16, count * LANE)] * copies
        shapes.append(done)
    return shapes


def landing_refs(orders, refs):
    near, far = [], []
    place = 0
    for order in orders:
        near.append([])
        far.append([])
        for _ in order:
            near[-1].append(refs[place : place + 2])
            far[-1].append(refs[place + 2 : place + 4])
            place += 4
    return near, far


def twin_sum(ref, cols, landed):
    @pl.loop(0, 32)
    def _(index):
        high, y = lax.div(index, 16), lax.rem(lax.div(index, 4), 4)
        x = lax.rem(index, 4)
        for low in range(2):
            add_into(ref.at[high, y, x, low, :, cols], landed.at[high, y, x, low])


def ffn_hidden(ffn, twos, backs, acts, start, width):
    value = twos[...].reshape(4 * TOK, D)
    gate = dot(value, mat(ffn, cut(start, width)))
    upper = dot(value, mat(ffn, cut(SLAB + start, width)))
    d_active = dot(backs[...].reshape(4 * TOK, D), mat(ffn, cut(2 * SLAB + start, width)))
    sig = jax.nn.sigmoid(gate)
    swish = gate * sig
    acts[:, cut(start, width)] = (d_active * upper * (sig * (1.0 + gate * (1.0 - sig)))).astype(HALF)
    acts[:, cut(SLAB + start, width)] = (d_active * swish).astype(HALF)
    acts[:, cut(2 * SLAB + start, width)] = (swish * upper).astype(HALF)


def ffn_tokens(ffn, acts, target, kinds):
    @pl.loop(0, D // TILE)
    def _(tile):
        total = 0.0
        for kind in kinds:
            cols = slice(kind * SLAB, (kind + 1) * SLAB)
            total += dot_nt(acts[:, cols], mat_rows(ffn, tile, cols))
        target[:, :, cut(tile * TILE, TILE)] = total.astype(HALF).reshape(4, TOK, TILE)


def ffn_weight_grads(ffn, acts, turned, half):
    @pl.loop(0, FFN_HALF // TILE)
    def _(tile):
        cols = cut(half * FFN_HALF + tile * TILE, TILE)
        side = half * jnp.minimum(lax.div(tile, 2), 1)
        value = dot(turned[side], acts[:, cols])
        ffn[:, :, :, :, :, cols] = value.astype(HALF).reshape(GRID + (16, TILE))


def turn(target, value):
    target[...] = jnp.transpose(value.astype(FLOAT)).astype(HALF)


def mixer_backward(here, flags, mix, proj, rows, branch, grads, small):
    follows = follows_of(here)
    first_ok, second_ok = flags[:, 0:1], flags[:, 1:2]

    @pl.loop(0, D // TILE)
    def _(tile):
        feats = cut(tile * TILE, TILE)
        gated = dot_nt(branch[0], mat_rows(mix, tile, slice(OUT_AT, OUT_AT + HALF_D)))
        gated += dot_nt(
            branch[1], mat_rows(mix, tile, slice(MIX_HALF + OUT_AT, MIX_HALF + OUT_AT + HALF_D))
        )
        b_all, c_all, v_all = (proj[which, :, feats] for which in range(3))
        mixed = b_all * v_all
        own = mixed[0:TOK]
        one, second = conv_terms(own, mixed[TOK:ALL] * follows)
        tap_one, tap_two = rows[3:4, feats], rows[4:5, feats]
        conv = rows[2:3, feats] * own + first_ok * tap_one * one + second_ok * tap_two * second
        d_c = gated * conv
        d_conv = gated * c_all[0:TOK]
        small[2:3, feats] = jnp.sum(d_conv * own, axis=0, keepdims=True)
        small[3:4, feats] = jnp.sum(d_conv * first_ok * one, axis=0, keepdims=True)
        small[4:5, feats] = jnp.sum(d_conv * second_ok * second, axis=0, keepdims=True)
        term_one = first_ok * tap_one * d_conv
        term_two = second_ok * tap_two * d_conv
        lines = row_index(TOK, TILE)
        zero = jnp.zeros((TOK, TILE), FLOAT)
        d_mixed = (
            rows[2:3, feats] * d_conv
            + jnp.where(lines < TOK - 1, pltpu.roll(term_one, TOK - 1, 0), zero)
            + jnp.where(lines < TOK - 2, pltpu.roll(term_two, TOK - 2, 0), zero)
        )
        lines = row_index(16, TILE)
        zero = jnp.zeros((16, TILE), FLOAT)
        d_halo = follows * (
            jnp.where(lines < 2, term_two[0:16], zero)
            + jnp.where(lines == 1, pltpu.roll(term_one[0:16], 1, 0), zero)
        )
        half, place = lax.div(tile, 2), lax.rem(tile, 2) * TILE
        for which, (main, edge) in enumerate(
            (
                (d_mixed * v_all[0:TOK], d_halo * v_all[TOK:ALL]),
                (d_c, zero),
                (d_mixed * b_all[0:TOK], d_halo * b_all[TOK:ALL]),
            )
        ):
            cols = cut(which * HALF_D + place, TILE)
            grads[half, 0:TOK, cols] = main.astype(HALF)
            grads[half, TOK:ALL, cols] = edge.astype(HALF)


def projection_back(mix, grads, normed_grad):
    @pl.loop(0, D // TILE)
    def _(tile):
        total = dot_nt(grads[0], mat_rows(mix, tile, slice(0, OUT_AT)))
        total += dot_nt(grads[1], mat_rows(mix, tile, slice(MIX_HALF, MIX_HALF + OUT_AT)))
        normed_grad[:, cut(tile * TILE, TILE)] = total


def mixer_weight_grads(here, grads, branch, turned, grads_in, branch_in, total):
    def put(cols, value):
        total[:, :, :, :, :, cols] = value.astype(HALF).reshape(GRID + (16, TILE))

    @pl.loop(0, OUT_AT // TILE)
    def _(tile):
        cols = cut(tile * TILE, TILE)
        put(cols, dot(turned[0], grads[here.core, :, cols]) + dot(turned[1], grads_in[:, cols]))

    @pl.loop(0, HALF_D // TILE)
    def _(tile):
        cols = cut(tile * TILE, TILE)
        value = dot(turned[2, :, 0:TOK], branch[here.core, :, cols])
        value += dot(turned[3, :, 0:TOK], branch_in[:, cols])
        put(cut(OUT_AT + tile * TILE, TILE), value)


def block_kernel(
    own, tail, tokens, flags, cotangent,
    mixed_out, grad_tokens, mix_owned, ffn_owned,
    mate, full, halo, mix, ffn, twos, backs, proj, normed, gated, resid, rows, acts, turned_ffn,
    total, mix_mate, ffn_landed, ffn_rest, ffn_mate, work, ffn_work,
    branch, grads, d_normed, small, turned, normed_in, gated_in, branch_in, grads_in, small_in,
    edge_in, d_resid, *scratch,
):
    two_near, two_far = scratch[0:2], scratch[2:4]
    out_near, out_far = scratch[4:6], scratch[6:8]
    *landing, send, recv, local_sem = scratch[8:]
    mix_near, mix_far = landing_refs(MIX_REDUCE, landing[:MIX_LANDING])
    ffn_near, ffn_far = landing_refs(FFN_REDUCE, landing[MIX_LANDING:])
    here = Here()
    mail = Mail(send, recv)
    x, core = here.at["x"], here.core
    twin = here.twin()
    greet(
        near_list(here, ("x", "y", "z"))
        + [here.beside("x", 2), twin, here.along(1), here.along(-1)]
    )
    rows_in = mail.post(own.at[1 - core], mate, twin)
    halo_in = mail.post(tail, halo, here.along(1))
    backs[x] = (flags[:, 2:3] * cotangent[...].astype(FLOAT)).astype(HALF)
    acts[:, 3 * SLAB : FFN_COLS] = jnp.zeros((4 * TOK, FFN_COLS - 3 * SLAB), HALF)
    rows_in.wait_recv()
    mine = lax.broadcasted_iota(jnp.int32, (16, OWN_COLS), 0) // 8 == core
    full[...] = jnp.where(mine, own[core].astype(FLOAT), mate[...].astype(FLOAT)).astype(HALF)

    mix_base, ffn_base = core * MIX_HALF, core * FFN_HALF
    ffn_own = blocks(ffn, here.at, cut(ffn_base, FFN_HALF))

    def slab(place):
        return full.at[:, cut(MIX_HALF + place * FFN_HALF, FFN_HALF)]

    rings = gather_rings(here, mail, mix, mix_base, MIX_PARTS, MIX_GATHER, 0)
    for ring, (first, chunks) in zip(rings, MIX_PARTS):
        ring.start(full.at[:, first * LANE : (first + chunks) * LANE])
    slabs = [
        mail.post(slab(here.ring("x", step)), ffn_own, here.beside("x", step)) for step in (1, 3, 2)
    ]
    keep_mix = pltpu.make_async_copy(
        full.at[:, 0:MIX_HALF], blocks(mix, here.at, cut(mix_base, MIX_HALF)), local_sem.at[0]
    )
    keep_slab = pltpu.make_async_copy(slab(x), ffn_own, local_sem.at[1])
    keep_mix.start()
    keep_slab.start()
    relay_all(rings)
    finish_all(rings)
    keep_mix.wait()
    mix_rings = gather_rings(here, mail, mix, mix_base, MIX_PARTS, MIX_GATHER, 1)
    start_all(mix_rings)
    keep_slab.wait()
    wait_all(slabs)
    ffn_rings = gather_rings(here, mail, ffn, ffn_base, FFN_PARTS, FFN_GATHER, 0)
    start_all(ffn_rings)
    relay_all(mix_rings + ffn_rings)
    finish_all(mix_rings)
    mix_rings = gather_rings(here, mail, mix, mix_base, MIX_PARTS, MIX_GATHER, 2)
    start_all(mix_rings)
    swaps = swap_pieces(here, mail, mix_rings, (0,))
    finish_all(ffn_rings)
    ffn_rings = gather_rings(here, mail, ffn, ffn_base, FFN_PARTS, FFN_GATHER, 1)
    relay_all(mix_rings)
    swaps += swap_pieces(here, mail, mix_rings, (1, -1))
    start_all(ffn_rings)
    stream = RingGather(here, mail, "x", row_pick(backs))
    stream.start()
    finish_all(mix_rings)
    swaps += swap_pieces(here, mail, mix_rings, (2,))
    ffn_swaps = swap_pieces(here, mail, ffn_rings, (0,))
    wait_all(swaps)
    halo_in.wait_recv()
    mixer_forward(here, tokens, halo, flags, mix, proj, normed, gated, resid, rows, twos.at[x])
    two_ring = RingGather(here, mail, "x", row_pick(twos))
    two_ring.start()
    relay_all(ffn_rings)
    stream.relay()
    ffn_swaps += swap_pieces(here, mail, ffn_rings, (1, -1))
    early = [mail.post(normed, normed_in, twin), mail.post(gated, gated_in, twin)]
    two_ring.relay()
    turn(turned.at[0, :, 0:ALL], normed[...])
    turn(turned.at[2, :, 0:TOK], gated[...])
    finish_all(ffn_rings)
    ffn_swaps += swap_pieces(here, mail, ffn_rings, (2,))
    stream.finish()
    for block in range(4):
        turn(turned_ffn.at[1, :, block * TOK : (block + 1) * TOK], backs[block])
    wait_all(ffn_swaps)
    two_ring.finish()
    gathered = len(mail.posted)

    @pl.loop(0, SLAB // TILE)
    def _(tile):
        ffn_hidden(ffn, twos, backs, acts, tile * TILE, TILE)

    ffn_hidden(ffn, twos, backs, acts, SLAB // TILE * TILE, SLAB % TILE)
    ffn_tokens(ffn, acts, work, (0, 1))
    two_ring = RingReduce(here, mail, "x", row_pick(work), two_near, two_far)
    two_ring.start()
    ffn_tokens(ffn, acts, ffn_work, (2,))
    for block in range(4):
        turn(turned_ffn.at[0, :, block * TOK : (block + 1) * TOK], twos[block])
    mail.settle(gathered)
    ffn_weight_grads(ffn, acts, turned_ffn, 1 - core)
    ffn_twin = mail.post(
        ffn.at[:, :, :, :, :, cut((1 - core) * FFN_HALF, FFN_HALF)], ffn_landed, twin
    )
    two_ring.relay()
    ffn_weight_grads(ffn, acts, turned_ffn, core)
    two_ring.finish()
    value = resid[...]
    scale = norm_scale(value)
    unit = value * scale
    d_two = work[x].astype(FLOAT)
    small[...] = jnp.zeros_like(small)
    small[1:2] = jnp.sum(d_two * unit, axis=0, keepdims=True)
    d_value = flags[:, 2:3] * cotangent[...].astype(FLOAT) + norm_back(unit, scale, rows[1:2], d_two)
    d_resid[...] = d_value
    branch[0] = d_value[:, 0:HALF_D].astype(HALF)
    branch[1] = d_value[:, HALF_D:D].astype(HALF)
    late = [mail.post(branch.at[1 - core], branch_in, twin)]
    out_ring = RingReduce(here, mail, "x", row_pick(ffn_work), out_near, out_far)
    out_ring.start()
    ffn_twin.wait_recv()
    twin_sum(ffn, cut(ffn_base, FFN_HALF), ffn_landed)
    ffn_rings = reduce_rings(here, mail, ffn, ffn_base, FFN_PARTS, FFN_REDUCE, ffn_near, ffn_far, 0)
    start_all(ffn_rings)
    mixer_backward(here, flags, mix, proj, rows, branch, grads, small)
    late.append(mail.post(grads.at[1 - core], grads_in, twin))
    relay_all(ffn_rings)
    out_ring.relay()
    projection_back(mix, grads, d_normed)
    x_own, x_edge = tokens[...].astype(FLOAT), halo[...].astype(FLOAT)
    scale = norm_scale(x_own)
    unit = x_own * scale
    small[0:1] = jnp.sum(d_normed[0:TOK] * unit, axis=0, keepdims=True) + jnp.sum(
        d_normed[TOK:ALL] * x_edge * norm_scale(x_edge), axis=0, keepdims=True
    )
    late.append(mail.post(small, small_in, twin))
    edge = mail.post(d_normed.at[pl.ds(TOK, 8)], edge_in, here.along(-1))
    wait_all(early)
    turn(turned.at[1, :, 0:ALL], normed_in[...])
    turn(turned.at[3, :, 0:TOK], gated_in[...])
    wait_all(late)
    mixer_weight_grads(here, grads, branch, turned, grads_in, branch_in, total)
    small_sum = small[...] + small_in[...]
    total[:, :, :, :, :, SMALL_AT:MIX_HALF] = (
        jnp.transpose(small_sum).astype(HALF).reshape(GRID + (16, LANE))
    )
    mix_rings = reduce_rings(here, mail, total, 0, MIX_PARTS, MIX_REDUCE, mix_near, mix_far, 0)
    start_all(mix_rings)
    finish_all(ffn_rings)
    ffn_rings = reduce_rings(here, mail, ffn, ffn_base, FFN_PARTS, FFN_REDUCE, ffn_near, ffn_far, 1)
    start_all(ffn_rings)
    relay_all(mix_rings)
    relay_all(ffn_rings)
    edge.wait_recv()
    d_first = (
        d_normed[0:TOK] + flags[:, 3:4] * edge_in[0:1] + flags[:, 4:5] * edge_in[1:2]
    )
    grad_tokens[...] = (d_resid[...] + norm_back(unit, scale, rows[0:1], d_first)).astype(HALF)
    finish_all(mix_rings)
    mix_rings = reduce_rings(here, mail, total, 0, MIX_PARTS, MIX_REDUCE, mix_near, mix_far, 1)
    start_all(mix_rings)
    finish_all(ffn_rings)
    copies = []
    for step in (1, 3, 2):
        there = here.ring("x", step)
        copies.append(
            mail.post(
                blocks(ffn, {**here.at, "x": there}, cut(ffn_base, FFN_HALF)),
                ffn_rest.at[x],
                here.beside("x", step),
            )
        )
    ffn_rest[x] = ffn_own[...]
    relay_all(mix_rings)
    out_ring.finish()
    mixed_out[...] = (flags[:, 2:3] * (resid[...] + ffn_work[x].astype(FLOAT))).astype(HALF)
    finish_all(mix_rings)
    mix_rings = reduce_rings(here, mail, total, 0, MIX_PARTS, MIX_REDUCE, mix_near, mix_far, 2)
    start_all(mix_rings)
    wait_all(copies)
    ffn_swap = mail.post(ffn_rest, ffn_mate, twin)
    ffn_owned[:, :, cut(core * FFN_HALF, FFN_HALF)] = ffn_rest[...].astype(FLOAT)
    relay_all(mix_rings)
    ffn_swap.wait_recv()
    ffn_owned[:, :, cut((1 - core) * FFN_HALF, FFN_HALF)] = ffn_mate[...].astype(FLOAT)
    finish_all(mix_rings)
    own_sum = blocks(total, here.at, slice(None))
    mix_swap = mail.post(own_sum, mix_mate, twin)
    mix_owned[:, cut(core * MIX_HALF, MIX_HALF)] = own_sum[...].astype(FLOAT)
    mix_swap.wait_recv()
    mix_owned[:, cut((1 - core) * MIX_HALF, MIX_HALF)] = mix_mate[...].astype(FLOAT)
    mail.settle(len(mail.posted))


def vmem():
    return pl.BlockSpec(memory_space=pltpu.VMEM)


def sems(count):
    return pltpu.SemaphoreType.DMA((count,))


def params(number):
    return pltpu.CompilerParams(
        collective_id=number, has_side_effects=True, vmem_limit_bytes=VMEM_LIMIT
    )


def shape(dims, dtype):
    return jax.ShapeDtypeStruct(dims, dtype)


def whole_block(own, tail, tokens, flags, cotangent):
    landing = [
        pltpu.VMEM(dims, HALF)
        for part in landing_shapes(MIX_PARTS, MIX_REDUCE) + landing_shapes(FFN_PARTS, FFN_REDUCE)
        for dims in part
    ]
    stream_landing = [pltpu.VMEM((TOK, D), HALF)] * 2 + [pltpu.VMEM((TOK // 2, D), HALF)] * 2
    return pl.pallas_call(
        block_kernel,
        out_shape=(
            shape((TOK, D), HALF),
            shape((TOK, D), HALF),
            shape((16, MIX_COLS), FLOAT),
            shape((4, 16, FFN_COLS), FLOAT),
        ),
        in_specs=[vmem()] * 5,
        out_specs=(vmem(),) * 4,
        scratch_shapes=[
            pltpu.VMEM((16, OWN_COLS), HALF),
            pltpu.VMEM((16, OWN_COLS), HALF),
            pltpu.VMEM((16, D), HALF),
            pltpu.VMEM(GRID + (16, MIX_COLS), HALF),
            pltpu.VMEM(GRID + (16, FFN_COLS), HALF),
            pltpu.VMEM((4, TOK, D), HALF),
            pltpu.VMEM((4, TOK, D), HALF),
            pltpu.VMEM((3, ALL, D), FLOAT),
            pltpu.VMEM((ALL, D), HALF),
            pltpu.VMEM((TOK, D), HALF),
            pltpu.VMEM((TOK, D), FLOAT),
            pltpu.VMEM((8, D), FLOAT),
            pltpu.VMEM((4 * TOK, FFN_COLS), HALF),
            pltpu.VMEM((2, D, 4 * TOK), HALF),
            pltpu.VMEM(GRID + (16, MIX_HALF), HALF),
            pltpu.VMEM((16, MIX_HALF), HALF),
            pltpu.VMEM(GRID + (16, FFN_HALF), HALF),
            pltpu.VMEM((4, 16, FFN_HALF), HALF),
            pltpu.VMEM((4, 16, FFN_HALF), HALF),
            pltpu.VMEM((4, TOK, D), HALF),
            pltpu.VMEM((4, TOK, D), HALF),
            pltpu.VMEM((2, TOK, HALF_D), HALF),
            pltpu.VMEM((2, ALL, OUT_AT), HALF),
            pltpu.VMEM((ALL, D), FLOAT),
            pltpu.VMEM((LANE, D), FLOAT),
            pltpu.VMEM((4, D, ALL), HALF),
            pltpu.VMEM((ALL, D), HALF),
            pltpu.VMEM((TOK, D), HALF),
            pltpu.VMEM((TOK, HALF_D), HALF),
            pltpu.VMEM((ALL, OUT_AT), HALF),
            pltpu.VMEM((LANE, D), FLOAT),
            pltpu.VMEM((8, D), FLOAT),
            pltpu.VMEM((TOK, D), FLOAT),
        ]
        + stream_landing * 2
        + landing
        + [sems(176), sems(176), sems(2)],
        compiler_params=params(0),
        name="whole_block",
    )(own, tail, tokens, flags, cotangent)


def local(
    tokens,
    gain_mix,
    in_weight,
    conv_weight,
    out_weight,
    gain_ffn,
    gate_weight,
    up_weight,
    down_weight,
    live_counts,
    positions,
    cotangent,
):
    core = lax.rem(lax.axis_index("seq"), 2)
    count = live_counts[0, 0]
    small = jnp.stack([gain_mix, gain_ffn, conv_weight[0], conv_weight[1], conv_weight[2]], axis=1)
    small = jnp.pad(small, ((0, 0), (0, LANE - 5)))
    mix_rows = jnp.concatenate(
        [
            in_weight.reshape(8, 3, 2, HALF_D).transpose(0, 2, 1, 3).reshape(8, 2, OUT_AT),
            out_weight.reshape(8, 2, HALF_D),
            jnp.stack([small, small], axis=1),
        ],
        axis=2,
    )
    ffn_rows = [
        weight.reshape(8, 4, SLAB) for weight in (gate_weight, up_weight, jnp.transpose(down_weight))
    ]
    ffn_rows = jnp.concatenate(ffn_rows + [jnp.zeros((8, 4, FFN_COLS - 3 * SLAB), HALF)], axis=2)
    ffn_rows = ffn_rows.reshape(8, 4, 2, FFN_HALF).transpose(0, 2, 1, 3).reshape(8, 2, 4 * FFN_HALF)
    own = jnp.concatenate([mix_rows, ffn_rows], axis=2).transpose(1, 0, 2)
    own = jnp.concatenate([own, own], axis=1)
    tail = jnp.pad(lax.dynamic_slice(tokens, (count - 2, 0), (2, D)), ((0, 14), (0, 0)))
    slots = jnp.arange(TOK, dtype=jnp.int32)
    flags = jnp.stack(
        [positions >= 1, positions >= 2, slots < count, slots == count - 2, slots == count - 1], axis=1
    )
    flags = jnp.pad(flags.astype(FLOAT), ((0, 0), (0, LANE - 5)))
    mixed_out, grad_tokens, owned_mix, owned_ffn = whole_block(own, tail, tokens, flags, cotangent)
    mine = lax.dynamic_slice(owned_mix, (8 * core, 0), (8, MIX_COLS)).reshape(8, 2, MIX_HALF)
    ffn_mine = lax.dynamic_slice(owned_ffn, (0, 8 * core, 0), (4, 8, FFN_COLS))
    ffn_mine = jnp.transpose(ffn_mine, (1, 0, 2))
    small_mine = jnp.transpose(mine[:, 0, SMALL_AT : SMALL_AT + 8])
    grad_in = mine[:, :, :OUT_AT].reshape(8, 2, 3, HALF_D).transpose(0, 2, 1, 3).reshape(8, 3 * D)
    return (
        mixed_out,
        grad_tokens,
        small_mine[0],
        grad_in,
        small_mine[2:5],
        mine[:, :, OUT_AT:SMALL_AT].reshape(8, D),
        small_mine[1],
        ffn_mine[:, :, :SLAB].reshape(8, 4 * SLAB),
        ffn_mine[:, :, SLAB : 2 * SLAB].reshape(8, 4 * SLAB),
        jnp.transpose(ffn_mine[:, :, 2 * SLAB : 3 * SLAB].reshape(8, 4 * SLAB)),
    )


def solution(mesh):
    rows = P(("fsdp", "seq"), None)
    flat = P(("fsdp", "seq"))
    cols = P(None, ("fsdp", "seq"))
    return jax.shard_map(
        local,
        mesh=mesh,
        in_specs=(rows, flat, rows, cols, rows, flat, rows, rows, cols, P("fsdp", "seq"), flat, rows),
        out_specs=(rows, rows, flat, rows, cols, rows, flat, rows, rows, cols),
        check_vma=False,
    )
```

```python
import jax
import jax.numpy as jnp
from jax import lax
from jax.experimental import pallas as pl
from jax.experimental.pallas import tpu as pltpu
from jax.sharding import PartitionSpec as P

EPS = 1e-05
FLOAT = jnp.float32
HALF = jnp.bfloat16
MESH = pl.DeviceIdType.MESH
LANE = 128
D = 1024
SLAB = 1152
MIX_COLS = 34 * LANE
FFN_COLS = 28 * LANE
MIX_HALF = MIX_COLS // 2
FFN_HALF = FFN_COLS // 2
OWN_COLS = MIX_HALF + 4 * FFN_HALF
HALF_D = D // 2
OUT_AT = 3 * HALF_D
SMALL_AT = 4 * HALF_D
TILE = 256
TOK = 128
ALL = TOK + 16
MIX_PARTS = ((0, 6), (6, 6), (12, 5))
MIX_GATHER = (("y", "z", "x"), ("z", "x", "y"), ("x", "y", "z"))
MIX_REDUCE = (("x", "z", "y"), ("y", "x", "z"), ("z", "y", "x"))
FFN_PARTS = ((0, 8), (8, 6))
FFN_GATHER = (("y", "z"), ("z", "y"))
FFN_REDUCE = (("y", "z"), ("z", "y"))
GRID = (2, 4, 4, 2)
MIX_LANDING = 4 * 3 * len(MIX_PARTS)
VMEM_LIMIT = 60 * 2**20


class Here:
    def __init__(self):
        fsdp = lax.axis_index("fsdp")
        seq = lax.axis_index("seq")
        self.fsdp, self.seq = fsdp, seq
        self.at = {
            "x": lax.div(seq, 4),
            "y": lax.rem(fsdp, 4),
            "z": lax.div(fsdp, 4) * 2 + lax.rem(lax.div(seq, 2), 2),
        }
        self.core = lax.rem(seq, 2)

    def device(self, core, **moved):
        at = {**self.at, **moved}
        return (
            lax.div(at["z"], 2) * 4 + at["y"],
            (at["x"] * 2 + lax.rem(at["z"], 2)) * 2 + core,
        )

    def ring(self, axis, step):
        return lax.rem(self.at[axis] + (step + 4) % 4, 4)

    def beside(self, axis, step):
        return self.device(self.core, **{axis: self.ring(axis, step)})

    def twin(self):
        return self.device(1 - self.core)

    def along(self, step):
        return (self.fsdp, lax.rem(self.seq + (step + 16) % 16, 16))


def greet(devices):
    barrier = pltpu.get_barrier_semaphore()
    for device in devices:
        pl.semaphore_signal(barrier, inc=1, device_id=device, device_id_type=MESH)
    return barrier, len(devices)


class Mail:
    def __init__(self, send, recv):
        self.send, self.recv, self.posted, self.settled = send, recv, [], 0

    def post(self, src, dst, device):
        place = len(self.posted)
        copy = pltpu.make_async_remote_copy(
            src_ref=src,
            dst_ref=dst,
            send_sem=self.send.at[place],
            recv_sem=self.recv.at[place],
            device_id=device,
            device_id_type=MESH,
        )
        copy.start()
        self.posted.append(copy)
        return copy

    def settle(self, count):
        for copy in self.posted[self.settled : count]:
            copy.wait_send()
        self.settled = count


def cut(start, count):
    return pl.ds(pl.multiple_of(start, LANE), count)


def blocks(ref, at, cols):
    whole = slice(None)
    z = at["z"]
    high, low = (whole, whole) if z is None else (lax.div(z, 2), lax.rem(z, 2))
    y = whole if at["y"] is None else at["y"]
    x = whole if at["x"] is None else at["x"]
    return ref.at[high, y, x, low, :, cols]


class RingGather:
    def __init__(self, here, mail, axis, pick):
        self.here, self.mail, self.axis, self.pick = here, mail, axis, pick

    def start(self, source=None):
        here, axis = self.here, self.axis
        own = self.pick(here.at[axis], None)
        source = own if source is None else source
        self.to_up = self.mail.post(source, own, here.beside(axis, 1))
        self.to_down = self.mail.post(source, own, here.beside(axis, -1))

    def relay(self):
        here, axis = self.here, self.axis
        self.to_up.wait_recv()
        first = self.pick(here.ring(axis, -1), 0)
        self.far_up = self.mail.post(first, first, here.beside(axis, 1))
        self.to_down.wait_recv()
        second = self.pick(here.ring(axis, 1), 1)
        self.far_down = self.mail.post(second, second, here.beside(axis, -1))

    def finish(self):
        self.far_up.wait_recv()
        self.far_down.wait_recv()


class RingReduce:
    def __init__(self, here, mail, axis, pick, near, far):
        self.here, self.mail, self.axis, self.pick = here, mail, axis, pick
        self.near, self.far = near, far

    def start(self):
        here, axis = self.here, self.axis
        away = here.ring(axis, 2)
        self.far_up = self.mail.post(self.pick(away, 0), self.far[0], here.beside(axis, 1))
        self.far_down = self.mail.post(self.pick(away, 1), self.far[1], here.beside(axis, -1))

    def relay(self):
        here, axis = self.here, self.axis
        above, below = here.ring(axis, 1), here.ring(axis, -1)
        self.far_up.wait_recv()
        add_into(self.pick(above, 0), self.far[0])
        self.to_up = self.mail.post(self.pick(above, None), self.near[0], here.beside(axis, 1))
        self.far_down.wait_recv()
        add_into(self.pick(below, 1), self.far[1])
        self.to_down = self.mail.post(self.pick(below, None), self.near[1], here.beside(axis, -1))

    def finish(self):
        self.to_up.wait_recv()
        self.to_down.wait_recv()
        own = self.pick(self.here.at[self.axis], None)
        add_into(own, self.near[0], self.near[1])


class DirectGather(RingGather):
    def start(self, source=None):
        here, axis = self.here, self.axis
        own = self.pick(here.at[axis], None)
        source = own if source is None else source
        self.copies = [
            self.mail.post(source, own, here.beside(axis, step)) for step in (1, -1, 2)
        ]

    def relay(self):
        pass

    def finish(self):
        wait_all(self.copies)


class DirectReduce(RingReduce):
    def start(self):
        here, axis = self.here, self.axis
        self.landed = [self.near[0], self.near[1], self.far[0]]
        self.copies = [
            self.mail.post(
                self.pick(here.ring(axis, step), None), landed, here.beside(axis, step)
            )
            for step, landed in zip((1, -1, 2), self.landed)
        ]

    def relay(self):
        pass

    def finish(self):
        wait_all(self.copies)
        add_into(self.pick(self.here.at[self.axis], None), *self.landed)


def add_into(target, *terms):
    if len(terms) == 1:
        target[...] = target[...] + terms[0][...]
        return
    total = target[...].astype(FLOAT)
    for term in terms:
        total = total + term[...].astype(FLOAT)
    target[...] = total.astype(target.dtype)


def column_pick(ref, fixed, axis, start, chunks):
    split = (chunks + 1) // 2

    def pick(place, half):
        first, count = {None: (0, chunks), 0: (0, split), 1: (split, chunks - split)}[half]
        return blocks(ref, {**fixed, axis: place}, cut(start + first * LANE, count * LANE))

    return pick


def row_pick(ref):
    def pick(place, half):
        rows = ref.shape[-2]
        part = {None: slice(None), 0: pl.ds(0, rows // 2), 1: pl.ds(rows // 2, rows // 2)}[half]
        return ref.at[place, part]

    return pick


def gather_rings(here, mail, ref, base, parts, orders, stage, kind=RingGather):
    rings = []
    for (first, chunks), order in zip(parts, orders):
        fixed = dict(here.at)
        for axis in ("x", "y", "z"):
            if axis not in order or axis in order[:stage]:
                fixed[axis] = None
        pick = column_pick(ref, fixed, order[stage], base + first * LANE, chunks)
        rings.append(kind(here, mail, order[stage], pick))
    return rings


def start_all(rings):
    for ring in rings:
        ring.start()


def relay_all(rings):
    for ring in rings:
        ring.relay()


def finish_all(rings):
    for ring in rings:
        ring.finish()


def run_rings(rings):
    start_all(rings)
    relay_all(rings)
    finish_all(rings)


def swap_pieces(here, mail, rings, steps):
    copies = []
    for ring in rings:
        for step in steps:
            piece = ring.pick(here.ring(ring.axis, step), None)
            copies.append(mail.post(piece, piece, here.twin()))
    return copies


def wait_all(copies):
    for copy in copies:
        copy.wait_recv()


def near_list(here, axes):
    return [here.beside(axis, step) for axis in axes for step in (1, -1)]


def mat(ref, cols):
    block = ref[:, :, :, :, :, cols]
    return block.reshape(D, block.shape[-1])


def mat_rows(ref, tile, cols):
    block = ref[lax.div(tile, 2), pl.ds(lax.rem(tile, 2) * 2, 2), :, :, :, cols]
    return block.reshape(TILE, block.shape[-1])


def mix_cols(tile, which):
    return cut(lax.div(tile, 2) * MIX_HALF + which * HALF_D + lax.rem(tile, 2) * TILE, TILE)


def dot(left, right):
    return jnp.dot(left, right, preferred_element_type=FLOAT)


def dot_nt(left, right):
    return lax.dot_general(
        left, right, (((1,), (1,)), ((), ())), preferred_element_type=FLOAT
    )


def norm_scale(values):
    return lax.rsqrt(jnp.mean(values * values, axis=-1, keepdims=True) + EPS)


def norm_back(normal, row_scale, gain_row, upstream):
    weighted = upstream * gain_row
    return row_scale * (
        weighted - normal * jnp.mean(weighted * normal, axis=-1, keepdims=True)
    )


def row_index(rows, cols):
    return lax.broadcasted_iota(jnp.int32, (rows, cols), 0)


def conv_terms(mixed, halo):
    rows = row_index(TOK, mixed.shape[1])
    one = pltpu.roll(mixed, 1, 0)
    two = pltpu.roll(mixed, 2, 0)
    one = jnp.where(rows == 0, halo[1:2], one)
    two = jnp.where(rows == 0, halo[0:1], jnp.where(rows == 1, halo[1:2], two))
    return one, two


def follows_of(here):
    return jnp.minimum(here.seq, 1).astype(FLOAT)


def mixer_forward(here, tokens, halo, flags, mix, proj, normed, gated, resid, rows, two):
    small = jnp.transpose(mat(mix, slice(SMALL_AT, SMALL_AT + LANE)).astype(FLOAT))
    rows[...] = small[0:8]
    gain = rows[0:1]
    x = tokens[...].astype(FLOAT)
    normed[0:TOK] = (x * norm_scale(x) * gain).astype(HALF)
    before = halo[...].astype(FLOAT)
    normed[TOK:ALL] = (before * norm_scale(before) * gain).astype(HALF)
    follows = follows_of(here)
    first_ok, second_ok = flags[:, 0:1], flags[:, 1:2]

    @pl.loop(0, D // TILE)
    def _(tile):
        feats = cut(tile * TILE, TILE)
        parts = [dot(normed[...], mat(mix, mix_cols(tile, which))) for which in range(3)]
        for which in range(3):
            proj[which, :, feats] = parts[which]
        mixed = parts[0] * parts[2]
        own = mixed[0:TOK]
        one, second = conv_terms(own, mixed[TOK:ALL] * follows)
        conv = (
            rows[2:3, feats] * own
            + first_ok * rows[3:4, feats] * one
            + second_ok * rows[4:5, feats] * second
        )
        gated[:, feats] = (parts[1][0:TOK] * conv).astype(HALF)

    @pl.loop(0, D // TILE)
    def _(tile):
        feats = cut(tile * TILE, TILE)
        branch = dot(gated[...], mat(mix, mix_cols(tile, 3)))
        resid[:, feats] = tokens[:, feats].astype(FLOAT) + branch

    value = resid[...]
    two[...] = (value * norm_scale(value) * rows[1:2]).astype(HALF)


def reduce_rings(here, mail, ref, base, parts, orders, near, far, stage):
    rings = []
    for number, ((first, chunks), order) in enumerate(zip(parts, orders)):
        fixed = {"x": None, "y": None, "z": None}
        for axis in order[:stage]:
            fixed[axis] = here.at[axis]
        pick = column_pick(ref, fixed, order[stage], base + first * LANE, chunks)
        kind = RingReduce if stage == 0 else DirectReduce
        rings.append(kind(here, mail, order[stage], pick, near[number][stage], far[number][stage]))
    return rings


def landing_shapes(parts, orders):
    shapes = []
    for (_, chunks), order in zip(parts, orders):
        split = (chunks + 1) // 2
        done = []
        for stage in range(len(order)):
            gone = order[: stage + 1]
            lead = ()
            if "z" not in gone:
                lead += (2,)
            if "y" not in gone:
                lead += (4,)
            if "x" not in gone:
                lead += (4,)
            if "z" not in gone:
                lead += (2,)
            done += [lead + (16, chunks * LANE)] * 2
            if stage == 0:
                done += [lead + (16, split * LANE), lead + (16, (chunks - split) * LANE)]
            else:
                done += [lead + (16, chunks * LANE), (16, LANE)]
        shapes.append(done)
    return shapes


def landing_refs(orders, refs):
    near, far = [], []
    place = 0
    for order in orders:
        near.append([])
        far.append([])
        for _ in order:
            near[-1].append(refs[place : place + 2])
            far[-1].append(refs[place + 2 : place + 4])
            place += 4
    return near, far


def twin_sum(ref, cols, landed, landed_cols):
    @pl.loop(0, 32)
    def _(index):
        high, y = lax.div(index, 16), lax.rem(lax.div(index, 4), 4)
        x = lax.rem(index, 4)
        for low in range(2):
            add_into(ref.at[high, y, x, low, :, cols], landed.at[high, y, x, low, :, landed_cols])


def ffn_hidden(ffn, twos, backs, acts, start, width):
    value = twos[...].reshape(4 * TOK, D)
    gate = dot(value, mat(ffn, cut(start, width)))
    upper = dot(value, mat(ffn, cut(SLAB + start, width)))
    d_active = dot(backs[...].reshape(4 * TOK, D), mat(ffn, cut(2 * SLAB + start, width)))
    sig = jax.nn.sigmoid(gate)
    swish = gate * sig
    acts[:, cut(start, width)] = (d_active * upper * (sig * (1.0 + gate * (1.0 - sig)))).astype(HALF)
    acts[:, cut(SLAB + start, width)] = (d_active * swish).astype(HALF)
    acts[:, cut(2 * SLAB + start, width)] = (swish * upper).astype(HALF)


def ffn_tokens(ffn, acts, target, kinds):
    @pl.loop(0, D // TILE)
    def _(tile):
        total = 0.0
        for kind in kinds:
            cols = slice(kind * SLAB, (kind + 1) * SLAB)
            total += dot_nt(acts[:, cols], mat_rows(ffn, tile, cols))
        target[:, :, cut(tile * TILE, TILE)] = total.astype(HALF).reshape(4, TOK, TILE)


def ffn_weight_grads(ffn, acts, turned, half, part):
    first, chunks = part

    @pl.loop(first * LANE // TILE, (first + chunks) * LANE // TILE)
    def _(tile):
        cols = cut(half * FFN_HALF + tile * TILE, TILE)
        side = half * jnp.minimum(lax.div(tile, 2), 1)
        value = dot(turned[side], acts[:, cols])
        ffn[:, :, :, :, :, cols] = value.astype(HALF).reshape(GRID + (16, TILE))


def turn(target, value):
    target[...] = jnp.transpose(value.astype(FLOAT)).astype(HALF)


def mixer_backward(here, flags, mix, proj, rows, branch, grads, small):
    follows = follows_of(here)
    first_ok, second_ok = flags[:, 0:1], flags[:, 1:2]

    @pl.loop(0, D // TILE)
    def _(tile):
        feats = cut(tile * TILE, TILE)
        gated = dot_nt(branch[0], mat_rows(mix, tile, slice(OUT_AT, OUT_AT + HALF_D)))
        gated += dot_nt(
            branch[1], mat_rows(mix, tile, slice(MIX_HALF + OUT_AT, MIX_HALF + OUT_AT + HALF_D))
        )
        b_all, c_all, v_all = (proj[which, :, feats] for which in range(3))
        mixed = b_all * v_all
        own = mixed[0:TOK]
        one, second = conv_terms(own, mixed[TOK:ALL] * follows)
        tap_one, tap_two = rows[3:4, feats], rows[4:5, feats]
        conv = rows[2:3, feats] * own + first_ok * tap_one * one + second_ok * tap_two * second
        d_c = gated * conv
        d_conv = gated * c_all[0:TOK]
        small[2:3, feats] = jnp.sum(d_conv * own, axis=0, keepdims=True)
        small[3:4, feats] = jnp.sum(d_conv * first_ok * one, axis=0, keepdims=True)
        small[4:5, feats] = jnp.sum(d_conv * second_ok * second, axis=0, keepdims=True)
        term_one = first_ok * tap_one * d_conv
        term_two = second_ok * tap_two * d_conv
        lines = row_index(TOK, TILE)
        zero = jnp.zeros((TOK, TILE), FLOAT)
        d_mixed = (
            rows[2:3, feats] * d_conv
            + jnp.where(lines < TOK - 1, pltpu.roll(term_one, TOK - 1, 0), zero)
            + jnp.where(lines < TOK - 2, pltpu.roll(term_two, TOK - 2, 0), zero)
        )
        lines = row_index(16, TILE)
        zero = jnp.zeros((16, TILE), FLOAT)
        d_halo = follows * (
            jnp.where(lines < 2, term_two[0:16], zero)
            + jnp.where(lines == 1, pltpu.roll(term_one[0:16], 1, 0), zero)
        )
        half, place = lax.div(tile, 2), lax.rem(tile, 2) * TILE
        for which, (main, edge) in enumerate(
            (
                (d_mixed * v_all[0:TOK], d_halo * v_all[TOK:ALL]),
                (d_c, zero),
                (d_mixed * b_all[0:TOK], d_halo * b_all[TOK:ALL]),
            )
        ):
            cols = cut(which * HALF_D + place, TILE)
            grads[half, 0:TOK, cols] = main.astype(HALF)
            grads[half, TOK:ALL, cols] = edge.astype(HALF)


def projection_back(mix, grads, normed_grad):
    @pl.loop(0, D // TILE)
    def _(tile):
        total = dot_nt(grads[0], mat_rows(mix, tile, slice(0, OUT_AT)))
        total += dot_nt(grads[1], mat_rows(mix, tile, slice(MIX_HALF, MIX_HALF + OUT_AT)))
        normed_grad[:, cut(tile * TILE, TILE)] = total


def mixer_weight_grads(here, grads, branch, turned, grads_in, branch_in, total):
    def put(cols, value):
        total[:, :, :, :, :, cols] = value.astype(HALF).reshape(GRID + (16, TILE))

    @pl.loop(0, OUT_AT // TILE)
    def _(tile):
        cols = cut(tile * TILE, TILE)
        put(cols, dot(turned[0], grads[here.core, :, cols]) + dot(turned[1], grads_in[:, cols]))

    @pl.loop(0, HALF_D // TILE)
    def _(tile):
        cols = cut(tile * TILE, TILE)
        value = dot(turned[2, :, 0:TOK], branch[here.core, :, cols])
        value += dot(turned[3, :, 0:TOK], branch_in[:, cols])
        put(cut(OUT_AT + tile * TILE, TILE), value)


def twice(value):
    value = value.astype(FLOAT)
    return jnp.concatenate([value, value], axis=0).astype(HALF)


def lay_out(own, in_rows, out_rows, gate_rows, up_rows, down_rows, small_rows):
    for half in range(2):
        for which in range(3):
            start = which * D + half * HALF_D
            own[half, :, which * HALF_D : (which + 1) * HALF_D] = twice(
                in_rows[:, start : start + HALF_D]
            )
        own[half, :, OUT_AT:SMALL_AT] = twice(out_rows[:, half * HALF_D : (half + 1) * HALF_D])
        own[half, :, SMALL_AT:MIX_HALF] = twice(small_rows[...])
    early = FFN_HALF - SLAB
    rest = SLAB - early
    for place in range(4):
        at, start = MIX_HALF + place * FFN_HALF, place * SLAB
        own[0, :, at : at + SLAB] = twice(gate_rows[:, start : start + SLAB])
        own[0, :, at + SLAB : at + FFN_HALF] = twice(up_rows[:, start : start + early])
        own[1, :, at : at + rest] = twice(up_rows[:, start + early : start + SLAB])
        own[1, :, at + rest : at + rest + SLAB] = twice(down_rows[:, start : start + SLAB])
        own[1, :, at + rest + SLAB : at + FFN_HALF] = jnp.zeros((16, LANE), HALF)


def block_kernel(
    in_rows, out_rows, gate_rows, up_rows, down_rows, small_rows, tail, tokens, flags, cotangent,
    mixed_out, grad_tokens, grad_in, grad_out, grad_small, grad_gate, grad_up, grad_down,
    own, mix_owned, ffn_owned,
    mate, full, halo, mix, ffn, twos, backs, proj, normed, gated, resid, rows, acts, turned_ffn,
    total, mix_mate, ffn_landed, ffn_rest, ffn_mate, work, ffn_work,
    branch, grads, d_normed, small, turned, normed_in, gated_in, branch_in, grads_in, small_in,
    edge_in, d_resid, *scratch,
):
    two_near, two_far = scratch[0:2], scratch[2:4]
    out_near, out_far = scratch[4:6], scratch[6:8]
    *landing, send, recv, local_sem = scratch[8:]
    mix_near, mix_far = landing_refs(MIX_REDUCE, landing[:MIX_LANDING])
    ffn_near, ffn_far = landing_refs(FFN_REDUCE, landing[MIX_LANDING:])
    here = Here()
    mail = Mail(send, recv)
    x, core = here.at["x"], here.core
    twin = here.twin()
    barrier, count = greet(
        near_list(here, ("x", "y", "z"))
        + [here.beside(axis, 2) for axis in ("x", "y", "z")]
        + [twin, here.along(1), here.along(-1)]
    )
    lay_out(own, in_rows, out_rows, gate_rows, up_rows, down_rows, small_rows)
    pl.semaphore_wait(barrier, count)
    rows_in = mail.post(own.at[1 - core], mate, twin)
    halo_in = mail.post(tail, halo, here.along(1))
    backs[x] = (flags[:, 2:3] * cotangent[...].astype(FLOAT)).astype(HALF)
    acts[:, 3 * SLAB : FFN_COLS] = jnp.zeros((4 * TOK, FFN_COLS - 3 * SLAB), HALF)
    rows_in.wait_recv()
    mine = lax.broadcasted_iota(jnp.int32, (16, OWN_COLS), 0) // 8 == core
    full[...] = jnp.where(mine, own[core].astype(FLOAT), mate[...].astype(FLOAT)).astype(HALF)

    mix_base, ffn_base = core * MIX_HALF, core * FFN_HALF
    ffn_own = blocks(ffn, here.at, cut(ffn_base, FFN_HALF))

    def slab(place):
        return full.at[:, cut(MIX_HALF + place * FFN_HALF, FFN_HALF)]

    rings = gather_rings(here, mail, mix, mix_base, MIX_PARTS, MIX_GATHER, 0, DirectGather)
    for ring, (first, chunks) in zip(rings, MIX_PARTS):
        ring.start(full.at[:, first * LANE : (first + chunks) * LANE])
    slabs = [
        mail.post(slab(here.ring("x", step)), ffn_own, here.beside("x", step)) for step in (1, 3, 2)
    ]
    keep_mix = pltpu.make_async_copy(
        full.at[:, 0:MIX_HALF], blocks(mix, here.at, cut(mix_base, MIX_HALF)), local_sem.at[0]
    )
    keep_slab = pltpu.make_async_copy(slab(x), ffn_own, local_sem.at[1])
    keep_mix.start()
    keep_slab.start()
    finish_all(rings)
    keep_mix.wait()
    mix_rings = gather_rings(here, mail, mix, mix_base, MIX_PARTS, MIX_GATHER, 1, DirectGather)
    start_all(mix_rings)
    keep_slab.wait()
    wait_all(slabs)
    ffn_rings = gather_rings(here, mail, ffn, ffn_base, FFN_PARTS, FFN_GATHER, 0)
    start_all(ffn_rings)
    stream = RingGather(here, mail, "x", row_pick(backs))
    stream.start()
    finish_all(mix_rings)
    mix_rings = gather_rings(here, mail, mix, mix_base, MIX_PARTS, MIX_GATHER, 2)
    start_all(mix_rings)
    swaps = swap_pieces(here, mail, mix_rings, (0,))
    relay_all(ffn_rings)
    relay_all(mix_rings)
    swaps += swap_pieces(here, mail, mix_rings, (1, -1))
    finish_all(ffn_rings)
    ffn_rings = gather_rings(here, mail, ffn, ffn_base, FFN_PARTS, FFN_GATHER, 1)
    stream.relay()
    finish_all(mix_rings)
    swaps += swap_pieces(here, mail, mix_rings, (2,))
    start_all(ffn_rings)
    ffn_swaps = swap_pieces(here, mail, ffn_rings, (0,))
    wait_all(swaps)
    halo_in.wait_recv()
    mixer_forward(here, tokens, halo, flags, mix, proj, normed, gated, resid, rows, twos.at[x])
    two_ring = RingGather(here, mail, "x", row_pick(twos))
    two_ring.start()
    relay_all(ffn_rings)
    ffn_swaps += swap_pieces(here, mail, ffn_rings, (1, -1))
    early = [mail.post(normed, normed_in, twin), mail.post(gated, gated_in, twin)]
    two_ring.relay()
    turn(turned.at[0, :, 0:ALL], normed[...])
    turn(turned.at[2, :, 0:TOK], gated[...])
    finish_all(ffn_rings)
    ffn_swaps += swap_pieces(here, mail, ffn_rings, (2,))
    stream.finish()
    for block in range(4):
        turn(turned_ffn.at[1, :, block * TOK : (block + 1) * TOK], backs[block])
    wait_all(ffn_swaps)
    two_ring.finish()
    gathered = len(mail.posted)

    @pl.loop(0, SLAB // TILE)
    def _(tile):
        ffn_hidden(ffn, twos, backs, acts, tile * TILE, TILE)

    ffn_hidden(ffn, twos, backs, acts, SLAB // TILE * TILE, SLAB % TILE)
    ffn_tokens(ffn, acts, work, (0, 1))
    two_ring = RingReduce(here, mail, "x", row_pick(work), two_near, two_far)
    two_ring.start()
    ffn_tokens(ffn, acts, ffn_work, (2,))
    for block in range(4):
        turn(turned_ffn.at[0, :, block * TOK : (block + 1) * TOK], twos[block])
    mail.settle(gathered)
    pieces, base = [], (1 - core) * FFN_HALF
    for number, (first, chunks) in enumerate(FFN_PARTS):
        ffn_weight_grads(ffn, acts, turned_ffn, 1 - core, (first, chunks))
        piece = slice(first * LANE, (first + chunks) * LANE)
        pieces.append(
            mail.post(
                ffn.at[:, :, :, :, :, cut(base + first * LANE, chunks * LANE)],
                ffn_landed.at[:, :, :, :, :, piece],
                twin,
            )
        )
        if number == 0:
            two_ring.relay()
    ffn_rings = reduce_rings(here, mail, ffn, ffn_base, FFN_PARTS, FFN_REDUCE, ffn_near, ffn_far, 0)
    for part in FFN_PARTS:
        ffn_weight_grads(ffn, acts, turned_ffn, core, part)

    def join(number):
        first, chunks = FFN_PARTS[number]
        pieces[number].wait_recv()
        twin_sum(
            ffn,
            cut(ffn_base + first * LANE, chunks * LANE),
            ffn_landed,
            slice(first * LANE, (first + chunks) * LANE),
        )
        ffn_rings[number].start()

    join(0)
    two_ring.finish()
    value = resid[...]
    scale = norm_scale(value)
    unit = value * scale
    d_two = work[x].astype(FLOAT)
    small[...] = jnp.zeros_like(small)
    small[1:2] = jnp.sum(d_two * unit, axis=0, keepdims=True)
    d_value = flags[:, 2:3] * cotangent[...].astype(FLOAT) + norm_back(unit, scale, rows[1:2], d_two)
    d_resid[...] = d_value
    branch[0] = d_value[:, 0:HALF_D].astype(HALF)
    branch[1] = d_value[:, HALF_D:D].astype(HALF)
    late = [mail.post(branch.at[1 - core], branch_in, twin)]
    out_ring = RingReduce(here, mail, "x", row_pick(ffn_work), out_near, out_far)
    out_ring.start()
    join(1)
    mixer_backward(here, flags, mix, proj, rows, branch, grads, small)
    late.append(mail.post(grads.at[1 - core], grads_in, twin))
    relay_all(ffn_rings)
    out_ring.relay()
    projection_back(mix, grads, d_normed)
    x_own, x_edge = tokens[...].astype(FLOAT), halo[...].astype(FLOAT)
    scale = norm_scale(x_own)
    unit = x_own * scale
    small[0:1] = jnp.sum(d_normed[0:TOK] * unit, axis=0, keepdims=True) + jnp.sum(
        d_normed[TOK:ALL] * x_edge * norm_scale(x_edge), axis=0, keepdims=True
    )
    late.append(mail.post(small, small_in, twin))
    edge = mail.post(d_normed.at[pl.ds(TOK, 8)], edge_in, here.along(-1))
    wait_all(early)
    turn(turned.at[1, :, 0:ALL], normed_in[...])
    turn(turned.at[3, :, 0:TOK], gated_in[...])
    wait_all(late)
    mixer_weight_grads(here, grads, branch, turned, grads_in, branch_in, total)
    small_sum = small[...] + small_in[...]
    total[:, :, :, :, :, SMALL_AT:MIX_HALF] = (
        jnp.transpose(small_sum).astype(HALF).reshape(GRID + (16, LANE))
    )
    mix_rings = reduce_rings(here, mail, total, 0, MIX_PARTS, MIX_REDUCE, mix_near, mix_far, 0)
    start_all(mix_rings)
    finish_all(ffn_rings)
    ffn_rings = reduce_rings(here, mail, ffn, ffn_base, FFN_PARTS, FFN_REDUCE, ffn_near, ffn_far, 1)
    start_all(ffn_rings)
    relay_all(mix_rings)
    relay_all(ffn_rings)
    edge.wait_recv()
    d_first = (
        d_normed[0:TOK] + flags[:, 3:4] * edge_in[0:1] + flags[:, 4:5] * edge_in[1:2]
    )
    grad_tokens[...] = (d_resid[...] + norm_back(unit, scale, rows[0:1], d_first)).astype(HALF)
    finish_all(mix_rings)
    mix_rings = reduce_rings(here, mail, total, 0, MIX_PARTS, MIX_REDUCE, mix_near, mix_far, 1)
    start_all(mix_rings)
    finish_all(ffn_rings)
    copies = []
    for step in (1, 3, 2):
        there = here.ring("x", step)
        copies.append(
            mail.post(
                blocks(ffn, {**here.at, "x": there}, cut(ffn_base, FFN_HALF)),
                ffn_rest.at[x],
                here.beside("x", step),
            )
        )
    ffn_rest[x] = ffn_own[...]
    relay_all(mix_rings)
    out_ring.finish()
    mixed_out[...] = (flags[:, 2:3] * (resid[...] + ffn_work[x].astype(FLOAT))).astype(HALF)
    finish_all(mix_rings)
    mix_rings = reduce_rings(here, mail, total, 0, MIX_PARTS, MIX_REDUCE, mix_near, mix_far, 2)
    start_all(mix_rings)
    wait_all(copies)
    ffn_swap = mail.post(ffn_rest, ffn_mate, twin)
    ffn_owned[:, :, cut(core * FFN_HALF, FFN_HALF)] = ffn_rest[...].astype(FLOAT)
    relay_all(mix_rings)
    ffn_swap.wait_recv()
    ffn_owned[:, :, cut((1 - core) * FFN_HALF, FFN_HALF)] = ffn_mate[...].astype(FLOAT)
    lines = pl.ds(pl.multiple_of(8 * core, 8), 8)
    for place in range(4):
        cols = slice(place * SLAB, (place + 1) * SLAB)
        for kind, target in enumerate((grad_gate, grad_up, grad_down)):
            target[:, cols] = ffn_owned[place, lines, kind * SLAB : (kind + 1) * SLAB]
    finish_all(mix_rings)
    own_sum = blocks(total, here.at, slice(None))
    mix_swap = mail.post(own_sum, mix_mate, twin)
    mix_owned[:, cut(core * MIX_HALF, MIX_HALF)] = own_sum[...].astype(FLOAT)
    mix_swap.wait_recv()
    mix_owned[:, cut((1 - core) * MIX_HALF, MIX_HALF)] = mix_mate[...].astype(FLOAT)
    for half in range(2):
        at = half * MIX_HALF
        for which in range(3):
            start = which * D + half * HALF_D
            grad_in[:, start : start + HALF_D] = mix_owned[
                lines, at + which * HALF_D : at + (which + 1) * HALF_D
            ]
        grad_out[:, half * HALF_D : (half + 1) * HALF_D] = mix_owned[lines, at + OUT_AT : at + SMALL_AT]
    grad_small[...] = mix_owned[lines, SMALL_AT:MIX_HALF]
    mail.settle(len(mail.posted))


def vmem():
    return pl.BlockSpec(memory_space=pltpu.VMEM)


def sems(count):
    return pltpu.SemaphoreType.DMA((count,))


def params(number):
    return pltpu.CompilerParams(
        collective_id=number, has_side_effects=True, vmem_limit_bytes=VMEM_LIMIT
    )


def shape(dims, dtype):
    return jax.ShapeDtypeStruct(dims, dtype)


def whole_block(*operands):
    landing = [
        pltpu.VMEM(dims, HALF)
        for part in landing_shapes(MIX_PARTS, MIX_REDUCE) + landing_shapes(FFN_PARTS, FFN_REDUCE)
        for dims in part
    ]
    stream_landing = [pltpu.VMEM((TOK, D), HALF)] * 2 + [pltpu.VMEM((TOK // 2, D), HALF)] * 2
    return pl.pallas_call(
        block_kernel,
        out_shape=(
            shape((TOK, D), HALF),
            shape((TOK, D), HALF),
            shape((8, 3 * D), FLOAT),
            shape((8, D), FLOAT),
            shape((8, LANE), FLOAT),
            shape((8, 4 * SLAB), FLOAT),
            shape((8, 4 * SLAB), FLOAT),
            shape((8, 4 * SLAB), FLOAT),
        ),
        in_specs=[vmem()] * 10,
        out_specs=(vmem(),) * 8,
        scratch_shapes=[
            pltpu.VMEM((2, 16, OWN_COLS), HALF),
            pltpu.VMEM((16, MIX_COLS), FLOAT),
            pltpu.VMEM((4, 16, FFN_COLS), FLOAT),
            pltpu.VMEM((16, OWN_COLS), HALF),
            pltpu.VMEM((16, OWN_COLS), HALF),
            pltpu.VMEM((16, D), HALF),
            pltpu.VMEM(GRID + (16, MIX_COLS), HALF),
            pltpu.VMEM(GRID + (16, FFN_COLS), HALF),
            pltpu.VMEM((4, TOK, D), HALF),
            pltpu.VMEM((4, TOK, D), HALF),
            pltpu.VMEM((3, ALL, D), FLOAT),
            pltpu.VMEM((ALL, D), HALF),
            pltpu.VMEM((TOK, D), HALF),
            pltpu.VMEM((TOK, D), FLOAT),
            pltpu.VMEM((8, D), FLOAT),
            pltpu.VMEM((4 * TOK, FFN_COLS), HALF),
            pltpu.VMEM((2, D, 4 * TOK), HALF),
            pltpu.VMEM(GRID + (16, MIX_HALF), HALF),
            pltpu.VMEM((16, MIX_HALF), HALF),
            pltpu.VMEM(GRID + (16, FFN_HALF), HALF),
            pltpu.VMEM((4, 16, FFN_HALF), HALF),
            pltpu.VMEM((4, 16, FFN_HALF), HALF),
            pltpu.VMEM((4, TOK, D), HALF),
            pltpu.VMEM((4, TOK, D), HALF),
            pltpu.VMEM((2, TOK, HALF_D), HALF),
            pltpu.VMEM((2, ALL, OUT_AT), HALF),
            pltpu.VMEM((ALL, D), FLOAT),
            pltpu.VMEM((LANE, D), FLOAT),
            pltpu.VMEM((4, D, ALL), HALF),
            pltpu.VMEM((ALL, D), HALF),
            pltpu.VMEM((TOK, D), HALF),
            pltpu.VMEM((TOK, HALF_D), HALF),
            pltpu.VMEM((ALL, OUT_AT), HALF),
            pltpu.VMEM((LANE, D), FLOAT),
            pltpu.VMEM((8, D), FLOAT),
            pltpu.VMEM((TOK, D), FLOAT),
        ]
        + stream_landing * 2
        + landing
        + [sems(176), sems(176), sems(2)],
        compiler_params=params(0),
        name="whole_block",
    )(*operands)


def local(
    tokens,
    gain_mix,
    in_weight,
    conv_weight,
    out_weight,
    gain_ffn,
    gate_weight,
    up_weight,
    down_weight,
    live_counts,
    positions,
    cotangent,
):
    count = live_counts[0, 0]
    small = jnp.stack([gain_mix, gain_ffn, conv_weight[0], conv_weight[1], conv_weight[2]], axis=1)
    small = jnp.pad(small, ((0, 0), (0, LANE - 5)))
    tail = jnp.pad(lax.dynamic_slice(tokens, (count - 2, 0), (2, D)), ((0, 14), (0, 0)))
    slots = jnp.arange(TOK, dtype=jnp.int32)
    flags = jnp.stack(
        [positions >= 1, positions >= 2, slots < count, slots == count - 2, slots == count - 1], axis=1
    )
    flags = jnp.pad(flags.astype(FLOAT), ((0, 0), (0, LANE - 5)))
    mixed_out, grad_tokens, grad_in, grad_out, grad_small, grad_gate, grad_up, grad_down = whole_block(
        in_weight, out_weight, gate_weight, up_weight, jnp.transpose(down_weight), small,
        tail, tokens, flags, cotangent,
    )
    grad_small = jnp.transpose(grad_small[:, :8])
    return (
        mixed_out,
        grad_tokens,
        grad_small[0],
        grad_in,
        grad_small[2:5],
        grad_out,
        grad_small[1],
        grad_gate,
        grad_up,
        jnp.transpose(grad_down),
    )


def solution(mesh):
    rows = P(("fsdp", "seq"), None)
    flat = P(("fsdp", "seq"))
    cols = P(None, ("fsdp", "seq"))
    return jax.shard_map(
        local,
        mesh=mesh,
        in_specs=(rows, flat, rows, cols, rows, flat, rows, rows, cols, P("fsdp", "seq"), flat, rows),
        out_specs=(rows, rows, flat, rows, cols, rows, flat, rows, rows, cols),
        check_vma=False,
    )
```

```python
import jax
import jax.numpy as jnp
from jax import lax
from jax.experimental import pallas as pl
from jax.experimental.pallas import tpu as pltpu
from jax.sharding import PartitionSpec as P

EPS = 1e-05
FLOAT = jnp.float32
HALF = jnp.bfloat16
MESH = pl.DeviceIdType.MESH
LANE = 128
D = 1024
SLAB = 1152
MIX_COLS = 34 * LANE
FFN_COLS = 28 * LANE
MIX_HALF = MIX_COLS // 2
FFN_HALF = FFN_COLS // 2
OWN_COLS = MIX_HALF + 4 * FFN_HALF
HALF_D = D // 2
OUT_AT = 3 * HALF_D
SMALL_AT = 4 * HALF_D
TILE = 256
TOK = 128
ALL = TOK + 16
MIX_PARTS = ((0, 6), (6, 6), (12, 5))
MIX_GATHER = (("y", "z", "x"), ("z", "x", "y"), ("x", "y", "z"))
MIX_REDUCE = (("x", "z", "y"), ("y", "x", "z"), ("z", "y", "x"))
FFN_PARTS = ((0, 8), (8, 6))
FFN_GATHER = (("y", "z"), ("z", "y"))
FFN_REDUCE = (("y", "z"), ("z", "y"))
GRID = (2, 4, 4, 2)
MIX_LANDING = 4 * 3 * len(MIX_PARTS)
VMEM_LIMIT = 60 * 2**20


class Here:
    def __init__(self):
        fsdp = lax.axis_index("fsdp")
        seq = lax.axis_index("seq")
        self.fsdp, self.seq = fsdp, seq
        self.at = {
            "x": lax.div(seq, 4),
            "y": lax.rem(fsdp, 4),
            "z": lax.div(fsdp, 4) * 2 + lax.rem(lax.div(seq, 2), 2),
        }
        self.core = lax.rem(seq, 2)

    def device(self, core, **moved):
        at = {**self.at, **moved}
        return (
            lax.div(at["z"], 2) * 4 + at["y"],
            (at["x"] * 2 + lax.rem(at["z"], 2)) * 2 + core,
        )

    def ring(self, axis, step):
        return lax.rem(self.at[axis] + (step + 4) % 4, 4)

    def beside(self, axis, step):
        return self.device(self.core, **{axis: self.ring(axis, step)})

    def twin(self):
        return self.device(1 - self.core)

    def along(self, step):
        return (self.fsdp, lax.rem(self.seq + (step + 16) % 16, 16))


def greet(devices):
    barrier = pltpu.get_barrier_semaphore()
    for device in devices:
        pl.semaphore_signal(barrier, inc=1, device_id=device, device_id_type=MESH)
    return barrier, len(devices)


class Mail:
    def __init__(self, send, recv):
        self.send, self.recv, self.posted, self.settled = send, recv, [], 0

    def post(self, src, dst, device):
        place = len(self.posted)
        copy = pltpu.make_async_remote_copy(
            src_ref=src,
            dst_ref=dst,
            send_sem=self.send.at[place],
            recv_sem=self.recv.at[place],
            device_id=device,
            device_id_type=MESH,
        )
        copy.start()
        self.posted.append(copy)
        return copy

    def settle(self, count):
        for copy in self.posted[self.settled : count]:
            copy.wait_send()
        self.settled = count


def cut(start, count):
    return pl.ds(pl.multiple_of(start, LANE), count)


def blocks(ref, at, cols):
    whole = slice(None)
    z = at["z"]
    high, low = (whole, whole) if z is None else (lax.div(z, 2), lax.rem(z, 2))
    y = whole if at["y"] is None else at["y"]
    x = whole if at["x"] is None else at["x"]
    return ref.at[high, y, x, low, :, cols]


class RingGather:
    def __init__(self, here, mail, axis, pick):
        self.here, self.mail, self.axis, self.pick = here, mail, axis, pick

    def start(self, source=None):
        here, axis = self.here, self.axis
        own = self.pick(here.at[axis], None)
        source = own if source is None else source
        self.to_up = self.mail.post(source, own, here.beside(axis, 1))
        self.to_down = self.mail.post(source, own, here.beside(axis, -1))

    def relay(self):
        here, axis = self.here, self.axis
        self.to_up.wait_recv()
        first = self.pick(here.ring(axis, -1), 0)
        self.far_up = self.mail.post(first, first, here.beside(axis, 1))
        self.to_down.wait_recv()
        second = self.pick(here.ring(axis, 1), 1)
        self.far_down = self.mail.post(second, second, here.beside(axis, -1))

    def finish(self):
        self.far_up.wait_recv()
        self.far_down.wait_recv()


class RingReduce:
    def __init__(self, here, mail, axis, pick, near, far):
        self.here, self.mail, self.axis, self.pick = here, mail, axis, pick
        self.near, self.far = near, far

    def start(self):
        here, axis = self.here, self.axis
        away = here.ring(axis, 2)
        self.far_up = self.mail.post(self.pick(away, 0), self.far[0], here.beside(axis, 1))
        self.far_down = self.mail.post(self.pick(away, 1), self.far[1], here.beside(axis, -1))

    def relay(self):
        here, axis = self.here, self.axis
        above, below = here.ring(axis, 1), here.ring(axis, -1)
        self.far_up.wait_recv()
        add_into(self.pick(above, 0), self.far[0])
        self.to_up = self.mail.post(self.pick(above, None), self.near[0], here.beside(axis, 1))
        self.far_down.wait_recv()
        add_into(self.pick(below, 1), self.far[1])
        self.to_down = self.mail.post(self.pick(below, None), self.near[1], here.beside(axis, -1))

    def finish(self):
        self.to_up.wait_recv()
        self.to_down.wait_recv()
        own = self.pick(self.here.at[self.axis], None)
        add_into(own, self.near[0], self.near[1])


class DirectGather(RingGather):
    def start(self, source=None):
        here, axis = self.here, self.axis
        own = self.pick(here.at[axis], None)
        source = own if source is None else source
        self.copies = [
            self.mail.post(source, own, here.beside(axis, step)) for step in (1, -1, 2)
        ]

    def relay(self):
        pass

    def finish(self):
        wait_all(self.copies)


class DirectReduce(RingReduce):
    def start(self):
        here, axis = self.here, self.axis
        self.landed = [self.near[0], self.near[1], self.far[0]]
        self.copies = [
            self.mail.post(
                self.pick(here.ring(axis, step), None), landed, here.beside(axis, step)
            )
            for step, landed in zip((1, -1, 2), self.landed)
        ]

    def relay(self):
        pass

    def finish(self):
        wait_all(self.copies)
        add_into(self.pick(self.here.at[self.axis], None), *self.landed)


def add_into(target, *terms):
    if len(terms) == 1:
        target[...] = target[...] + terms[0][...]
        return
    total = target[...].astype(FLOAT)
    for term in terms:
        total = total + term[...].astype(FLOAT)
    target[...] = total.astype(target.dtype)


def column_pick(ref, fixed, axis, start, chunks):
    split = (chunks + 1) // 2

    def pick(place, half):
        first, count = {None: (0, chunks), 0: (0, split), 1: (split, chunks - split)}[half]
        return blocks(ref, {**fixed, axis: place}, cut(start + first * LANE, count * LANE))

    return pick


def row_pick(ref):
    def pick(place, half):
        rows = ref.shape[-2]
        part = {None: slice(None), 0: pl.ds(0, rows // 2), 1: pl.ds(rows // 2, rows // 2)}[half]
        return ref.at[place, part]

    return pick


def gather_rings(here, mail, ref, base, parts, orders, stage, kind=RingGather):
    rings = []
    for (first, chunks), order in zip(parts, orders):
        fixed = dict(here.at)
        for axis in ("x", "y", "z"):
            if axis not in order or axis in order[:stage]:
                fixed[axis] = None
        pick = column_pick(ref, fixed, order[stage], base + first * LANE, chunks)
        rings.append(kind(here, mail, order[stage], pick))
    return rings


def start_all(rings):
    for ring in rings:
        ring.start()


def relay_all(rings):
    for ring in rings:
        ring.relay()


def finish_all(rings):
    for ring in rings:
        ring.finish()


def run_rings(rings):
    start_all(rings)
    relay_all(rings)
    finish_all(rings)


def swap_pieces(here, mail, rings, steps):
    copies = []
    for ring in rings:
        for step in steps:
            piece = ring.pick(here.ring(ring.axis, step), None)
            copies.append(mail.post(piece, piece, here.twin()))
    return copies


def wait_all(copies):
    for copy in copies:
        copy.wait_recv()


def near_list(here, axes):
    return [here.beside(axis, step) for axis in axes for step in (1, -1)]


def mat(ref, cols):
    block = ref[:, :, :, :, :, cols]
    return block.reshape(D, block.shape[-1])


def mat_rows(ref, tile, cols):
    block = ref[lax.div(tile, 2), pl.ds(lax.rem(tile, 2) * 2, 2), :, :, :, cols]
    return block.reshape(TILE, block.shape[-1])


def mix_cols(tile, which):
    return cut(lax.div(tile, 2) * MIX_HALF + which * HALF_D + lax.rem(tile, 2) * TILE, TILE)


def dot(left, right):
    return jnp.dot(left, right, preferred_element_type=FLOAT)


def dot_nt(left, right):
    return lax.dot_general(
        left, right, (((1,), (1,)), ((), ())), preferred_element_type=FLOAT
    )


def norm_scale(values):
    return lax.rsqrt(jnp.mean(values * values, axis=-1, keepdims=True) + EPS)


def norm_back(normal, row_scale, gain_row, upstream):
    weighted = upstream * gain_row
    return row_scale * (
        weighted - normal * jnp.mean(weighted * normal, axis=-1, keepdims=True)
    )


def row_index(rows, cols):
    return lax.broadcasted_iota(jnp.int32, (rows, cols), 0)


def conv_terms(mixed, halo):
    rows = row_index(TOK, mixed.shape[1])
    one = pltpu.roll(mixed, 1, 0)
    two = pltpu.roll(mixed, 2, 0)
    one = jnp.where(rows == 0, halo[1:2], one)
    two = jnp.where(rows == 0, halo[0:1], jnp.where(rows == 1, halo[1:2], two))
    return one, two


def follows_of(here):
    return jnp.minimum(here.seq, 1).astype(FLOAT)


def mixer_forward(here, tokens, halo, flags, mix, proj, normed, gated, resid, rows, two):
    small = jnp.transpose(mat(mix, slice(SMALL_AT, SMALL_AT + LANE)).astype(FLOAT))
    rows[...] = small[0:8]
    gain = rows[0:1]
    x = tokens[...].astype(FLOAT)
    normed[0:TOK] = (x * norm_scale(x) * gain).astype(HALF)
    before = halo[...].astype(FLOAT)
    normed[TOK:ALL] = (before * norm_scale(before) * gain).astype(HALF)
    follows = follows_of(here)
    first_ok, second_ok = flags[:, 0:1], flags[:, 1:2]

    @pl.loop(0, D // TILE)
    def _(tile):
        feats = cut(tile * TILE, TILE)
        parts = [dot(normed[...], mat(mix, mix_cols(tile, which))) for which in range(3)]
        for which in range(3):
            proj[which, :, feats] = parts[which]
        mixed = parts[0] * parts[2]
        own = mixed[0:TOK]
        one, second = conv_terms(own, mixed[TOK:ALL] * follows)
        conv = (
            rows[2:3, feats] * own
            + first_ok * rows[3:4, feats] * one
            + second_ok * rows[4:5, feats] * second
        )
        gated[:, feats] = (parts[1][0:TOK] * conv).astype(HALF)

    @pl.loop(0, D // TILE)
    def _(tile):
        feats = cut(tile * TILE, TILE)
        branch = dot(gated[...], mat(mix, mix_cols(tile, 3)))
        resid[:, feats] = tokens[:, feats].astype(FLOAT) + branch

    value = resid[...]
    two[...] = (value * norm_scale(value) * rows[1:2]).astype(HALF)


def reduce_rings(here, mail, ref, base, parts, orders, near, far, stage):
    rings = []
    for number, ((first, chunks), order) in enumerate(zip(parts, orders)):
        fixed = {"x": None, "y": None, "z": None}
        for axis in order[:stage]:
            fixed[axis] = here.at[axis]
        pick = column_pick(ref, fixed, order[stage], base + first * LANE, chunks)
        kind = RingReduce if stage == 0 else DirectReduce
        rings.append(kind(here, mail, order[stage], pick, near[number][stage], far[number][stage]))
    return rings


def landing_shapes(parts, orders):
    shapes = []
    for (_, chunks), order in zip(parts, orders):
        split = (chunks + 1) // 2
        done = []
        for stage in range(len(order)):
            gone = order[: stage + 1]
            lead = ()
            if "z" not in gone:
                lead += (2,)
            if "y" not in gone:
                lead += (4,)
            if "x" not in gone:
                lead += (4,)
            if "z" not in gone:
                lead += (2,)
            done += [lead + (16, chunks * LANE)] * 2
            if stage == 0:
                done += [lead + (16, split * LANE), lead + (16, (chunks - split) * LANE)]
            else:
                done += [lead + (16, chunks * LANE), (16, LANE)]
        shapes.append(done)
    return shapes


def landing_refs(orders, refs):
    near, far = [], []
    place = 0
    for order in orders:
        near.append([])
        far.append([])
        for _ in order:
            near[-1].append(refs[place : place + 2])
            far[-1].append(refs[place + 2 : place + 4])
            place += 4
    return near, far


def ffn_hidden(ffn, twos, backs, acts, start, width):
    value = twos[...].reshape(4 * TOK, D)
    gate = dot(value, mat(ffn, cut(start, width)))
    upper = dot(value, mat(ffn, cut(SLAB + start, width)))
    d_active = dot(backs[...].reshape(4 * TOK, D), mat(ffn, cut(2 * SLAB + start, width)))
    sig = jax.nn.sigmoid(gate)
    swish = gate * sig
    acts[:, cut(start, width)] = (d_active * upper * (sig * (1.0 + gate * (1.0 - sig)))).astype(HALF)
    acts[:, cut(SLAB + start, width)] = (d_active * swish).astype(HALF)
    acts[:, cut(2 * SLAB + start, width)] = (swish * upper).astype(HALF)


def ffn_tokens(ffn, acts, target, kinds):
    @pl.loop(0, D // TILE)
    def _(tile):
        total = 0.0
        for kind in kinds:
            cols = slice(kind * SLAB, (kind + 1) * SLAB)
            total += dot_nt(acts[:, cols], mat_rows(ffn, tile, cols))
        target[:, :, cut(tile * TILE, TILE)] = total.astype(HALF).reshape(4, TOK, TILE)


def ffn_weight_grads(ffn, acts, acts_in, turned, half, part):
    first, chunks = part

    @pl.loop(first * LANE // TILE, (first + chunks) * LANE // TILE)
    def _(tile):
        cols = cut(half * FFN_HALF + tile * TILE, TILE)
        side = half * jnp.minimum(lax.div(tile, 2), 1)
        value = dot(turned[0, side], acts[:, cols])
        value += dot(turned[1, side], acts_in[:, cut(tile * TILE, TILE)])
        ffn[:, :, :, :, :, cols] = value.astype(HALF).reshape(GRID + (16, TILE))


def turn(target, value):
    target[...] = jnp.transpose(value.astype(FLOAT)).astype(HALF)


def mixer_backward(here, flags, mix, proj, rows, branch, grads, small):
    follows = follows_of(here)
    first_ok, second_ok = flags[:, 0:1], flags[:, 1:2]

    @pl.loop(0, D // TILE)
    def _(tile):
        feats = cut(tile * TILE, TILE)
        gated = dot_nt(branch[0], mat_rows(mix, tile, slice(OUT_AT, OUT_AT + HALF_D)))
        gated += dot_nt(
            branch[1], mat_rows(mix, tile, slice(MIX_HALF + OUT_AT, MIX_HALF + OUT_AT + HALF_D))
        )
        b_all, c_all, v_all = (proj[which, :, feats] for which in range(3))
        mixed = b_all * v_all
        own = mixed[0:TOK]
        one, second = conv_terms(own, mixed[TOK:ALL] * follows)
        tap_one, tap_two = rows[3:4, feats], rows[4:5, feats]
        conv = rows[2:3, feats] * own + first_ok * tap_one * one + second_ok * tap_two * second
        d_c = gated * conv
        d_conv = gated * c_all[0:TOK]
        small[2:3, feats] = jnp.sum(d_conv * own, axis=0, keepdims=True)
        small[3:4, feats] = jnp.sum(d_conv * first_ok * one, axis=0, keepdims=True)
        small[4:5, feats] = jnp.sum(d_conv * second_ok * second, axis=0, keepdims=True)
        term_one = first_ok * tap_one * d_conv
        term_two = second_ok * tap_two * d_conv
        lines = row_index(TOK, TILE)
        zero = jnp.zeros((TOK, TILE), FLOAT)
        d_mixed = (
            rows[2:3, feats] * d_conv
            + jnp.where(lines < TOK - 1, pltpu.roll(term_one, TOK - 1, 0), zero)
            + jnp.where(lines < TOK - 2, pltpu.roll(term_two, TOK - 2, 0), zero)
        )
        lines = row_index(16, TILE)
        zero = jnp.zeros((16, TILE), FLOAT)
        d_halo = follows * (
            jnp.where(lines < 2, term_two[0:16], zero)
            + jnp.where(lines == 1, pltpu.roll(term_one[0:16], 1, 0), zero)
        )
        half, place = lax.div(tile, 2), lax.rem(tile, 2) * TILE
        for which, (main, edge) in enumerate(
            (
                (d_mixed * v_all[0:TOK], d_halo * v_all[TOK:ALL]),
                (d_c, zero),
                (d_mixed * b_all[0:TOK], d_halo * b_all[TOK:ALL]),
            )
        ):
            cols = cut(which * HALF_D + place, TILE)
            grads[half, 0:TOK, cols] = main.astype(HALF)
            grads[half, TOK:ALL, cols] = edge.astype(HALF)


def projection_back(mix, grads, normed_grad):
    @pl.loop(0, D // TILE)
    def _(tile):
        total = dot_nt(grads[0], mat_rows(mix, tile, slice(0, OUT_AT)))
        total += dot_nt(grads[1], mat_rows(mix, tile, slice(MIX_HALF, MIX_HALF + OUT_AT)))
        normed_grad[:, cut(tile * TILE, TILE)] = total


def mixer_weight_grads(here, grads, branch, turned, grads_in, branch_in, total):
    def put(cols, value):
        total[:, :, :, :, :, cols] = value.astype(HALF).reshape(GRID + (16, TILE))

    @pl.loop(0, OUT_AT // TILE)
    def _(tile):
        cols = cut(tile * TILE, TILE)
        put(cols, dot(turned[0], grads[here.core, :, cols]) + dot(turned[1], grads_in[:, cols]))

    @pl.loop(0, HALF_D // TILE)
    def _(tile):
        cols = cut(tile * TILE, TILE)
        value = dot(turned[2, :, 0:TOK], branch[here.core, :, cols])
        value += dot(turned[3, :, 0:TOK], branch_in[:, cols])
        put(cut(OUT_AT + tile * TILE, TILE), value)


def twice(value):
    value = value.astype(FLOAT)
    return jnp.concatenate([value, value], axis=0).astype(HALF)


def lay_out(own, in_rows, out_rows, gate_rows, up_rows, down_rows, small_rows):
    for half in range(2):
        for which in range(3):
            start = which * D + half * HALF_D
            own[half, :, which * HALF_D : (which + 1) * HALF_D] = twice(
                in_rows[:, start : start + HALF_D]
            )
        own[half, :, OUT_AT:SMALL_AT] = twice(out_rows[:, half * HALF_D : (half + 1) * HALF_D])
        own[half, :, SMALL_AT:MIX_HALF] = twice(small_rows[...])
    early = FFN_HALF - SLAB
    rest = SLAB - early
    for place in range(4):
        at, start = MIX_HALF + place * FFN_HALF, place * SLAB
        own[0, :, at : at + SLAB] = twice(gate_rows[:, start : start + SLAB])
        own[0, :, at + SLAB : at + FFN_HALF] = twice(up_rows[:, start : start + early])
        own[1, :, at : at + rest] = twice(up_rows[:, start + early : start + SLAB])
        own[1, :, at + rest : at + rest + SLAB] = twice(down_rows[:, start : start + SLAB])
        own[1, :, at + rest + SLAB : at + FFN_HALF] = jnp.zeros((16, LANE), HALF)


def lay_flags(board, flags, tail, tokens, positions, counts):
    slots = lax.broadcasted_iota(jnp.int32, (1, LANE), 1)
    place, count = positions[...], jnp.broadcast_to(counts[...], (1, LANE))

    def bit(condition):
        return jnp.where(condition, jnp.ones((1, LANE), FLOAT), jnp.zeros((1, LANE), FLOAT))

    board[...] = jnp.zeros_like(board)
    board[0:1] = bit(place >= 1)
    board[1:2] = bit(place >= 2)
    board[2:3] = bit(slots < count)
    for row in (3, 16):
        board[row : row + 1] = bit(slots == count - 2)
        board[row + 1 : row + 2] = bit(slots == count - 1)
    flags[...] = jnp.transpose(board[...])
    tail[...] = dot(board[16:32].astype(HALF), tokens[...]).astype(HALF)


def lay_small(board, small_rows, vectors):
    board[...] = jnp.zeros_like(board)
    board[0:5, 0:8] = vectors[...].astype(FLOAT)
    small_rows[...] = jnp.transpose(board[...])[0:8].astype(HALF)


def block_kernel(
    in_rows, out_rows, gate_rows, up_rows, down_rows, vectors, tokens, positions, counts, cotangent,
    mixed_out, grad_tokens, grad_in, grad_out, grad_small, grad_gate, grad_up, grad_down,
    own, mix_owned, ffn_owned, board, small_rows, flags, tail,
    mate, full, halo, mix, ffn, twos, backs, proj, normed, gated, resid, rows, acts, turned_ffn,
    total, mix_mate, acts_in, ffn_rest, ffn_mate, work, ffn_work,
    branch, grads, d_normed, small, turned, normed_in, gated_in, branch_in, grads_in, small_in,
    edge_in, d_resid, *scratch,
):
    two_near, two_far = scratch[0:2], scratch[2:4]
    out_near, out_far = scratch[4:6], scratch[6:8]
    *landing, send, recv, local_sem = scratch[8:]
    mix_near, mix_far = landing_refs(MIX_REDUCE, landing[:MIX_LANDING])
    ffn_near, ffn_far = landing_refs(FFN_REDUCE, landing[MIX_LANDING:])
    here = Here()
    mail = Mail(send, recv)
    x, core = here.at["x"], here.core
    twin = here.twin()
    barrier, count = greet(
        near_list(here, ("x", "y", "z"))
        + [here.beside(axis, 2) for axis in ("x", "y", "z")]
        + [twin, here.along(1), here.along(-1)]
    )
    lay_flags(board, flags, tail, tokens, positions, counts)
    lay_small(board, small_rows, vectors)
    lay_out(own, in_rows, out_rows, gate_rows, up_rows, down_rows, small_rows)
    pl.semaphore_wait(barrier, count)
    rows_in = mail.post(own.at[1 - core], mate, twin)
    halo_in = mail.post(tail, halo, here.along(1))
    backs[x] = (flags[:, 2:3] * cotangent[...].astype(FLOAT)).astype(HALF)
    acts[:, 3 * SLAB : FFN_COLS] = jnp.zeros((4 * TOK, FFN_COLS - 3 * SLAB), HALF)
    rows_in.wait_recv()
    mine = lax.broadcasted_iota(jnp.int32, (16, OWN_COLS), 0) // 8 == core
    full[...] = jnp.where(mine, own[core].astype(FLOAT), mate[...].astype(FLOAT)).astype(HALF)

    mix_base, ffn_base = core * MIX_HALF, core * FFN_HALF
    ffn_own = blocks(ffn, here.at, cut(ffn_base, FFN_HALF))

    def slab(place):
        return full.at[:, cut(MIX_HALF + place * FFN_HALF, FFN_HALF)]

    rings = gather_rings(here, mail, mix, mix_base, MIX_PARTS, MIX_GATHER, 0, DirectGather)
    for ring, (first, chunks) in zip(rings, MIX_PARTS):
        ring.start(full.at[:, first * LANE : (first + chunks) * LANE])
    slabs = [
        mail.post(slab(here.ring("x", step)), ffn_own, here.beside("x", step)) for step in (1, 3, 2)
    ]
    keep_mix = pltpu.make_async_copy(
        full.at[:, 0:MIX_HALF], blocks(mix, here.at, cut(mix_base, MIX_HALF)), local_sem.at[0]
    )
    keep_slab = pltpu.make_async_copy(slab(x), ffn_own, local_sem.at[1])
    keep_mix.start()
    keep_slab.start()
    finish_all(rings)
    keep_mix.wait()
    mix_rings = gather_rings(here, mail, mix, mix_base, MIX_PARTS, MIX_GATHER, 1, DirectGather)
    start_all(mix_rings)
    keep_slab.wait()
    wait_all(slabs)
    ffn_rings = gather_rings(here, mail, ffn, ffn_base, FFN_PARTS, FFN_GATHER, 0)
    start_all(ffn_rings)
    finish_all(mix_rings)
    mix_rings = gather_rings(here, mail, mix, mix_base, MIX_PARTS, MIX_GATHER, 2)
    start_all(mix_rings)
    swaps = swap_pieces(here, mail, mix_rings, (0,))
    relay_all(ffn_rings)
    relay_all(mix_rings)
    swaps += swap_pieces(here, mail, mix_rings, (1, -1))
    stream = RingGather(here, mail, "x", row_pick(backs))
    stream.start()
    finish_all(ffn_rings)
    ffn_rings = gather_rings(here, mail, ffn, ffn_base, FFN_PARTS, FFN_GATHER, 1)
    finish_all(mix_rings)
    swaps += swap_pieces(here, mail, mix_rings, (2,))
    start_all(ffn_rings)
    stream.relay()
    ffn_swaps = swap_pieces(here, mail, ffn_rings, (0,))
    wait_all(swaps)
    halo_in.wait_recv()
    mixer_forward(here, tokens, halo, flags, mix, proj, normed, gated, resid, rows, twos.at[x])
    two_ring = RingGather(here, mail, "x", row_pick(twos))
    two_ring.start()
    relay_all(ffn_rings)
    ffn_swaps += swap_pieces(here, mail, ffn_rings, (1, -1))
    early = [mail.post(normed, normed_in, twin), mail.post(gated, gated_in, twin)]
    two_ring.relay()
    turn(turned.at[0, :, 0:ALL], normed[...])
    turn(turned.at[2, :, 0:TOK], gated[...])
    finish_all(ffn_rings)
    ffn_swaps += swap_pieces(here, mail, ffn_rings, (2,))
    stream.finish()
    for block in range(4):
        turn(turned_ffn.at[0, 1, :, block * TOK : (block + 1) * TOK], backs[block])
    shared = [mail.post(turned_ffn.at[0, 1], turned_ffn.at[1, 1], twin)]
    wait_all(ffn_swaps)
    two_ring.finish()
    gathered = len(mail.posted)

    @pl.loop(0, SLAB // TILE)
    def _(tile):
        ffn_hidden(ffn, twos, backs, acts, tile * TILE, TILE)

    ffn_hidden(ffn, twos, backs, acts, SLAB // TILE * TILE, SLAB % TILE)
    shared.append(
        mail.post(acts.at[:, cut((1 - core) * FFN_HALF, FFN_HALF)], acts_in, twin)
    )
    ffn_tokens(ffn, acts, work, (0, 1))
    two_ring = RingReduce(here, mail, "x", row_pick(work), two_near, two_far)
    two_ring.start()
    for block in range(4):
        turn(turned_ffn.at[0, 0, :, block * TOK : (block + 1) * TOK], twos[block])
    shared.append(mail.post(turned_ffn.at[0, 0], turned_ffn.at[1, 0], twin))
    ffn_tokens(ffn, acts, ffn_work, (2,))
    two_ring.relay()
    mail.settle(gathered)
    wait_all(shared)
    ffn_rings = reduce_rings(here, mail, ffn, ffn_base, FFN_PARTS, FFN_REDUCE, ffn_near, ffn_far, 0)
    for part, ring in zip(FFN_PARTS, ffn_rings):
        ffn_weight_grads(ffn, acts, acts_in, turned_ffn, core, part)
        ring.start()
    two_ring.finish()
    value = resid[...]
    scale = norm_scale(value)
    unit = value * scale
    d_two = work[x].astype(FLOAT)
    small[...] = jnp.zeros_like(small)
    small[1:2] = jnp.sum(d_two * unit, axis=0, keepdims=True)
    d_value = flags[:, 2:3] * cotangent[...].astype(FLOAT) + norm_back(unit, scale, rows[1:2], d_two)
    d_resid[...] = d_value
    branch[0] = d_value[:, 0:HALF_D].astype(HALF)
    branch[1] = d_value[:, HALF_D:D].astype(HALF)
    late = [mail.post(branch.at[1 - core], branch_in, twin)]
    out_ring = RingReduce(here, mail, "x", row_pick(ffn_work), out_near, out_far)
    out_ring.start()
    mixer_backward(here, flags, mix, proj, rows, branch, grads, small)
    late.append(mail.post(grads.at[1 - core], grads_in, twin))
    relay_all(ffn_rings)
    out_ring.relay()
    projection_back(mix, grads, d_normed)
    x_own, x_edge = tokens[...].astype(FLOAT), halo[...].astype(FLOAT)
    scale = norm_scale(x_own)
    unit = x_own * scale
    small[0:1] = jnp.sum(d_normed[0:TOK] * unit, axis=0, keepdims=True) + jnp.sum(
        d_normed[TOK:ALL] * x_edge * norm_scale(x_edge), axis=0, keepdims=True
    )
    late.append(mail.post(small, small_in, twin))
    edge = mail.post(d_normed.at[pl.ds(TOK, 8)], edge_in, here.along(-1))
    wait_all(early)
    turn(turned.at[1, :, 0:ALL], normed_in[...])
    turn(turned.at[3, :, 0:TOK], gated_in[...])
    wait_all(late)
    mixer_weight_grads(here, grads, branch, turned, grads_in, branch_in, total)
    small_sum = small[...] + small_in[...]
    total[:, :, :, :, :, SMALL_AT:MIX_HALF] = (
        jnp.transpose(small_sum).astype(HALF).reshape(GRID + (16, LANE))
    )
    mix_rings = reduce_rings(here, mail, total, 0, MIX_PARTS, MIX_REDUCE, mix_near, mix_far, 0)
    start_all(mix_rings)
    finish_all(ffn_rings)
    ffn_rings = reduce_rings(here, mail, ffn, ffn_base, FFN_PARTS, FFN_REDUCE, ffn_near, ffn_far, 1)
    start_all(ffn_rings)
    relay_all(mix_rings)
    relay_all(ffn_rings)
    edge.wait_recv()
    d_first = (
        d_normed[0:TOK] + flags[:, 3:4] * edge_in[0:1] + flags[:, 4:5] * edge_in[1:2]
    )
    grad_tokens[...] = (d_resid[...] + norm_back(unit, scale, rows[0:1], d_first)).astype(HALF)
    finish_all(mix_rings)
    mix_rings = reduce_rings(here, mail, total, 0, MIX_PARTS, MIX_REDUCE, mix_near, mix_far, 1)
    start_all(mix_rings)
    finish_all(ffn_rings)
    copies = []
    for step in (1, 3, 2):
        there = here.ring("x", step)
        copies.append(
            mail.post(
                blocks(ffn, {**here.at, "x": there}, cut(ffn_base, FFN_HALF)),
                ffn_rest.at[x],
                here.beside("x", step),
            )
        )
    ffn_rest[x] = ffn_own[...]
    relay_all(mix_rings)
    out_ring.finish()
    mixed_out[...] = (flags[:, 2:3] * (resid[...] + ffn_work[x].astype(FLOAT))).astype(HALF)
    finish_all(mix_rings)
    mix_rings = reduce_rings(here, mail, total, 0, MIX_PARTS, MIX_REDUCE, mix_near, mix_far, 2)
    start_all(mix_rings)
    wait_all(copies)
    ffn_swap = mail.post(ffn_rest, ffn_mate, twin)
    ffn_owned[:, :, cut(core * FFN_HALF, FFN_HALF)] = ffn_rest[...].astype(FLOAT)
    relay_all(mix_rings)
    ffn_swap.wait_recv()
    ffn_owned[:, :, cut((1 - core) * FFN_HALF, FFN_HALF)] = ffn_mate[...].astype(FLOAT)
    lines = pl.ds(pl.multiple_of(8 * core, 8), 8)
    for place in range(4):
        cols = slice(place * SLAB, (place + 1) * SLAB)
        for kind, target in enumerate((grad_gate, grad_up, grad_down)):
            target[:, cols] = ffn_owned[place, lines, kind * SLAB : (kind + 1) * SLAB]
    finish_all(mix_rings)
    own_sum = blocks(total, here.at, slice(None))
    mix_swap = mail.post(own_sum, mix_mate, twin)
    mix_owned[:, cut(core * MIX_HALF, MIX_HALF)] = own_sum[...].astype(FLOAT)
    mix_swap.wait_recv()
    mix_owned[:, cut((1 - core) * MIX_HALF, MIX_HALF)] = mix_mate[...].astype(FLOAT)
    for half in range(2):
        at = half * MIX_HALF
        for which in range(3):
            start = which * D + half * HALF_D
            grad_in[:, start : start + HALF_D] = mix_owned[
                lines, at + which * HALF_D : at + (which + 1) * HALF_D
            ]
        grad_out[:, half * HALF_D : (half + 1) * HALF_D] = mix_owned[lines, at + OUT_AT : at + SMALL_AT]
    grad_small[...] = mix_owned[lines, SMALL_AT:MIX_HALF]
    mail.settle(len(mail.posted))


def write_kernel(*refs):
    count = (len(refs) - 2) // 2
    ins, outs = refs[:count], refs[count:]
    for source, target in zip(ins[:-1], outs):
        target[...] = source[...]
    small = jnp.transpose(ins[-1][...])
    outs[-3][...] = small[0:1, 0:8]
    outs[-2][...] = small[1:2, 0:8]
    outs[-1][...] = small[2:5, 0:8]


def vmem():
    return pl.BlockSpec(memory_space=pltpu.VMEM)


def sems(count):
    return pltpu.SemaphoreType.DMA((count,))


def params(number):
    return pltpu.CompilerParams(
        collective_id=number, has_side_effects=True, vmem_limit_bytes=VMEM_LIMIT
    )


def shape(dims, dtype):
    return jax.ShapeDtypeStruct(dims, dtype)


def whole_block(*operands):
    landing = [
        pltpu.VMEM(dims, HALF)
        for part in landing_shapes(MIX_PARTS, MIX_REDUCE) + landing_shapes(FFN_PARTS, FFN_REDUCE)
        for dims in part
    ]
    stream_landing = [pltpu.VMEM((TOK, D), HALF)] * 2 + [pltpu.VMEM((TOK // 2, D), HALF)] * 2
    return pl.pallas_call(
        block_kernel,
        out_shape=(
            shape((TOK, D), HALF),
            shape((TOK, D), HALF),
            shape((8, 3 * D), FLOAT),
            shape((8, D), FLOAT),
            shape((8, LANE), FLOAT),
            shape((8, 4 * SLAB), FLOAT),
            shape((8, 4 * SLAB), FLOAT),
            shape((8, 4 * SLAB), FLOAT),
        ),
        in_specs=[vmem()] * 10,
        out_specs=(vmem(),) * 8,
        scratch_shapes=[
            pltpu.VMEM((2, 16, OWN_COLS), HALF),
            pltpu.VMEM((16, MIX_COLS), FLOAT),
            pltpu.VMEM((4, 16, FFN_COLS), FLOAT),
            pltpu.VMEM((LANE, LANE), FLOAT),
            pltpu.VMEM((8, LANE), HALF),
            pltpu.VMEM((TOK, LANE), FLOAT),
            pltpu.VMEM((16, D), HALF),
            pltpu.VMEM((16, OWN_COLS), HALF),
            pltpu.VMEM((16, OWN_COLS), HALF),
            pltpu.VMEM((16, D), HALF),
            pltpu.VMEM(GRID + (16, MIX_COLS), HALF),
            pltpu.VMEM(GRID + (16, FFN_COLS), HALF),
            pltpu.VMEM((4, TOK, D), HALF),
            pltpu.VMEM((4, TOK, D), HALF),
            pltpu.VMEM((3, ALL, D), FLOAT),
            pltpu.VMEM((ALL, D), HALF),
            pltpu.VMEM((TOK, D), HALF),
            pltpu.VMEM((TOK, D), FLOAT),
            pltpu.VMEM((8, D), FLOAT),
            pltpu.VMEM((4 * TOK, FFN_COLS), HALF),
            pltpu.VMEM((2, 2, D, 4 * TOK), HALF),
            pltpu.VMEM(GRID + (16, MIX_HALF), HALF),
            pltpu.VMEM((16, MIX_HALF), HALF),
            pltpu.VMEM((4 * TOK, FFN_HALF), HALF),
            pltpu.VMEM((4, 16, FFN_HALF), HALF),
            pltpu.VMEM((4, 16, FFN_HALF), HALF),
            pltpu.VMEM((4, TOK, D), HALF),
            pltpu.VMEM((4, TOK, D), HALF),
            pltpu.VMEM((2, TOK, HALF_D), HALF),
            pltpu.VMEM((2, ALL, OUT_AT), HALF),
            pltpu.VMEM((ALL, D), FLOAT),
            pltpu.VMEM((LANE, D), FLOAT),
            pltpu.VMEM((4, D, ALL), HALF),
            pltpu.VMEM((ALL, D), HALF),
            pltpu.VMEM((TOK, D), HALF),
            pltpu.VMEM((TOK, HALF_D), HALF),
            pltpu.VMEM((ALL, OUT_AT), HALF),
            pltpu.VMEM((LANE, D), FLOAT),
            pltpu.VMEM((8, D), FLOAT),
            pltpu.VMEM((TOK, D), FLOAT),
        ]
        + stream_landing * 2
        + landing
        + [sems(176), sems(176), sems(2)],
        compiler_params=params(0),
        name="whole_block",
    )(*operands)


def local(
    tokens,
    gain_mix,
    in_weight,
    conv_weight,
    out_weight,
    gain_ffn,
    gate_weight,
    up_weight,
    down_weight,
    live_counts,
    positions,
    cotangent,
):
    vectors = jnp.concatenate([gain_mix[None], gain_ffn[None], conv_weight], axis=0)
    mixed_out, grad_tokens, grad_in, grad_out, grad_small, grad_gate, grad_up, grad_down = whole_block(
        in_weight, out_weight, gate_weight, up_weight, jnp.transpose(down_weight), vectors,
        tokens, positions.reshape(1, TOK), live_counts, cotangent,
    )
    plain = (mixed_out, grad_tokens, grad_in, grad_out, grad_gate, grad_up, grad_down)
    mixed_out, grad_tokens, grad_in, grad_out, grad_gate, grad_up, grad_down, one, two, taps = (
        pl.pallas_call(
            write_kernel,
            out_shape=tuple(shape(value.shape, value.dtype) for value in plain)
            + (
                shape((1, 8), FLOAT),
                shape((1, 8), FLOAT),
                shape((3, 8), FLOAT),
            ),
            in_specs=[vmem()] * 8,
            out_specs=(vmem(),) * 10,
            name="write",
            compiler_params=pltpu.CompilerParams(vmem_limit_bytes=VMEM_LIMIT),
        )(*plain, grad_small)
    )
    return (
        mixed_out,
        grad_tokens,
        one.reshape(8),
        grad_in,
        taps,
        grad_out,
        two.reshape(8),
        grad_gate,
        grad_up,
        jnp.transpose(grad_down),
    )


def solution(mesh):
    rows = P(("fsdp", "seq"), None)
    flat = P(("fsdp", "seq"))
    cols = P(None, ("fsdp", "seq"))
    return jax.shard_map(
        local,
        mesh=mesh,
        in_specs=(rows, flat, rows, cols, rows, flat, rows, rows, cols, P("fsdp", "seq"), flat, rows),
        out_specs=(rows, rows, flat, rows, cols, rows, flat, rows, rows, cols),
        check_vma=False,
    )
```

```python
import jax
import jax.numpy as jnp
from jax import lax
from jax.experimental import pallas as pl
from jax.experimental.pallas import tpu as pltpu
from jax.sharding import PartitionSpec as P

EPS = 1e-05
FLOAT = jnp.float32
HALF = jnp.bfloat16
MESH = pl.DeviceIdType.MESH
LANE = 128
D = 1024
SLAB = 1152
MIX_COLS = 34 * LANE
FFN_COLS = 28 * LANE
MIX_HALF = MIX_COLS // 2
FFN_HALF = FFN_COLS // 2
OWN_COLS = MIX_HALF + 4 * FFN_HALF
HALF_D = D // 2
OUT_AT = 3 * HALF_D
SMALL_AT = 4 * HALF_D
TILE = 256
TOK = 128
ALL = TOK + 16
MIX_PARTS = ((0, 6), (6, 6), (12, 5))
MIX_GATHER = (("y", "z", "x"), ("z", "x", "y"), ("x", "y", "z"))
MIX_REDUCE = (("x", "z", "y"), ("y", "x", "z"), ("z", "y", "x"))
FFN_PARTS = ((0, 8), (8, 6))
FFN_GATHER = (("y", "z"), ("z", "y"))
FFN_REDUCE = (("y", "z"), ("z", "y"))
GRID = (2, 4, 4, 2)
MIX_LANDING = 4 * 3 * len(MIX_PARTS)
VMEM_LIMIT = 60 * 2**20


class Here:
    def __init__(self):
        fsdp = lax.axis_index("fsdp")
        seq = lax.axis_index("seq")
        self.fsdp, self.seq = fsdp, seq
        self.at = {
            "x": lax.div(seq, 4),
            "y": lax.rem(fsdp, 4),
            "z": lax.div(fsdp, 4) * 2 + lax.rem(lax.div(seq, 2), 2),
        }
        self.core = lax.rem(seq, 2)

    def device(self, core, **moved):
        at = {**self.at, **moved}
        return (
            lax.div(at["z"], 2) * 4 + at["y"],
            (at["x"] * 2 + lax.rem(at["z"], 2)) * 2 + core,
        )

    def ring(self, axis, step):
        return lax.rem(self.at[axis] + (step + 4) % 4, 4)

    def beside(self, axis, step):
        return self.device(self.core, **{axis: self.ring(axis, step)})

    def twin(self):
        return self.device(1 - self.core)

    def along(self, step):
        return (self.fsdp, lax.rem(self.seq + (step + 16) % 16, 16))


def greet(devices):
    barrier = pltpu.get_barrier_semaphore()
    for device in devices:
        pl.semaphore_signal(barrier, inc=1, device_id=device, device_id_type=MESH)
    return barrier, len(devices)


class Mail:
    def __init__(self, send, recv):
        self.send, self.recv, self.posted, self.settled = send, recv, [], 0

    def post(self, src, dst, device):
        place = len(self.posted)
        copy = pltpu.make_async_remote_copy(
            src_ref=src,
            dst_ref=dst,
            send_sem=self.send.at[place],
            recv_sem=self.recv.at[place],
            device_id=device,
            device_id_type=MESH,
        )
        copy.start()
        self.posted.append(copy)
        return copy

    def settle(self, count):
        for copy in self.posted[self.settled : count]:
            copy.wait_send()
        self.settled = count


def cut(start, count):
    return pl.ds(pl.multiple_of(start, LANE), count)


def blocks(ref, at, cols):
    whole = slice(None)
    z = at["z"]
    high, low = (whole, whole) if z is None else (lax.div(z, 2), lax.rem(z, 2))
    y = whole if at["y"] is None else at["y"]
    x = whole if at["x"] is None else at["x"]
    return ref.at[high, y, x, low, :, cols]


class RingGather:
    def __init__(self, here, mail, axis, pick):
        self.here, self.mail, self.axis, self.pick = here, mail, axis, pick

    def start(self, source=None):
        here, axis = self.here, self.axis
        own = self.pick(here.at[axis], None)
        source = own if source is None else source
        self.to_up = self.mail.post(source, own, here.beside(axis, 1))
        self.to_down = self.mail.post(source, own, here.beside(axis, -1))

    def relay(self):
        here, axis = self.here, self.axis
        self.to_up.wait_recv()
        first = self.pick(here.ring(axis, -1), 0)
        self.far_up = self.mail.post(first, first, here.beside(axis, 1))
        self.to_down.wait_recv()
        second = self.pick(here.ring(axis, 1), 1)
        self.far_down = self.mail.post(second, second, here.beside(axis, -1))

    def finish(self):
        self.far_up.wait_recv()
        self.far_down.wait_recv()


class RingReduce:
    def __init__(self, here, mail, axis, pick, near, far):
        self.here, self.mail, self.axis, self.pick = here, mail, axis, pick
        self.near, self.far = near, far

    def start(self):
        here, axis = self.here, self.axis
        away = here.ring(axis, 2)
        self.far_up = self.mail.post(self.pick(away, 0), self.far[0], here.beside(axis, 1))
        self.far_down = self.mail.post(self.pick(away, 1), self.far[1], here.beside(axis, -1))

    def relay(self):
        here, axis = self.here, self.axis
        above, below = here.ring(axis, 1), here.ring(axis, -1)
        self.far_up.wait_recv()
        add_into(self.pick(above, 0), self.far[0])
        self.to_up = self.mail.post(self.pick(above, None), self.near[0], here.beside(axis, 1))
        self.far_down.wait_recv()
        add_into(self.pick(below, 1), self.far[1])
        self.to_down = self.mail.post(self.pick(below, None), self.near[1], here.beside(axis, -1))

    def finish(self):
        self.to_up.wait_recv()
        self.to_down.wait_recv()
        own = self.pick(self.here.at[self.axis], None)
        add_into(own, self.near[0], self.near[1])


class DirectGather(RingGather):
    def start(self, source=None):
        here, axis = self.here, self.axis
        own = self.pick(here.at[axis], None)
        source = own if source is None else source
        self.copies = [
            self.mail.post(source, own, here.beside(axis, step)) for step in (1, -1, 2)
        ]

    def relay(self):
        pass

    def finish(self):
        wait_all(self.copies)


class DirectReduce(RingReduce):
    def start(self):
        here, axis = self.here, self.axis
        self.landed = [self.near[0], self.near[1], self.far[0]]
        self.copies = [
            self.mail.post(
                self.pick(here.ring(axis, step), None), landed, here.beside(axis, step)
            )
            for step, landed in zip((1, -1, 2), self.landed)
        ]

    def relay(self):
        pass

    def finish(self):
        wait_all(self.copies)
        add_into(self.pick(self.here.at[self.axis], None), *self.landed)


def add_into(target, *terms):
    if len(terms) == 1:
        target[...] = target[...] + terms[0][...]
        return
    total = target[...].astype(FLOAT)
    for term in terms:
        total = total + term[...].astype(FLOAT)
    target[...] = total.astype(target.dtype)


def column_pick(ref, fixed, axis, start, chunks):
    split = (chunks + 1) // 2

    def pick(place, half):
        first, count = {None: (0, chunks), 0: (0, split), 1: (split, chunks - split)}[half]
        return blocks(ref, {**fixed, axis: place}, cut(start + first * LANE, count * LANE))

    return pick


def row_pick(ref):
    def pick(place, half):
        rows = ref.shape[-2]
        part = {None: slice(None), 0: pl.ds(0, rows // 2), 1: pl.ds(rows // 2, rows // 2)}[half]
        return ref.at[place, part]

    return pick


def gather_rings(here, mail, ref, base, parts, orders, stage, kind=RingGather):
    rings = []
    for (first, chunks), order in zip(parts, orders):
        fixed = dict(here.at)
        for axis in ("x", "y", "z"):
            if axis not in order or axis in order[:stage]:
                fixed[axis] = None
        pick = column_pick(ref, fixed, order[stage], base + first * LANE, chunks)
        rings.append(kind(here, mail, order[stage], pick))
    return rings


def start_all(rings):
    for ring in rings:
        ring.start()


def relay_all(rings):
    for ring in rings:
        ring.relay()


def finish_all(rings):
    for ring in rings:
        ring.finish()


def chain(rings, later):
    for ring, following in zip(rings, later):
        ring.finish()
        following.start()
    return later


def swap_pieces(here, mail, rings, steps):
    copies = []
    for ring in rings:
        for step in steps:
            piece = ring.pick(here.ring(ring.axis, step), None)
            copies.append(mail.post(piece, piece, here.twin()))
    return copies


def wait_all(copies):
    for copy in copies:
        copy.wait_recv()


def near_list(here, axes):
    return [here.beside(axis, step) for axis in axes for step in (1, -1)]


def mat(ref, cols):
    block = ref[:, :, :, :, :, cols]
    return block.reshape(D, block.shape[-1])


def mat_rows(ref, tile, cols):
    block = ref[lax.div(tile, 2), pl.ds(lax.rem(tile, 2) * 2, 2), :, :, :, cols]
    return block.reshape(TILE, block.shape[-1])


def mix_cols(tile, which):
    return cut(lax.div(tile, 2) * MIX_HALF + which * HALF_D + lax.rem(tile, 2) * TILE, TILE)


def dot(left, right):
    return jnp.dot(left, right, preferred_element_type=FLOAT)


def dot_nt(left, right):
    return lax.dot_general(
        left, right, (((1,), (1,)), ((), ())), preferred_element_type=FLOAT
    )


def norm_scale(values):
    return lax.rsqrt(jnp.mean(values * values, axis=-1, keepdims=True) + EPS)


def norm_back(normal, row_scale, gain_row, upstream):
    weighted = upstream * gain_row
    return row_scale * (
        weighted - normal * jnp.mean(weighted * normal, axis=-1, keepdims=True)
    )


def row_index(rows, cols):
    return lax.broadcasted_iota(jnp.int32, (rows, cols), 0)


def conv_terms(mixed, halo):
    rows = row_index(TOK, mixed.shape[1])
    one = pltpu.roll(mixed, 1, 0)
    two = pltpu.roll(mixed, 2, 0)
    one = jnp.where(rows == 0, halo[1:2], one)
    two = jnp.where(rows == 0, halo[0:1], jnp.where(rows == 1, halo[1:2], two))
    return one, two


def follows_of(here):
    return jnp.minimum(here.seq, 1).astype(FLOAT)


def mixer_forward(here, tokens, halo, flags, mix, proj, normed, gated, resid, rows, two):
    small = jnp.transpose(mat(mix, slice(SMALL_AT, SMALL_AT + LANE)).astype(FLOAT))
    rows[...] = small[0:8]
    gain = rows[0:1]
    x = tokens[...].astype(FLOAT)
    normed[0:TOK] = (x * norm_scale(x) * gain).astype(HALF)
    before = halo[...].astype(FLOAT)
    normed[TOK:ALL] = (before * norm_scale(before) * gain).astype(HALF)
    follows = follows_of(here)
    first_ok, second_ok = flags[:, 0:1], flags[:, 1:2]

    @pl.loop(0, D // TILE)
    def _(tile):
        feats = cut(tile * TILE, TILE)
        parts = [dot(normed[...], mat(mix, mix_cols(tile, which))) for which in range(3)]
        for which in range(3):
            proj[which, :, feats] = parts[which]
        mixed = parts[0] * parts[2]
        own = mixed[0:TOK]
        one, second = conv_terms(own, mixed[TOK:ALL] * follows)
        conv = (
            rows[2:3, feats] * own
            + first_ok * rows[3:4, feats] * one
            + second_ok * rows[4:5, feats] * second
        )
        gated[:, feats] = (parts[1][0:TOK] * conv).astype(HALF)

    @pl.loop(0, D // TILE)
    def _(tile):
        feats = cut(tile * TILE, TILE)
        branch = dot(gated[...], mat(mix, mix_cols(tile, 3)))
        resid[:, feats] = tokens[:, feats].astype(FLOAT) + branch

    value = resid[...]
    two[...] = (value * norm_scale(value) * rows[1:2]).astype(HALF)


def reduce_rings(here, mail, ref, base, parts, orders, near, far, stage):
    rings = []
    for number, ((first, chunks), order) in enumerate(zip(parts, orders)):
        fixed = {"x": None, "y": None, "z": None}
        for axis in order[:stage]:
            fixed[axis] = here.at[axis]
        pick = column_pick(ref, fixed, order[stage], base + first * LANE, chunks)
        kind = RingReduce if stage == 0 else DirectReduce
        rings.append(kind(here, mail, order[stage], pick, near[number][stage], far[number][stage]))
    return rings


def landing_shapes(parts, orders):
    shapes = []
    for (_, chunks), order in zip(parts, orders):
        split = (chunks + 1) // 2
        done = []
        for stage in range(len(order)):
            gone = order[: stage + 1]
            lead = ()
            if "z" not in gone:
                lead += (2,)
            if "y" not in gone:
                lead += (4,)
            if "x" not in gone:
                lead += (4,)
            if "z" not in gone:
                lead += (2,)
            done += [lead + (16, chunks * LANE)] * 2
            if stage == 0:
                done += [lead + (16, split * LANE), lead + (16, (chunks - split) * LANE)]
            else:
                done += [lead + (16, chunks * LANE), (16, LANE)]
        shapes.append(done)
    return shapes


def landing_refs(orders, refs):
    near, far = [], []
    place = 0
    for order in orders:
        near.append([])
        far.append([])
        for _ in order:
            near[-1].append(refs[place : place + 2])
            far[-1].append(refs[place + 2 : place + 4])
            place += 4
    return near, far


def ffn_hidden(ffn, twos, backs, acts, start, width):
    value = twos[...].reshape(4 * TOK, D)
    gate = dot(value, mat(ffn, cut(start, width)))
    upper = dot(value, mat(ffn, cut(SLAB + start, width)))
    d_active = dot(backs[...].reshape(4 * TOK, D), mat(ffn, cut(2 * SLAB + start, width)))
    sig = jax.nn.sigmoid(gate)
    swish = gate * sig
    acts[:, cut(start, width)] = (d_active * upper * (sig * (1.0 + gate * (1.0 - sig)))).astype(HALF)
    acts[:, cut(SLAB + start, width)] = (d_active * swish).astype(HALF)
    acts[:, cut(2 * SLAB + start, width)] = (swish * upper).astype(HALF)


def ffn_tokens(ffn, acts, target, kinds):
    @pl.loop(0, D // TILE)
    def _(tile):
        total = 0.0
        for kind in kinds:
            cols = slice(kind * SLAB, (kind + 1) * SLAB)
            total += dot_nt(acts[:, cols], mat_rows(ffn, tile, cols))
        target[:, :, cut(tile * TILE, TILE)] = total.astype(HALF).reshape(4, TOK, TILE)


def ffn_weight_grads(ffn, acts, acts_in, turned, half, part):
    first, chunks = part

    @pl.loop(first * LANE // TILE, (first + chunks) * LANE // TILE)
    def _(tile):
        cols = cut(half * FFN_HALF + tile * TILE, TILE)
        side = half * jnp.minimum(lax.div(tile, 2), 1)
        value = dot(turned[0, side], acts[:, cols])
        value += dot(turned[1, side], acts_in[:, cut(tile * TILE, TILE)])
        ffn[:, :, :, :, :, cols] = value.astype(HALF).reshape(GRID + (16, TILE))


def turn(target, value):
    target[...] = jnp.transpose(value.astype(FLOAT)).astype(HALF)


def mixer_backward(here, flags, mix, proj, rows, branch, grads, small):
    follows = follows_of(here)
    first_ok, second_ok = flags[:, 0:1], flags[:, 1:2]

    @pl.loop(0, D // TILE)
    def _(tile):
        feats = cut(tile * TILE, TILE)
        gated = dot_nt(branch[0], mat_rows(mix, tile, slice(OUT_AT, OUT_AT + HALF_D)))
        gated += dot_nt(
            branch[1], mat_rows(mix, tile, slice(MIX_HALF + OUT_AT, MIX_HALF + OUT_AT + HALF_D))
        )
        b_all, c_all, v_all = (proj[which, :, feats] for which in range(3))
        mixed = b_all * v_all
        own = mixed[0:TOK]
        one, second = conv_terms(own, mixed[TOK:ALL] * follows)
        tap_one, tap_two = rows[3:4, feats], rows[4:5, feats]
        conv = rows[2:3, feats] * own + first_ok * tap_one * one + second_ok * tap_two * second
        d_c = gated * conv
        d_conv = gated * c_all[0:TOK]
        small[2:3, feats] = jnp.sum(d_conv * own, axis=0, keepdims=True)
        small[3:4, feats] = jnp.sum(d_conv * first_ok * one, axis=0, keepdims=True)
        small[4:5, feats] = jnp.sum(d_conv * second_ok * second, axis=0, keepdims=True)
        term_one = first_ok * tap_one * d_conv
        term_two = second_ok * tap_two * d_conv
        lines = row_index(TOK, TILE)
        zero = jnp.zeros((TOK, TILE), FLOAT)
        d_mixed = (
            rows[2:3, feats] * d_conv
            + jnp.where(lines < TOK - 1, pltpu.roll(term_one, TOK - 1, 0), zero)
            + jnp.where(lines < TOK - 2, pltpu.roll(term_two, TOK - 2, 0), zero)
        )
        lines = row_index(16, TILE)
        zero = jnp.zeros((16, TILE), FLOAT)
        d_halo = follows * (
            jnp.where(lines < 2, term_two[0:16], zero)
            + jnp.where(lines == 1, pltpu.roll(term_one[0:16], 1, 0), zero)
        )
        half, place = lax.div(tile, 2), lax.rem(tile, 2) * TILE
        for which, (main, edge) in enumerate(
            (
                (d_mixed * v_all[0:TOK], d_halo * v_all[TOK:ALL]),
                (d_c, zero),
                (d_mixed * b_all[0:TOK], d_halo * b_all[TOK:ALL]),
            )
        ):
            cols = cut(which * HALF_D + place, TILE)
            grads[half, 0:TOK, cols] = main.astype(HALF)
            grads[half, TOK:ALL, cols] = edge.astype(HALF)


def projection_back(mix, grads, normed_grad):
    @pl.loop(0, D // TILE)
    def _(tile):
        total = dot_nt(grads[0], mat_rows(mix, tile, slice(0, OUT_AT)))
        total += dot_nt(grads[1], mat_rows(mix, tile, slice(MIX_HALF, MIX_HALF + OUT_AT)))
        normed_grad[:, cut(tile * TILE, TILE)] = total


def mixer_weight_grads(here, grads, branch, turned, grads_in, branch_in, total, rings):
    def put(cols, value):
        total[:, :, :, :, :, cols] = value.astype(HALF).reshape(GRID + (16, TILE))

    for ring, (first, chunks) in zip(rings[:2], MIX_PARTS):

        @pl.loop(first * LANE // TILE, (first + chunks) * LANE // TILE)
        def _(tile):
            cols = cut(tile * TILE, TILE)
            put(cols, dot(turned[0], grads[here.core, :, cols]) + dot(turned[1], grads_in[:, cols]))

        ring.start()

    @pl.loop(0, HALF_D // TILE)
    def _(tile):
        cols = cut(tile * TILE, TILE)
        value = dot(turned[2, :, 0:TOK], branch[here.core, :, cols])
        value += dot(turned[3, :, 0:TOK], branch_in[:, cols])
        put(cut(OUT_AT + tile * TILE, TILE), value)


def twice(value):
    value = value.astype(FLOAT)
    return jnp.concatenate([value, value], axis=0).astype(HALF)


def lay_out(own, in_rows, out_rows, gate_rows, up_rows, down_rows, small_rows):
    for half in range(2):
        for which in range(3):
            start = which * D + half * HALF_D
            own[half, :, which * HALF_D : (which + 1) * HALF_D] = twice(
                in_rows[:, start : start + HALF_D]
            )
        own[half, :, OUT_AT:SMALL_AT] = twice(out_rows[:, half * HALF_D : (half + 1) * HALF_D])
        own[half, :, SMALL_AT:MIX_HALF] = twice(small_rows[...])
    early = FFN_HALF - SLAB
    rest = SLAB - early
    for place in range(4):
        at, start = MIX_HALF + place * FFN_HALF, place * SLAB
        own[0, :, at : at + SLAB] = twice(gate_rows[:, start : start + SLAB])
        own[0, :, at + SLAB : at + FFN_HALF] = twice(up_rows[:, start : start + early])
        own[1, :, at : at + rest] = twice(up_rows[:, start + early : start + SLAB])
        own[1, :, at + rest : at + rest + SLAB] = twice(down_rows[:, start : start + SLAB])
        own[1, :, at + rest + SLAB : at + FFN_HALF] = jnp.zeros((16, LANE), HALF)


def lay_flags(board, flags, tail, tokens, positions, counts):
    slots = lax.broadcasted_iota(jnp.int32, (1, LANE), 1)
    place, count = positions[...], jnp.broadcast_to(counts[...], (1, LANE))

    def bit(condition):
        return jnp.where(condition, jnp.ones((1, LANE), FLOAT), jnp.zeros((1, LANE), FLOAT))

    board[...] = jnp.zeros_like(board)
    board[0:1] = bit(place >= 1)
    board[1:2] = bit(place >= 2)
    board[2:3] = bit(slots < count)
    for row in (3, 16):
        board[row : row + 1] = bit(slots == count - 2)
        board[row + 1 : row + 2] = bit(slots == count - 1)
    flags[...] = jnp.transpose(board[...])
    tail[...] = dot(board[16:32].astype(HALF), tokens[...]).astype(HALF)


def lay_small(board, small_rows, vectors):
    board[...] = jnp.zeros_like(board)
    board[0:5, 0:8] = vectors[...].astype(FLOAT)
    small_rows[...] = jnp.transpose(board[...])[0:8].astype(HALF)


def block_kernel(
    in_rows, out_rows, gate_rows, up_rows, down_rows, vectors, tokens, positions, counts, cotangent,
    mixed_out, grad_tokens, grad_in, grad_out, grad_small, grad_gate, grad_up, grad_down,
    own, mix_owned, ffn_owned, board, small_rows, flags, tail,
    mate, full, halo, mix, ffn, twos, backs, proj, normed, gated, resid, rows, acts, turned_ffn,
    total, mix_mate, acts_in, ffn_rest, ffn_mate, work, ffn_work,
    branch, grads, d_normed, small, turned, normed_in, gated_in, branch_in, grads_in, small_in,
    edge_in, d_resid, *scratch,
):
    two_near, two_far = scratch[0:2], scratch[2:4]
    out_near, out_far = scratch[4:6], scratch[6:8]
    *landing, send, recv, local_sem = scratch[8:]
    mix_near, mix_far = landing_refs(MIX_REDUCE, landing[:MIX_LANDING])
    ffn_near, ffn_far = landing_refs(FFN_REDUCE, landing[MIX_LANDING:])
    here = Here()
    mail = Mail(send, recv)
    x, core = here.at["x"], here.core
    twin = here.twin()
    barrier, count = greet(
        near_list(here, ("x", "y", "z"))
        + [here.beside(axis, 2) for axis in ("x", "y", "z")]
        + [twin, here.along(1), here.along(-1)]
    )
    lay_flags(board, flags, tail, tokens, positions, counts)
    lay_small(board, small_rows, vectors)
    lay_out(own, in_rows, out_rows, gate_rows, up_rows, down_rows, small_rows)
    pl.semaphore_wait(barrier, count)
    rows_in = mail.post(own.at[1 - core], mate, twin)
    halo_in = mail.post(tail, halo, here.along(1))
    backs[x] = (flags[:, 2:3] * cotangent[...].astype(FLOAT)).astype(HALF)
    acts[:, 3 * SLAB : FFN_COLS] = jnp.zeros((4 * TOK, FFN_COLS - 3 * SLAB), HALF)
    rows_in.wait_recv()
    mine = lax.broadcasted_iota(jnp.int32, (16, OWN_COLS), 0) // 8 == core
    full[...] = jnp.where(mine, own[core].astype(FLOAT), mate[...].astype(FLOAT)).astype(HALF)

    mix_base, ffn_base = core * MIX_HALF, core * FFN_HALF
    ffn_own = blocks(ffn, here.at, cut(ffn_base, FFN_HALF))

    def slab(place):
        return full.at[:, cut(MIX_HALF + place * FFN_HALF, FFN_HALF)]

    rings = gather_rings(here, mail, mix, mix_base, MIX_PARTS, MIX_GATHER, 0, DirectGather)
    for ring, (first, chunks) in zip(rings, MIX_PARTS):
        ring.start(full.at[:, first * LANE : (first + chunks) * LANE])
    slabs = [
        mail.post(slab(here.ring("x", step)), ffn_own, here.beside("x", step)) for step in (1, 3, 2)
    ]
    keep_mix = pltpu.make_async_copy(
        full.at[:, 0:MIX_HALF], blocks(mix, here.at, cut(mix_base, MIX_HALF)), local_sem.at[0]
    )
    keep_slab = pltpu.make_async_copy(slab(x), ffn_own, local_sem.at[1])
    keep_mix.start()
    keep_slab.start()
    keep_mix.wait()
    mix_rings = chain(
        rings,
        gather_rings(here, mail, mix, mix_base, MIX_PARTS, MIX_GATHER, 1, DirectGather),
    )
    keep_slab.wait()
    wait_all(slabs)
    ffn_rings = gather_rings(here, mail, ffn, ffn_base, FFN_PARTS, FFN_GATHER, 0)
    start_all(ffn_rings)
    mix_rings = chain(
        mix_rings, gather_rings(here, mail, mix, mix_base, MIX_PARTS, MIX_GATHER, 2)
    )
    swaps = swap_pieces(here, mail, mix_rings, (0,))
    relay_all(ffn_rings)
    relay_all(mix_rings)
    swaps += swap_pieces(here, mail, mix_rings, (1, -1))
    stream = RingGather(here, mail, "x", row_pick(backs))
    stream.start()
    finish_all(ffn_rings)
    ffn_rings = gather_rings(here, mail, ffn, ffn_base, FFN_PARTS, FFN_GATHER, 1)
    start_all(ffn_rings)
    for ring in mix_rings:
        ring.finish()
        swaps += swap_pieces(here, mail, [ring], (2,))
    stream.relay()
    ffn_swaps = swap_pieces(here, mail, ffn_rings, (0,))
    wait_all(swaps)
    halo_in.wait_recv()
    mixer_forward(here, tokens, halo, flags, mix, proj, normed, gated, resid, rows, twos.at[x])
    two_ring = RingGather(here, mail, "x", row_pick(twos))
    two_ring.start()
    relay_all(ffn_rings)
    ffn_swaps += swap_pieces(here, mail, ffn_rings, (1, -1))
    early = [mail.post(normed, normed_in, twin), mail.post(gated, gated_in, twin)]
    two_ring.relay()
    turn(turned.at[0, :, 0:ALL], normed[...])
    turn(turned.at[2, :, 0:TOK], gated[...])
    finish_all(ffn_rings)
    ffn_swaps += swap_pieces(here, mail, ffn_rings, (2,))
    stream.finish()
    for block in range(4):
        turn(turned_ffn.at[0, 1, :, block * TOK : (block + 1) * TOK], backs[block])
    shared = [mail.post(turned_ffn.at[0, 1], turned_ffn.at[1, 1], twin)]
    wait_all(ffn_swaps)
    two_ring.finish()
    gathered = len(mail.posted)

    @pl.loop(0, SLAB // TILE)
    def _(tile):
        ffn_hidden(ffn, twos, backs, acts, tile * TILE, TILE)

    ffn_hidden(ffn, twos, backs, acts, SLAB // TILE * TILE, SLAB % TILE)
    shared.append(
        mail.post(acts.at[:, cut((1 - core) * FFN_HALF, FFN_HALF)], acts_in, twin)
    )
    ffn_tokens(ffn, acts, work, (0, 1))
    two_ring = RingReduce(here, mail, "x", row_pick(work), two_near, two_far)
    two_ring.start()
    for block in range(4):
        turn(turned_ffn.at[0, 0, :, block * TOK : (block + 1) * TOK], twos[block])
    shared.append(mail.post(turned_ffn.at[0, 0], turned_ffn.at[1, 0], twin))
    ffn_tokens(ffn, acts, ffn_work, (2,))
    two_ring.relay()
    mail.settle(gathered)
    wait_all(shared)
    ffn_rings = reduce_rings(here, mail, ffn, ffn_base, FFN_PARTS, FFN_REDUCE, ffn_near, ffn_far, 0)
    for part, ring in zip(FFN_PARTS, ffn_rings):
        ffn_weight_grads(ffn, acts, acts_in, turned_ffn, core, part)
        ring.start()
    two_ring.finish()
    value = resid[...]
    scale = norm_scale(value)
    unit = value * scale
    d_two = work[x].astype(FLOAT)
    small[...] = jnp.zeros_like(small)
    small[1:2] = jnp.sum(d_two * unit, axis=0, keepdims=True)
    d_value = flags[:, 2:3] * cotangent[...].astype(FLOAT) + norm_back(unit, scale, rows[1:2], d_two)
    d_resid[...] = d_value
    branch[0] = d_value[:, 0:HALF_D].astype(HALF)
    branch[1] = d_value[:, HALF_D:D].astype(HALF)
    late = [mail.post(branch.at[1 - core], branch_in, twin)]
    out_ring = RingReduce(here, mail, "x", row_pick(ffn_work), out_near, out_far)
    out_ring.start()
    mixer_backward(here, flags, mix, proj, rows, branch, grads, small)
    late.append(mail.post(grads.at[1 - core], grads_in, twin))
    relay_all(ffn_rings)
    out_ring.relay()
    projection_back(mix, grads, d_normed)
    x_own, x_edge = tokens[...].astype(FLOAT), halo[...].astype(FLOAT)
    scale = norm_scale(x_own)
    unit = x_own * scale
    small[0:1] = jnp.sum(d_normed[0:TOK] * unit, axis=0, keepdims=True) + jnp.sum(
        d_normed[TOK:ALL] * x_edge * norm_scale(x_edge), axis=0, keepdims=True
    )
    late.append(mail.post(small, small_in, twin))
    edge = mail.post(d_normed.at[pl.ds(TOK, 8)], edge_in, here.along(-1))
    wait_all(early)
    turn(turned.at[1, :, 0:ALL], normed_in[...])
    turn(turned.at[3, :, 0:TOK], gated_in[...])
    wait_all(late)
    mix_rings = reduce_rings(here, mail, total, 0, MIX_PARTS, MIX_REDUCE, mix_near, mix_far, 0)
    mixer_weight_grads(here, grads, branch, turned, grads_in, branch_in, total, mix_rings)
    small_sum = small[...] + small_in[...]
    total[:, :, :, :, :, SMALL_AT:MIX_HALF] = (
        jnp.transpose(small_sum).astype(HALF).reshape(GRID + (16, LANE))
    )
    mix_rings[2].start()
    ffn_rings = chain(
        ffn_rings,
        reduce_rings(here, mail, ffn, ffn_base, FFN_PARTS, FFN_REDUCE, ffn_near, ffn_far, 1),
    )
    relay_all(mix_rings)
    relay_all(ffn_rings)
    edge.wait_recv()
    d_first = (
        d_normed[0:TOK] + flags[:, 3:4] * edge_in[0:1] + flags[:, 4:5] * edge_in[1:2]
    )
    grad_tokens[...] = (d_resid[...] + norm_back(unit, scale, rows[0:1], d_first)).astype(HALF)
    mix_rings = chain(
        mix_rings,
        reduce_rings(here, mail, total, 0, MIX_PARTS, MIX_REDUCE, mix_near, mix_far, 1),
    )
    finish_all(ffn_rings)
    copies = []
    for step in (1, 3, 2):
        there = here.ring("x", step)
        copies.append(
            mail.post(
                blocks(ffn, {**here.at, "x": there}, cut(ffn_base, FFN_HALF)),
                ffn_rest.at[x],
                here.beside("x", step),
            )
        )
    ffn_rest[x] = ffn_own[...]
    relay_all(mix_rings)
    out_ring.finish()
    mixed_out[...] = (flags[:, 2:3] * (resid[...] + ffn_work[x].astype(FLOAT))).astype(HALF)
    mix_rings = chain(
        mix_rings,
        reduce_rings(here, mail, total, 0, MIX_PARTS, MIX_REDUCE, mix_near, mix_far, 2),
    )
    wait_all(copies)
    ffn_swap = mail.post(ffn_rest, ffn_mate, twin)
    ffn_owned[:, :, cut(core * FFN_HALF, FFN_HALF)] = ffn_rest[...].astype(FLOAT)
    relay_all(mix_rings)
    ffn_swap.wait_recv()
    ffn_owned[:, :, cut((1 - core) * FFN_HALF, FFN_HALF)] = ffn_mate[...].astype(FLOAT)
    lines = pl.ds(pl.multiple_of(8 * core, 8), 8)
    for place in range(4):
        cols = slice(place * SLAB, (place + 1) * SLAB)
        for kind, target in enumerate((grad_gate, grad_up, grad_down)):
            target[:, cols] = ffn_owned[place, lines, kind * SLAB : (kind + 1) * SLAB]
    finish_all(mix_rings)
    own_sum = blocks(total, here.at, slice(None))
    mix_swap = mail.post(own_sum, mix_mate, twin)
    mix_owned[:, cut(core * MIX_HALF, MIX_HALF)] = own_sum[...].astype(FLOAT)
    mix_swap.wait_recv()
    mix_owned[:, cut((1 - core) * MIX_HALF, MIX_HALF)] = mix_mate[...].astype(FLOAT)
    for half in range(2):
        at = half * MIX_HALF
        for which in range(3):
            start = which * D + half * HALF_D
            grad_in[:, start : start + HALF_D] = mix_owned[
                lines, at + which * HALF_D : at + (which + 1) * HALF_D
            ]
        grad_out[:, half * HALF_D : (half + 1) * HALF_D] = mix_owned[lines, at + OUT_AT : at + SMALL_AT]
    grad_small[...] = mix_owned[lines, SMALL_AT:MIX_HALF]
    mail.settle(len(mail.posted))


def write_kernel(*refs):
    count = (len(refs) - 2) // 2
    ins, outs = refs[:count], refs[count:]
    for source, target in zip(ins[:-1], outs):
        target[...] = source[...]
    small = jnp.transpose(ins[-1][...])
    outs[-3][...] = small[0:1, 0:8]
    outs[-2][...] = small[1:2, 0:8]
    outs[-1][...] = small[2:5, 0:8]


def vmem():
    return pl.BlockSpec(memory_space=pltpu.VMEM)


def sems(count):
    return pltpu.SemaphoreType.DMA((count,))


def params(number):
    return pltpu.CompilerParams(
        collective_id=number, has_side_effects=True, vmem_limit_bytes=VMEM_LIMIT
    )


def shape(dims, dtype):
    return jax.ShapeDtypeStruct(dims, dtype)


def whole_block(*operands):
    landing = [
        pltpu.VMEM(dims, HALF)
        for part in landing_shapes(MIX_PARTS, MIX_REDUCE) + landing_shapes(FFN_PARTS, FFN_REDUCE)
        for dims in part
    ]
    stream_landing = [pltpu.VMEM((TOK, D), HALF)] * 2 + [pltpu.VMEM((TOK // 2, D), HALF)] * 2
    return pl.pallas_call(
        block_kernel,
        out_shape=(
            shape((TOK, D), HALF),
            shape((TOK, D), HALF),
            shape((8, 3 * D), FLOAT),
            shape((8, D), FLOAT),
            shape((8, LANE), FLOAT),
            shape((8, 4 * SLAB), FLOAT),
            shape((8, 4 * SLAB), FLOAT),
            shape((8, 4 * SLAB), FLOAT),
        ),
        in_specs=[vmem()] * 10,
        out_specs=(vmem(),) * 8,
        scratch_shapes=[
            pltpu.VMEM((2, 16, OWN_COLS), HALF),
            pltpu.VMEM((16, MIX_COLS), FLOAT),
            pltpu.VMEM((4, 16, FFN_COLS), FLOAT),
            pltpu.VMEM((LANE, LANE), FLOAT),
            pltpu.VMEM((8, LANE), HALF),
            pltpu.VMEM((TOK, LANE), FLOAT),
            pltpu.VMEM((16, D), HALF),
            pltpu.VMEM((16, OWN_COLS), HALF),
            pltpu.VMEM((16, OWN_COLS), HALF),
            pltpu.VMEM((16, D), HALF),
            pltpu.VMEM(GRID + (16, MIX_COLS), HALF),
            pltpu.VMEM(GRID + (16, FFN_COLS), HALF),
            pltpu.VMEM((4, TOK, D), HALF),
            pltpu.VMEM((4, TOK, D), HALF),
            pltpu.VMEM((3, ALL, D), FLOAT),
            pltpu.VMEM((ALL, D), HALF),
            pltpu.VMEM((TOK, D), HALF),
            pltpu.VMEM((TOK, D), FLOAT),
            pltpu.VMEM((8, D), FLOAT),
            pltpu.VMEM((4 * TOK, FFN_COLS), HALF),
            pltpu.VMEM((2, 2, D, 4 * TOK), HALF),
            pltpu.VMEM(GRID + (16, MIX_HALF), HALF),
            pltpu.VMEM((16, MIX_HALF), HALF),
            pltpu.VMEM((4 * TOK, FFN_HALF), HALF),
            pltpu.VMEM((4, 16, FFN_HALF), HALF),
            pltpu.VMEM((4, 16, FFN_HALF), HALF),
            pltpu.VMEM((4, TOK, D), HALF),
            pltpu.VMEM((4, TOK, D), HALF),
            pltpu.VMEM((2, TOK, HALF_D), HALF),
            pltpu.VMEM((2, ALL, OUT_AT), HALF),
            pltpu.VMEM((ALL, D), FLOAT),
            pltpu.VMEM((LANE, D), FLOAT),
            pltpu.VMEM((4, D, ALL), HALF),
            pltpu.VMEM((ALL, D), HALF),
            pltpu.VMEM((TOK, D), HALF),
            pltpu.VMEM((TOK, HALF_D), HALF),
            pltpu.VMEM((ALL, OUT_AT), HALF),
            pltpu.VMEM((LANE, D), FLOAT),
            pltpu.VMEM((8, D), FLOAT),
            pltpu.VMEM((TOK, D), FLOAT),
        ]
        + stream_landing * 2
        + landing
        + [sems(176), sems(176), sems(2)],
        compiler_params=params(0),
        name="whole_block",
    )(*operands)


def local(
    tokens,
    gain_mix,
    in_weight,
    conv_weight,
    out_weight,
    gain_ffn,
    gate_weight,
    up_weight,
    down_weight,
    live_counts,
    positions,
    cotangent,
):
    vectors = jnp.concatenate([gain_mix[None], gain_ffn[None], conv_weight], axis=0)
    mixed_out, grad_tokens, grad_in, grad_out, grad_small, grad_gate, grad_up, grad_down = whole_block(
        in_weight, out_weight, gate_weight, up_weight, jnp.transpose(down_weight), vectors,
        tokens, positions.reshape(1, TOK), live_counts, cotangent,
    )
    plain = (mixed_out, grad_tokens, grad_in, grad_out, grad_gate, grad_up, grad_down)
    mixed_out, grad_tokens, grad_in, grad_out, grad_gate, grad_up, grad_down, one, two, taps = (
        pl.pallas_call(
            write_kernel,
            out_shape=tuple(shape(value.shape, value.dtype) for value in plain)
            + (
                shape((1, 8), FLOAT),
                shape((1, 8), FLOAT),
                shape((3, 8), FLOAT),
            ),
            in_specs=[vmem()] * 8,
            out_specs=(vmem(),) * 10,
            name="write",
            compiler_params=pltpu.CompilerParams(vmem_limit_bytes=VMEM_LIMIT),
        )(*plain, grad_small)
    )
    return (
        mixed_out,
        grad_tokens,
        one.reshape(8),
        grad_in,
        taps,
        grad_out,
        two.reshape(8),
        grad_gate,
        grad_up,
        jnp.transpose(grad_down),
    )


def solution(mesh):
    rows = P(("fsdp", "seq"), None)
    flat = P(("fsdp", "seq"))
    cols = P(None, ("fsdp", "seq"))
    return jax.shard_map(
        local,
        mesh=mesh,
        in_specs=(rows, flat, rows, cols, rows, flat, rows, rows, cols, P("fsdp", "seq"), flat, rows),
        out_specs=(rows, rows, flat, rows, cols, rows, flat, rows, rows, cols),
        check_vma=False,
    )
```

```python
import jax
import jax.numpy as jnp
from jax import lax
from jax.experimental import pallas as pl
from jax.experimental.pallas import tpu as pltpu
from jax.sharding import PartitionSpec as P

EPS = 1e-05
FLOAT = jnp.float32
HALF = jnp.bfloat16
MESH = pl.DeviceIdType.MESH
LANE = 128
D = 1024
SLAB = 1152
MIX_COLS = 34 * LANE
FFN_COLS = 28 * LANE
MIX_HALF = MIX_COLS // 2
FFN_HALF = FFN_COLS // 2
OWN_COLS = MIX_HALF + 4 * FFN_HALF
HALF_D = D // 2
OUT_AT = 3 * HALF_D
SMALL_AT = 4 * HALF_D
TILE = 256
TOK = 128
ALL = TOK + 16
MIX_PARTS = ((0, 6), (6, 6), (12, 5))
MIX_GATHER = (("y", "z", "x"), ("z", "x", "y"), ("x", "y", "z"))
MIX_REDUCE = (("x", "z", "y"), ("y", "x", "z"), ("z", "y", "x"))
FFN_PARTS = ((0, 8), (8, 6))
FFN_GATHER = (("y", "z"), ("z", "y"))
FFN_REDUCE = (("y", "z"), ("z", "y"))
GRID = (2, 4, 4, 2)
MIX_LANDING = 4 * 3 * len(MIX_PARTS)
VMEM_LIMIT = 60 * 2**20


class Here:
    def __init__(self):
        fsdp = lax.axis_index("fsdp")
        seq = lax.axis_index("seq")
        self.fsdp, self.seq = fsdp, seq
        self.at = {
            "x": lax.div(seq, 4),
            "y": lax.rem(fsdp, 4),
            "z": lax.div(fsdp, 4) * 2 + lax.rem(lax.div(seq, 2), 2),
        }
        self.core = lax.rem(seq, 2)

    def device(self, core, **moved):
        at = {**self.at, **moved}
        return (
            lax.div(at["z"], 2) * 4 + at["y"],
            (at["x"] * 2 + lax.rem(at["z"], 2)) * 2 + core,
        )

    def ring(self, axis, step):
        return lax.rem(self.at[axis] + (step + 4) % 4, 4)

    def beside(self, axis, step):
        return self.device(self.core, **{axis: self.ring(axis, step)})

    def twin(self):
        return self.device(1 - self.core)

    def along(self, step):
        return (self.fsdp, lax.rem(self.seq + (step + 16) % 16, 16))


def greet(devices):
    barrier = pltpu.get_barrier_semaphore()
    for device in devices:
        pl.semaphore_signal(barrier, inc=1, device_id=device, device_id_type=MESH)
    return barrier, len(devices)


class Mail:
    def __init__(self, send, recv):
        self.send, self.recv, self.posted, self.settled = send, recv, [], 0

    def post(self, src, dst, device):
        place = len(self.posted)
        copy = pltpu.make_async_remote_copy(
            src_ref=src,
            dst_ref=dst,
            send_sem=self.send.at[place],
            recv_sem=self.recv.at[place],
            device_id=device,
            device_id_type=MESH,
        )
        copy.start()
        self.posted.append(copy)
        return copy

    def settle(self, count):
        for copy in self.posted[self.settled : count]:
            copy.wait_send()
        self.settled = count


def cut(start, count):
    return pl.ds(pl.multiple_of(start, LANE), count)


def blocks(ref, at, cols):
    whole = slice(None)
    z = at["z"]
    high, low = (whole, whole) if z is None else (lax.div(z, 2), lax.rem(z, 2))
    y = whole if at["y"] is None else at["y"]
    x = whole if at["x"] is None else at["x"]
    return ref.at[high, y, x, low, :, cols]


class RingGather:
    def __init__(self, here, mail, axis, pick):
        self.here, self.mail, self.axis, self.pick = here, mail, axis, pick

    def start(self, source=None):
        here, axis = self.here, self.axis
        own = self.pick(here.at[axis], None)
        source = own if source is None else source
        self.to_up = self.mail.post(source, own, here.beside(axis, 1))
        self.to_down = self.mail.post(source, own, here.beside(axis, -1))

    def relay(self):
        here, axis = self.here, self.axis
        self.to_up.wait_recv()
        first = self.pick(here.ring(axis, -1), 0)
        self.far_up = self.mail.post(first, first, here.beside(axis, 1))
        self.to_down.wait_recv()
        second = self.pick(here.ring(axis, 1), 1)
        self.far_down = self.mail.post(second, second, here.beside(axis, -1))

    def finish(self):
        self.far_up.wait_recv()
        self.far_down.wait_recv()


class RingReduce:
    def __init__(self, here, mail, axis, pick, near, far):
        self.here, self.mail, self.axis, self.pick = here, mail, axis, pick
        self.near, self.far = near, far

    def start(self):
        here, axis = self.here, self.axis
        away = here.ring(axis, 2)
        self.far_up = self.mail.post(self.pick(away, 0), self.far[0], here.beside(axis, 1))
        self.far_down = self.mail.post(self.pick(away, 1), self.far[1], here.beside(axis, -1))

    def relay(self):
        here, axis = self.here, self.axis
        above, below = here.ring(axis, 1), here.ring(axis, -1)
        self.far_up.wait_recv()
        add_into(self.pick(above, 0), self.far[0])
        self.to_up = self.mail.post(self.pick(above, None), self.near[0], here.beside(axis, 1))
        self.far_down.wait_recv()
        add_into(self.pick(below, 1), self.far[1])
        self.to_down = self.mail.post(self.pick(below, None), self.near[1], here.beside(axis, -1))

    def finish(self):
        self.to_up.wait_recv()
        self.to_down.wait_recv()
        own = self.pick(self.here.at[self.axis], None)
        add_into(own, self.near[0], self.near[1])


class DirectGather(RingGather):
    def start(self, source=None):
        here, axis = self.here, self.axis
        own = self.pick(here.at[axis], None)
        source = own if source is None else source
        self.copies = [
            self.mail.post(source, own, here.beside(axis, step)) for step in (1, -1, 2)
        ]

    def relay(self):
        pass

    def finish(self):
        wait_all(self.copies)


class DirectReduce(RingReduce):
    def start(self):
        here, axis = self.here, self.axis
        self.landed = [self.near[0], self.near[1], self.far[0]]
        self.copies = [
            self.mail.post(
                self.pick(here.ring(axis, step), None), landed, here.beside(axis, step)
            )
            for step, landed in zip((1, -1, 2), self.landed)
        ]

    def relay(self):
        pass

    def finish(self):
        wait_all(self.copies)
        add_into(self.pick(self.here.at[self.axis], None), *self.landed)


def add_into(target, *terms):
    if len(terms) == 1:
        target[...] = target[...] + terms[0][...]
        return
    total = target[...].astype(FLOAT)
    for term in terms:
        total = total + term[...].astype(FLOAT)
    target[...] = total.astype(target.dtype)


def column_pick(ref, fixed, axis, start, chunks):
    split = (chunks + 1) // 2

    def pick(place, half):
        first, count = {None: (0, chunks), 0: (0, split), 1: (split, chunks - split)}[half]
        return blocks(ref, {**fixed, axis: place}, cut(start + first * LANE, count * LANE))

    return pick


def row_pick(ref):
    def pick(place, half):
        rows = ref.shape[-2]
        part = {None: slice(None), 0: pl.ds(0, rows // 2), 1: pl.ds(rows // 2, rows // 2)}[half]
        return ref.at[place, part]

    return pick


def gather_rings(here, mail, ref, base, parts, orders, stage, kind=RingGather):
    rings = []
    for (first, chunks), order in zip(parts, orders):
        fixed = dict(here.at)
        for axis in ("x", "y", "z"):
            if axis not in order or axis in order[:stage]:
                fixed[axis] = None
        pick = column_pick(ref, fixed, order[stage], base + first * LANE, chunks)
        rings.append(kind(here, mail, order[stage], pick))
    return rings


def start_all(rings):
    for ring in rings:
        ring.start()


def relay_all(rings):
    for ring in rings:
        ring.relay()


def finish_all(rings):
    for ring in rings:
        ring.finish()


def chain(rings, later):
    for ring, following in zip(rings, later):
        ring.finish()
        following.start()
    return later


def swap_pieces(here, mail, rings, steps):
    copies = []
    for ring in rings:
        for step in steps:
            piece = ring.pick(here.ring(ring.axis, step), None)
            copies.append(mail.post(piece, piece, here.twin()))
    return copies


def wait_all(copies):
    for copy in copies:
        copy.wait_recv()


def near_list(here, axes):
    return [here.beside(axis, step) for axis in axes for step in (1, -1)]


def mat(ref, cols):
    block = ref[:, :, :, :, :, cols]
    return block.reshape(D, block.shape[-1])


def mat_rows(ref, tile, cols):
    block = ref[lax.div(tile, 2), pl.ds(lax.rem(tile, 2) * 2, 2), :, :, :, cols]
    return block.reshape(TILE, block.shape[-1])


def mix_cols(tile, which):
    return cut(lax.div(tile, 2) * MIX_HALF + which * HALF_D + lax.rem(tile, 2) * TILE, TILE)


def dot(left, right):
    return jnp.dot(left, right, preferred_element_type=FLOAT)


def dot_nt(left, right):
    return lax.dot_general(
        left, right, (((1,), (1,)), ((), ())), preferred_element_type=FLOAT
    )


def norm_scale(values):
    return lax.rsqrt(jnp.mean(values * values, axis=-1, keepdims=True) + EPS)


def norm_back(normal, row_scale, gain_row, upstream):
    weighted = upstream * gain_row
    return row_scale * (
        weighted - normal * jnp.mean(weighted * normal, axis=-1, keepdims=True)
    )


def row_index(rows, cols):
    return lax.broadcasted_iota(jnp.int32, (rows, cols), 0)


def conv_terms(mixed, halo):
    rows = row_index(TOK, mixed.shape[1])
    one = pltpu.roll(mixed, 1, 0)
    two = pltpu.roll(mixed, 2, 0)
    one = jnp.where(rows == 0, halo[1:2], one)
    two = jnp.where(rows == 0, halo[0:1], jnp.where(rows == 1, halo[1:2], two))
    return one, two


def follows_of(here):
    return jnp.minimum(here.seq, 1).astype(FLOAT)


def mixer_forward(here, tokens, halo, flags, mix, proj, normed, gated, resid, rows, two):
    small = jnp.transpose(mat(mix, slice(SMALL_AT, SMALL_AT + LANE)).astype(FLOAT))
    rows[...] = small[0:8]
    gain = rows[0:1]
    x = tokens[...].astype(FLOAT)
    normed[0:TOK] = (x * norm_scale(x) * gain).astype(HALF)
    before = halo[...].astype(FLOAT)
    normed[TOK:ALL] = (before * norm_scale(before) * gain).astype(HALF)
    follows = follows_of(here)
    first_ok, second_ok = flags[:, 0:1], flags[:, 1:2]

    @pl.loop(0, D // TILE)
    def _(tile):
        feats = cut(tile * TILE, TILE)
        parts = [dot(normed[...], mat(mix, mix_cols(tile, which))) for which in range(3)]
        for which in range(3):
            proj[which, :, feats] = parts[which]
        mixed = parts[0] * parts[2]
        own = mixed[0:TOK]
        one, second = conv_terms(own, mixed[TOK:ALL] * follows)
        conv = (
            rows[2:3, feats] * own
            + first_ok * rows[3:4, feats] * one
            + second_ok * rows[4:5, feats] * second
        )
        gated[:, feats] = (parts[1][0:TOK] * conv).astype(HALF)

    @pl.loop(0, D // TILE)
    def _(tile):
        feats = cut(tile * TILE, TILE)
        branch = dot(gated[...], mat(mix, mix_cols(tile, 3)))
        resid[:, feats] = tokens[:, feats].astype(FLOAT) + branch

    value = resid[...]
    two[...] = (value * norm_scale(value) * rows[1:2]).astype(HALF)


def reduce_rings(here, mail, ref, base, parts, orders, near, far, stage):
    rings = []
    for number, ((first, chunks), order) in enumerate(zip(parts, orders)):
        fixed = {"x": None, "y": None, "z": None}
        for axis in order[:stage]:
            fixed[axis] = here.at[axis]
        pick = column_pick(ref, fixed, order[stage], base + first * LANE, chunks)
        kind = RingReduce if stage <= 1 else DirectReduce
        rings.append(kind(here, mail, order[stage], pick, near[number][stage], far[number][stage]))
    return rings


def landing_shapes(parts, orders):
    shapes = []
    for (_, chunks), order in zip(parts, orders):
        split = (chunks + 1) // 2
        done = []
        for stage in range(len(order)):
            gone = order[: stage + 1]
            lead = ()
            if "z" not in gone:
                lead += (2,)
            if "y" not in gone:
                lead += (4,)
            if "x" not in gone:
                lead += (4,)
            if "z" not in gone:
                lead += (2,)
            done += [lead + (16, chunks * LANE)] * 2
            if stage <= 1:
                done += [lead + (16, split * LANE), lead + (16, (chunks - split) * LANE)]
            else:
                done += [lead + (16, chunks * LANE), (16, LANE)]
        shapes.append(done)
    return shapes


def landing_refs(orders, refs):
    near, far = [], []
    place = 0
    for order in orders:
        near.append([])
        far.append([])
        for _ in order:
            near[-1].append(refs[place : place + 2])
            far[-1].append(refs[place + 2 : place + 4])
            place += 4
    return near, far


def ffn_hidden(ffn, twos, backs, acts, start, width):
    value = twos[...].reshape(4 * TOK, D)
    gate = dot(value, mat(ffn, cut(start, width)))
    upper = dot(value, mat(ffn, cut(SLAB + start, width)))
    d_active = dot(backs[...].reshape(4 * TOK, D), mat(ffn, cut(2 * SLAB + start, width)))
    sig = jax.nn.sigmoid(gate)
    swish = gate * sig
    acts[:, cut(start, width)] = (d_active * upper * (sig * (1.0 + gate * (1.0 - sig)))).astype(HALF)
    acts[:, cut(SLAB + start, width)] = (d_active * swish).astype(HALF)
    acts[:, cut(2 * SLAB + start, width)] = (swish * upper).astype(HALF)


def ffn_tokens(ffn, acts, target, kinds):
    @pl.loop(0, D // TILE)
    def _(tile):
        total = 0.0
        for kind in kinds:
            cols = slice(kind * SLAB, (kind + 1) * SLAB)
            total += dot_nt(acts[:, cols], mat_rows(ffn, tile, cols))
        target[:, :, cut(tile * TILE, TILE)] = total.astype(HALF).reshape(4, TOK, TILE)


def ffn_weight_grads(ffn, acts, acts_in, turned, half, part):
    first, chunks = part

    @pl.loop(first * LANE // TILE, (first + chunks) * LANE // TILE)
    def _(tile):
        cols = cut(half * FFN_HALF + tile * TILE, TILE)
        side = half * jnp.minimum(lax.div(tile, 2), 1)
        value = dot(turned[0, side], acts[:, cols])
        value += dot(turned[1, side], acts_in[:, cut(tile * TILE, TILE)])
        ffn[:, :, :, :, :, cols] = value.astype(HALF).reshape(GRID + (16, TILE))


def turn(target, value):
    target[...] = jnp.transpose(value.astype(FLOAT)).astype(HALF)


def mixer_backward(here, flags, mix, proj, rows, branch, grads, small):
    follows = follows_of(here)
    first_ok, second_ok = flags[:, 0:1], flags[:, 1:2]

    @pl.loop(0, D // TILE)
    def _(tile):
        feats = cut(tile * TILE, TILE)
        gated = dot_nt(branch[0], mat_rows(mix, tile, slice(OUT_AT, OUT_AT + HALF_D)))
        gated += dot_nt(
            branch[1], mat_rows(mix, tile, slice(MIX_HALF + OUT_AT, MIX_HALF + OUT_AT + HALF_D))
        )
        b_all, c_all, v_all = (proj[which, :, feats] for which in range(3))
        mixed = b_all * v_all
        own = mixed[0:TOK]
        one, second = conv_terms(own, mixed[TOK:ALL] * follows)
        tap_one, tap_two = rows[3:4, feats], rows[4:5, feats]
        conv = rows[2:3, feats] * own + first_ok * tap_one * one + second_ok * tap_two * second
        d_c = gated * conv
        d_conv = gated * c_all[0:TOK]
        small[2:3, feats] = jnp.sum(d_conv * own, axis=0, keepdims=True)
        small[3:4, feats] = jnp.sum(d_conv * first_ok * one, axis=0, keepdims=True)
        small[4:5, feats] = jnp.sum(d_conv * second_ok * second, axis=0, keepdims=True)
        term_one = first_ok * tap_one * d_conv
        term_two = second_ok * tap_two * d_conv
        lines = row_index(TOK, TILE)
        zero = jnp.zeros((TOK, TILE), FLOAT)
        d_mixed = (
            rows[2:3, feats] * d_conv
            + jnp.where(lines < TOK - 1, pltpu.roll(term_one, TOK - 1, 0), zero)
            + jnp.where(lines < TOK - 2, pltpu.roll(term_two, TOK - 2, 0), zero)
        )
        lines = row_index(16, TILE)
        zero = jnp.zeros((16, TILE), FLOAT)
        d_halo = follows * (
            jnp.where(lines < 2, term_two[0:16], zero)
            + jnp.where(lines == 1, pltpu.roll(term_one[0:16], 1, 0), zero)
        )
        half, place = lax.div(tile, 2), lax.rem(tile, 2) * TILE
        for which, (main, edge) in enumerate(
            (
                (d_mixed * v_all[0:TOK], d_halo * v_all[TOK:ALL]),
                (d_c, zero),
                (d_mixed * b_all[0:TOK], d_halo * b_all[TOK:ALL]),
            )
        ):
            cols = cut(which * HALF_D + place, TILE)
            grads[half, 0:TOK, cols] = main.astype(HALF)
            grads[half, TOK:ALL, cols] = edge.astype(HALF)


def projection_back(mix, grads, normed_grad):
    @pl.loop(0, D // TILE)
    def _(tile):
        total = dot_nt(grads[0], mat_rows(mix, tile, slice(0, OUT_AT)))
        total += dot_nt(grads[1], mat_rows(mix, tile, slice(MIX_HALF, MIX_HALF + OUT_AT)))
        normed_grad[:, cut(tile * TILE, TILE)] = total


def mixer_weight_grads(here, grads, branch, turned, grads_in, branch_in, total, rings):
    def put(cols, value):
        total[:, :, :, :, :, cols] = value.astype(HALF).reshape(GRID + (16, TILE))

    for ring, (first, chunks) in zip(rings[:2], MIX_PARTS):

        @pl.loop(first * LANE // TILE, (first + chunks) * LANE // TILE)
        def _(tile):
            cols = cut(tile * TILE, TILE)
            put(cols, dot(turned[0], grads[here.core, :, cols]) + dot(turned[1], grads_in[:, cols]))

        ring.start()

    @pl.loop(0, HALF_D // TILE)
    def _(tile):
        cols = cut(tile * TILE, TILE)
        value = dot(turned[2, :, 0:TOK], branch[here.core, :, cols])
        value += dot(turned[3, :, 0:TOK], branch_in[:, cols])
        put(cut(OUT_AT + tile * TILE, TILE), value)


def twice(value):
    value = value.astype(FLOAT)
    return jnp.concatenate([value, value], axis=0).astype(HALF)


def lay_out(own, in_rows, out_rows, gate_rows, up_rows, down_rows, small_rows):
    for half in range(2):
        for which in range(3):
            start = which * D + half * HALF_D
            own[half, :, which * HALF_D : (which + 1) * HALF_D] = twice(
                in_rows[:, start : start + HALF_D]
            )
        own[half, :, OUT_AT:SMALL_AT] = twice(out_rows[:, half * HALF_D : (half + 1) * HALF_D])
        own[half, :, SMALL_AT:MIX_HALF] = twice(small_rows[...])
    early = FFN_HALF - SLAB
    rest = SLAB - early
    for place in range(4):
        at, start = MIX_HALF + place * FFN_HALF, place * SLAB
        own[0, :, at : at + SLAB] = twice(gate_rows[:, start : start + SLAB])
        own[0, :, at + SLAB : at + FFN_HALF] = twice(up_rows[:, start : start + early])
        own[1, :, at : at + rest] = twice(up_rows[:, start + early : start + SLAB])
        own[1, :, at + rest : at + rest + SLAB] = twice(down_rows[:, start : start + SLAB])
        own[1, :, at + rest + SLAB : at + FFN_HALF] = jnp.zeros((16, LANE), HALF)


def lay_flags(board, flags, tail, tokens, positions, counts):
    slots = lax.broadcasted_iota(jnp.int32, (1, LANE), 1)
    place, count = positions[...], jnp.broadcast_to(counts[...], (1, LANE))

    def bit(condition):
        return jnp.where(condition, jnp.ones((1, LANE), FLOAT), jnp.zeros((1, LANE), FLOAT))

    board[...] = jnp.zeros_like(board)
    board[0:1] = bit(place >= 1)
    board[1:2] = bit(place >= 2)
    board[2:3] = bit(slots < count)
    for row in (3, 16):
        board[row : row + 1] = bit(slots == count - 2)
        board[row + 1 : row + 2] = bit(slots == count - 1)
    flags[...] = jnp.transpose(board[...])
    tail[...] = dot(board[16:32].astype(HALF), tokens[...]).astype(HALF)


def lay_small(board, small_rows, vectors):
    board[...] = jnp.zeros_like(board)
    board[0:5, 0:8] = vectors[...].astype(FLOAT)
    small_rows[...] = jnp.transpose(board[...])[0:8].astype(HALF)


def block_kernel(
    in_rows, out_rows, gate_rows, up_rows, down_rows, vectors, tokens, positions, counts, cotangent,
    mixed_out, grad_tokens, grad_in, grad_out, grad_small, grad_gate, grad_up, grad_down,
    own, mix_owned, ffn_owned, board, small_rows, flags, tail,
    mate, full, halo, mix, ffn, twos, backs, proj, normed, gated, resid, rows, acts, turned_ffn,
    total, mix_mate, acts_in, ffn_rest, ffn_mate, work, ffn_work,
    branch, grads, d_normed, small, turned, normed_in, gated_in, branch_in, grads_in, small_in,
    edge_in, d_resid, *scratch,
):
    two_near, two_far = scratch[0:2], scratch[2:4]
    out_near, out_far = scratch[4:6], scratch[6:8]
    *landing, send, recv, local_sem = scratch[8:]
    mix_near, mix_far = landing_refs(MIX_REDUCE, landing[:MIX_LANDING])
    ffn_near, ffn_far = landing_refs(FFN_REDUCE, landing[MIX_LANDING:])
    here = Here()
    mail = Mail(send, recv)
    x, core = here.at["x"], here.core
    twin = here.twin()
    barrier, count = greet(
        near_list(here, ("x", "y", "z"))
        + [here.beside(axis, 2) for axis in ("x", "y", "z")]
        + [twin, here.along(1), here.along(-1)]
    )
    lay_flags(board, flags, tail, tokens, positions, counts)
    lay_small(board, small_rows, vectors)
    lay_out(own, in_rows, out_rows, gate_rows, up_rows, down_rows, small_rows)
    pl.semaphore_wait(barrier, count)
    rows_in = mail.post(own.at[1 - core], mate, twin)
    halo_in = mail.post(tail, halo, here.along(1))
    backs[x] = (flags[:, 2:3] * cotangent[...].astype(FLOAT)).astype(HALF)
    acts[:, 3 * SLAB : FFN_COLS] = jnp.zeros((4 * TOK, FFN_COLS - 3 * SLAB), HALF)
    rows_in.wait_recv()
    mine = lax.broadcasted_iota(jnp.int32, (16, OWN_COLS), 0) // 8 == core
    full[...] = jnp.where(mine, own[core].astype(FLOAT), mate[...].astype(FLOAT)).astype(HALF)

    mix_base, ffn_base = core * MIX_HALF, core * FFN_HALF
    ffn_own = blocks(ffn, here.at, cut(ffn_base, FFN_HALF))

    def slab(place):
        return full.at[:, cut(MIX_HALF + place * FFN_HALF, FFN_HALF)]

    rings = gather_rings(here, mail, mix, mix_base, MIX_PARTS, MIX_GATHER, 0, DirectGather)
    for ring, (first, chunks) in zip(rings, MIX_PARTS):
        ring.start(full.at[:, first * LANE : (first + chunks) * LANE])
    slabs = [
        mail.post(slab(here.ring("x", step)), ffn_own, here.beside("x", step)) for step in (1, 3, 2)
    ]
    keep_mix = pltpu.make_async_copy(
        full.at[:, 0:MIX_HALF], blocks(mix, here.at, cut(mix_base, MIX_HALF)), local_sem.at[0]
    )
    keep_slab = pltpu.make_async_copy(slab(x), ffn_own, local_sem.at[1])
    keep_mix.start()
    keep_slab.start()
    keep_mix.wait()
    mix_rings = chain(
        rings,
        gather_rings(here, mail, mix, mix_base, MIX_PARTS, MIX_GATHER, 1, DirectGather),
    )
    keep_slab.wait()
    wait_all(slabs)
    ffn_rings = gather_rings(here, mail, ffn, ffn_base, FFN_PARTS, FFN_GATHER, 0)
    start_all(ffn_rings)
    mix_rings = chain(
        mix_rings, gather_rings(here, mail, mix, mix_base, MIX_PARTS, MIX_GATHER, 2)
    )
    swaps = swap_pieces(here, mail, mix_rings, (0,))
    relay_all(ffn_rings)
    relay_all(mix_rings)
    swaps += swap_pieces(here, mail, mix_rings, (1, -1))
    stream = RingGather(here, mail, "x", row_pick(backs))
    stream.start()
    finish_all(ffn_rings)
    ffn_rings = gather_rings(here, mail, ffn, ffn_base, FFN_PARTS, FFN_GATHER, 1)
    start_all(ffn_rings)
    for ring in mix_rings:
        ring.finish()
        swaps += swap_pieces(here, mail, [ring], (2,))
    stream.relay()
    ffn_swaps = swap_pieces(here, mail, ffn_rings, (0,))
    wait_all(swaps)
    halo_in.wait_recv()
    mixer_forward(here, tokens, halo, flags, mix, proj, normed, gated, resid, rows, twos.at[x])
    two_ring = RingGather(here, mail, "x", row_pick(twos))
    two_ring.start()
    relay_all(ffn_rings)
    ffn_swaps += swap_pieces(here, mail, ffn_rings, (1, -1))
    early = [mail.post(normed, normed_in, twin), mail.post(gated, gated_in, twin)]
    two_ring.relay()
    turn(turned.at[0, :, 0:ALL], normed[...])
    turn(turned.at[2, :, 0:TOK], gated[...])
    finish_all(ffn_rings)
    ffn_swaps += swap_pieces(here, mail, ffn_rings, (2,))
    stream.finish()
    for block in range(4):
        turn(turned_ffn.at[0, 1, :, block * TOK : (block + 1) * TOK], backs[block])
    shared = [mail.post(turned_ffn.at[0, 1], turned_ffn.at[1, 1], twin)]
    wait_all(ffn_swaps)
    two_ring.finish()
    gathered = len(mail.posted)

    @pl.loop(0, SLAB // TILE)
    def _(tile):
        ffn_hidden(ffn, twos, backs, acts, tile * TILE, TILE)

    ffn_hidden(ffn, twos, backs, acts, SLAB // TILE * TILE, SLAB % TILE)
    shared.append(
        mail.post(acts.at[:, cut((1 - core) * FFN_HALF, FFN_HALF)], acts_in, twin)
    )
    ffn_tokens(ffn, acts, work, (0, 1))
    two_ring = RingReduce(here, mail, "x", row_pick(work), two_near, two_far)
    two_ring.start()
    for block in range(4):
        turn(turned_ffn.at[0, 0, :, block * TOK : (block + 1) * TOK], twos[block])
    shared.append(mail.post(turned_ffn.at[0, 0], turned_ffn.at[1, 0], twin))
    ffn_tokens(ffn, acts, ffn_work, (2,))
    two_ring.relay()
    mail.settle(gathered)
    wait_all(shared)
    ffn_rings = reduce_rings(here, mail, ffn, ffn_base, FFN_PARTS, FFN_REDUCE, ffn_near, ffn_far, 0)
    for part, ring in zip(FFN_PARTS, ffn_rings):
        ffn_weight_grads(ffn, acts, acts_in, turned_ffn, core, part)
        ring.start()
    two_ring.finish()
    value = resid[...]
    scale = norm_scale(value)
    unit = value * scale
    d_two = work[x].astype(FLOAT)
    small[...] = jnp.zeros_like(small)
    small[1:2] = jnp.sum(d_two * unit, axis=0, keepdims=True)
    d_value = flags[:, 2:3] * cotangent[...].astype(FLOAT) + norm_back(unit, scale, rows[1:2], d_two)
    d_resid[...] = d_value
    branch[0] = d_value[:, 0:HALF_D].astype(HALF)
    branch[1] = d_value[:, HALF_D:D].astype(HALF)
    late = [mail.post(branch.at[1 - core], branch_in, twin)]
    out_ring = RingReduce(here, mail, "x", row_pick(ffn_work), out_near, out_far)
    out_ring.start()
    mixer_backward(here, flags, mix, proj, rows, branch, grads, small)
    late.append(mail.post(grads.at[1 - core], grads_in, twin))
    relay_all(ffn_rings)
    out_ring.relay()
    projection_back(mix, grads, d_normed)
    x_own, x_edge = tokens[...].astype(FLOAT), halo[...].astype(FLOAT)
    scale = norm_scale(x_own)
    unit = x_own * scale
    small[0:1] = jnp.sum(d_normed[0:TOK] * unit, axis=0, keepdims=True) + jnp.sum(
        d_normed[TOK:ALL] * x_edge * norm_scale(x_edge), axis=0, keepdims=True
    )
    late.append(mail.post(small, small_in, twin))
    edge = mail.post(d_normed.at[pl.ds(TOK, 8)], edge_in, here.along(-1))
    wait_all(early)
    turn(turned.at[1, :, 0:ALL], normed_in[...])
    turn(turned.at[3, :, 0:TOK], gated_in[...])
    wait_all(late)
    mix_rings = reduce_rings(here, mail, total, 0, MIX_PARTS, MIX_REDUCE, mix_near, mix_far, 0)
    mixer_weight_grads(here, grads, branch, turned, grads_in, branch_in, total, mix_rings)
    small_sum = small[...] + small_in[...]
    total[:, :, :, :, :, SMALL_AT:MIX_HALF] = (
        jnp.transpose(small_sum).astype(HALF).reshape(GRID + (16, LANE))
    )
    mix_rings[2].start()
    ffn_rings = chain(
        ffn_rings,
        reduce_rings(here, mail, ffn, ffn_base, FFN_PARTS, FFN_REDUCE, ffn_near, ffn_far, 1),
    )
    relay_all(mix_rings)
    relay_all(ffn_rings)
    edge.wait_recv()
    d_first = (
        d_normed[0:TOK] + flags[:, 3:4] * edge_in[0:1] + flags[:, 4:5] * edge_in[1:2]
    )
    grad_tokens[...] = (d_resid[...] + norm_back(unit, scale, rows[0:1], d_first)).astype(HALF)
    mix_rings = chain(
        mix_rings,
        reduce_rings(here, mail, total, 0, MIX_PARTS, MIX_REDUCE, mix_near, mix_far, 1),
    )
    finish_all(ffn_rings)
    copies = []
    for step in (1, 3, 2):
        there = here.ring("x", step)
        copies.append(
            mail.post(
                blocks(ffn, {**here.at, "x": there}, cut(ffn_base, FFN_HALF)),
                ffn_rest.at[x],
                here.beside("x", step),
            )
        )
    ffn_rest[x] = ffn_own[...]
    relay_all(mix_rings)
    out_ring.finish()
    mixed_out[...] = (flags[:, 2:3] * (resid[...] + ffn_work[x].astype(FLOAT))).astype(HALF)
    mix_rings = chain(
        mix_rings,
        reduce_rings(here, mail, total, 0, MIX_PARTS, MIX_REDUCE, mix_near, mix_far, 2),
    )
    wait_all(copies)
    ffn_swap = mail.post(ffn_rest, ffn_mate, twin)
    ffn_owned[:, :, cut(core * FFN_HALF, FFN_HALF)] = ffn_rest[...].astype(FLOAT)
    relay_all(mix_rings)
    ffn_swap.wait_recv()
    ffn_owned[:, :, cut((1 - core) * FFN_HALF, FFN_HALF)] = ffn_mate[...].astype(FLOAT)
    lines = pl.ds(pl.multiple_of(8 * core, 8), 8)
    for place in range(4):
        cols = slice(place * SLAB, (place + 1) * SLAB)
        for kind, target in enumerate((grad_gate, grad_up, grad_down)):
            target[:, cols] = ffn_owned[place, lines, kind * SLAB : (kind + 1) * SLAB]
    finish_all(mix_rings)
    own_sum = blocks(total, here.at, slice(None))
    mix_swap = mail.post(own_sum, mix_mate, twin)
    mix_owned[:, cut(core * MIX_HALF, MIX_HALF)] = own_sum[...].astype(FLOAT)
    mix_swap.wait_recv()
    mix_owned[:, cut((1 - core) * MIX_HALF, MIX_HALF)] = mix_mate[...].astype(FLOAT)
    for half in range(2):
        at = half * MIX_HALF
        for which in range(3):
            start = which * D + half * HALF_D
            grad_in[:, start : start + HALF_D] = mix_owned[
                lines, at + which * HALF_D : at + (which + 1) * HALF_D
            ]
        grad_out[:, half * HALF_D : (half + 1) * HALF_D] = mix_owned[lines, at + OUT_AT : at + SMALL_AT]
    grad_small[...] = mix_owned[lines, SMALL_AT:MIX_HALF]
    mail.settle(len(mail.posted))


def write_kernel(*refs):
    count = (len(refs) - 2) // 2
    ins, outs = refs[:count], refs[count:]
    for source, target in zip(ins[:-1], outs):
        target[...] = source[...]
    small = jnp.transpose(ins[-1][...])
    outs[-3][...] = small[0:1, 0:8]
    outs[-2][...] = small[1:2, 0:8]
    outs[-1][...] = small[2:5, 0:8]


def vmem():
    return pl.BlockSpec(memory_space=pltpu.VMEM)


def sems(count):
    return pltpu.SemaphoreType.DMA((count,))


def params(number):
    return pltpu.CompilerParams(
        collective_id=number, has_side_effects=True, vmem_limit_bytes=VMEM_LIMIT
    )


def shape(dims, dtype):
    return jax.ShapeDtypeStruct(dims, dtype)


def whole_block(*operands):
    landing = [
        pltpu.VMEM(dims, HALF)
        for part in landing_shapes(MIX_PARTS, MIX_REDUCE) + landing_shapes(FFN_PARTS, FFN_REDUCE)
        for dims in part
    ]
    stream_landing = [pltpu.VMEM((TOK, D), HALF)] * 2 + [pltpu.VMEM((TOK // 2, D), HALF)] * 2
    return pl.pallas_call(
        block_kernel,
        out_shape=(
            shape((TOK, D), HALF),
            shape((TOK, D), HALF),
            shape((8, 3 * D), FLOAT),
            shape((8, D), FLOAT),
            shape((8, LANE), FLOAT),
            shape((8, 4 * SLAB), FLOAT),
            shape((8, 4 * SLAB), FLOAT),
            shape((8, 4 * SLAB), FLOAT),
        ),
        in_specs=[vmem()] * 10,
        out_specs=(vmem(),) * 8,
        scratch_shapes=[
            pltpu.VMEM((2, 16, OWN_COLS), HALF),
            pltpu.VMEM((16, MIX_COLS), FLOAT),
            pltpu.VMEM((4, 16, FFN_COLS), FLOAT),
            pltpu.VMEM((LANE, LANE), FLOAT),
            pltpu.VMEM((8, LANE), HALF),
            pltpu.VMEM((TOK, LANE), FLOAT),
            pltpu.VMEM((16, D), HALF),
            pltpu.VMEM((16, OWN_COLS), HALF),
            pltpu.VMEM((16, OWN_COLS), HALF),
            pltpu.VMEM((16, D), HALF),
            pltpu.VMEM(GRID + (16, MIX_COLS), HALF),
            pltpu.VMEM(GRID + (16, FFN_COLS), HALF),
            pltpu.VMEM((4, TOK, D), HALF),
            pltpu.VMEM((4, TOK, D), HALF),
            pltpu.VMEM((3, ALL, D), FLOAT),
            pltpu.VMEM((ALL, D), HALF),
            pltpu.VMEM((TOK, D), HALF),
            pltpu.VMEM((TOK, D), FLOAT),
            pltpu.VMEM((8, D), FLOAT),
            pltpu.VMEM((4 * TOK, FFN_COLS), HALF),
            pltpu.VMEM((2, 2, D, 4 * TOK), HALF),
            pltpu.VMEM(GRID + (16, MIX_HALF), HALF),
            pltpu.VMEM((16, MIX_HALF), HALF),
            pltpu.VMEM((4 * TOK, FFN_HALF), HALF),
            pltpu.VMEM((4, 16, FFN_HALF), HALF),
            pltpu.VMEM((4, 16, FFN_HALF), HALF),
            pltpu.VMEM((4, TOK, D), HALF),
            pltpu.VMEM((4, TOK, D), HALF),
            pltpu.VMEM((2, TOK, HALF_D), HALF),
            pltpu.VMEM((2, ALL, OUT_AT), HALF),
            pltpu.VMEM((ALL, D), FLOAT),
            pltpu.VMEM((LANE, D), FLOAT),
            pltpu.VMEM((4, D, ALL), HALF),
            pltpu.VMEM((ALL, D), HALF),
            pltpu.VMEM((TOK, D), HALF),
            pltpu.VMEM((TOK, HALF_D), HALF),
            pltpu.VMEM((ALL, OUT_AT), HALF),
            pltpu.VMEM((LANE, D), FLOAT),
            pltpu.VMEM((8, D), FLOAT),
            pltpu.VMEM((TOK, D), FLOAT),
        ]
        + stream_landing * 2
        + landing
        + [sems(176), sems(176), sems(2)],
        compiler_params=params(0),
        name="whole_block",
    )(*operands)


def local(
    tokens,
    gain_mix,
    in_weight,
    conv_weight,
    out_weight,
    gain_ffn,
    gate_weight,
    up_weight,
    down_weight,
    live_counts,
    positions,
    cotangent,
):
    vectors = jnp.concatenate([gain_mix[None], gain_ffn[None], conv_weight], axis=0)
    mixed_out, grad_tokens, grad_in, grad_out, grad_small, grad_gate, grad_up, grad_down = whole_block(
        in_weight, out_weight, gate_weight, up_weight, jnp.transpose(down_weight), vectors,
        tokens, positions.reshape(1, TOK), live_counts, cotangent,
    )
    plain = (mixed_out, grad_tokens, grad_in, grad_out, grad_gate, grad_up, grad_down)
    mixed_out, grad_tokens, grad_in, grad_out, grad_gate, grad_up, grad_down, one, two, taps = (
        pl.pallas_call(
            write_kernel,
            out_shape=tuple(shape(value.shape, value.dtype) for value in plain)
            + (
                shape((1, 8), FLOAT),
                shape((1, 8), FLOAT),
                shape((3, 8), FLOAT),
            ),
            in_specs=[vmem()] * 8,
            out_specs=(vmem(),) * 10,
            name="write",
            compiler_params=pltpu.CompilerParams(vmem_limit_bytes=VMEM_LIMIT),
        )(*plain, grad_small)
    )
    return (
        mixed_out,
        grad_tokens,
        one.reshape(8),
        grad_in,
        taps,
        grad_out,
        two.reshape(8),
        grad_gate,
        grad_up,
        jnp.transpose(grad_down),
    )


def solution(mesh):
    rows = P(("fsdp", "seq"), None)
    flat = P(("fsdp", "seq"))
    cols = P(None, ("fsdp", "seq"))
    return jax.shard_map(
        local,
        mesh=mesh,
        in_specs=(rows, flat, rows, cols, rows, flat, rows, rows, cols, P("fsdp", "seq"), flat, rows),
        out_specs=(rows, rows, flat, rows, cols, rows, flat, rows, rows, cols),
        check_vma=False,
    )
```

```python
import jax
import jax.numpy as jnp
from jax import lax
from jax.experimental import pallas as pl
from jax.experimental.pallas import tpu as pltpu
from jax.sharding import PartitionSpec as P

EPS = 1e-05
FLOAT = jnp.float32
HALF = jnp.bfloat16
MESH = pl.DeviceIdType.MESH
LANE = 128
D = 1024
SLAB = 1152
MIX_COLS = 34 * LANE
FFN_COLS = 28 * LANE
MIX_HALF = MIX_COLS // 2
FFN_HALF = FFN_COLS // 2
OWN_COLS = MIX_HALF + 4 * FFN_HALF
HALF_D = D // 2
OUT_AT = 3 * HALF_D
SMALL_AT = 4 * HALF_D
TILE = 256
TOK = 128
ALL = TOK + 16
MIX_PARTS = ((0, 6), (6, 6), (12, 5))
MIX_GATHER = (("y", "z", "x"), ("z", "x", "y"), ("x", "y", "z"))
MIX_REDUCE = (("x", "z", "y"), ("y", "x", "z"), ("z", "y", "x"))
FFN_PARTS = ((0, 8), (8, 6))
FFN_GATHER = (("y", "z"), ("z", "y"))
FFN_REDUCE = (("y", "z"), ("z", "y"))
GRID = (2, 4, 4, 2)
MIX_LANDING = 4 * 3 * len(MIX_PARTS)
VMEM_LIMIT = 60 * 2**20


class Here:
    def __init__(self):
        fsdp = lax.axis_index("fsdp")
        seq = lax.axis_index("seq")
        self.fsdp, self.seq = fsdp, seq
        self.at = {
            "x": lax.div(seq, 4),
            "y": lax.rem(fsdp, 4),
            "z": lax.div(fsdp, 4) * 2 + lax.rem(lax.div(seq, 2), 2),
        }
        self.core = lax.rem(seq, 2)

    def device(self, core, **moved):
        at = {**self.at, **moved}
        return (
            lax.div(at["z"], 2) * 4 + at["y"],
            (at["x"] * 2 + lax.rem(at["z"], 2)) * 2 + core,
        )

    def ring(self, axis, step):
        return lax.rem(self.at[axis] + (step + 4) % 4, 4)

    def beside(self, axis, step):
        return self.device(self.core, **{axis: self.ring(axis, step)})

    def twin(self):
        return self.device(1 - self.core)

    def along(self, step):
        return (self.fsdp, lax.rem(self.seq + (step + 16) % 16, 16))


def greet(devices):
    barrier = pltpu.get_barrier_semaphore()
    for device in devices:
        pl.semaphore_signal(barrier, inc=1, device_id=device, device_id_type=MESH)
    return barrier, len(devices)


class Mail:
    def __init__(self, send, recv):
        self.send, self.recv, self.posted, self.settled = send, recv, [], 0

    def post(self, src, dst, device):
        place = len(self.posted)
        copy = pltpu.make_async_remote_copy(
            src_ref=src,
            dst_ref=dst,
            send_sem=self.send.at[place],
            recv_sem=self.recv.at[place],
            device_id=device,
            device_id_type=MESH,
        )
        copy.start()
        self.posted.append(copy)
        return copy

    def settle(self, count):
        for copy in self.posted[self.settled : count]:
            copy.wait_send()
        self.settled = count


def cut(start, count):
    return pl.ds(pl.multiple_of(start, LANE), count)


def blocks(ref, at, cols):
    whole = slice(None)
    z = at["z"]
    high, low = (whole, whole) if z is None else (lax.div(z, 2), lax.rem(z, 2))
    y = whole if at["y"] is None else at["y"]
    x = whole if at["x"] is None else at["x"]
    return ref.at[high, y, x, low, :, cols]


class RingGather:
    def __init__(self, here, mail, axis, pick):
        self.here, self.mail, self.axis, self.pick = here, mail, axis, pick

    def start(self, source=None):
        here, axis = self.here, self.axis
        own = self.pick(here.at[axis], None)
        source = own if source is None else source
        self.to_up = self.mail.post(source, own, here.beside(axis, 1))
        self.to_down = self.mail.post(source, own, here.beside(axis, -1))

    def relay(self):
        here, axis = self.here, self.axis
        self.to_up.wait_recv()
        first = self.pick(here.ring(axis, -1), 0)
        self.far_up = self.mail.post(first, first, here.beside(axis, 1))
        self.to_down.wait_recv()
        second = self.pick(here.ring(axis, 1), 1)
        self.far_down = self.mail.post(second, second, here.beside(axis, -1))

    def finish(self):
        self.far_up.wait_recv()
        self.far_down.wait_recv()


class RingReduce:
    def __init__(self, here, mail, axis, pick, near, far):
        self.here, self.mail, self.axis, self.pick = here, mail, axis, pick
        self.near, self.far = near, far

    def start(self):
        here, axis = self.here, self.axis
        away = here.ring(axis, 2)
        self.far_up = self.mail.post(self.pick(away, 0), self.far[0], here.beside(axis, 1))
        self.far_down = self.mail.post(self.pick(away, 1), self.far[1], here.beside(axis, -1))

    def relay(self):
        here, axis = self.here, self.axis
        above, below = here.ring(axis, 1), here.ring(axis, -1)
        self.far_up.wait_recv()
        add_into(self.pick(above, 0), self.far[0])
        self.to_up = self.mail.post(self.pick(above, None), self.near[0], here.beside(axis, 1))
        self.far_down.wait_recv()
        add_into(self.pick(below, 1), self.far[1])
        self.to_down = self.mail.post(self.pick(below, None), self.near[1], here.beside(axis, -1))

    def finish(self):
        self.to_up.wait_recv()
        self.to_down.wait_recv()
        own = self.pick(self.here.at[self.axis], None)
        add_into(own, self.near[0], self.near[1])


class DirectGather(RingGather):
    def start(self, source=None):
        here, axis = self.here, self.axis
        own = self.pick(here.at[axis], None)
        source = own if source is None else source
        self.copies = [
            self.mail.post(source, own, here.beside(axis, step)) for step in (1, -1, 2)
        ]

    def relay(self):
        pass

    def finish(self):
        wait_all(self.copies)


class DirectReduce(RingReduce):
    def start(self):
        here, axis = self.here, self.axis
        self.landed = [self.near[0], self.near[1], self.far[0]]
        self.copies = [
            self.mail.post(
                self.pick(here.ring(axis, step), None), landed, here.beside(axis, step)
            )
            for step, landed in zip((1, -1, 2), self.landed)
        ]

    def relay(self):
        pass

    def finish(self):
        wait_all(self.copies)
        add_into(self.pick(self.here.at[self.axis], None), *self.landed)


def add_into(target, *terms):
    if len(terms) == 1:
        target[...] = target[...] + terms[0][...]
        return
    total = target[...].astype(FLOAT)
    for term in terms:
        total = total + term[...].astype(FLOAT)
    target[...] = total.astype(target.dtype)


def column_pick(ref, fixed, axis, start, chunks):
    split = (chunks + 1) // 2

    def pick(place, half):
        first, count = {None: (0, chunks), 0: (0, split), 1: (split, chunks - split)}[half]
        return blocks(ref, {**fixed, axis: place}, cut(start + first * LANE, count * LANE))

    return pick


def row_pick(ref):
    def pick(place, half):
        rows = ref.shape[-2]
        part = {None: slice(None), 0: pl.ds(0, rows // 2), 1: pl.ds(rows // 2, rows // 2)}[half]
        return ref.at[place, part]

    return pick


def gather_rings(here, mail, ref, base, parts, orders, stage, kind=RingGather):
    rings = []
    for (first, chunks), order in zip(parts, orders):
        fixed = dict(here.at)
        for axis in ("x", "y", "z"):
            if axis not in order or axis in order[:stage]:
                fixed[axis] = None
        pick = column_pick(ref, fixed, order[stage], base + first * LANE, chunks)
        rings.append(kind(here, mail, order[stage], pick))
    return rings


def start_all(rings):
    for ring in rings:
        ring.start()


def relay_all(rings):
    for ring in rings:
        ring.relay()


def finish_all(rings):
    for ring in rings:
        ring.finish()


def chain(rings, later):
    for ring, following in zip(rings, later):
        ring.finish()
        following.start()
    return later


def swap_pieces(here, mail, rings, steps):
    copies = []
    for ring in rings:
        for step in steps:
            piece = ring.pick(here.ring(ring.axis, step), None)
            copies.append(mail.post(piece, piece, here.twin()))
    return copies


def wait_all(copies):
    for copy in copies:
        copy.wait_recv()


def near_list(here, axes):
    return [here.beside(axis, step) for axis in axes for step in (1, -1)]


def mat(ref, cols):
    block = ref[:, :, :, :, :, cols]
    return block.reshape(D, block.shape[-1])


def mat_rows(ref, tile, cols):
    block = ref[lax.div(tile, 2), pl.ds(lax.rem(tile, 2) * 2, 2), :, :, :, cols]
    return block.reshape(TILE, block.shape[-1])


def mix_cols(tile, which):
    return cut(lax.div(tile, 2) * MIX_HALF + which * HALF_D + lax.rem(tile, 2) * TILE, TILE)


def dot(left, right):
    return jnp.dot(left, right, preferred_element_type=FLOAT)


def dot_nt(left, right):
    return lax.dot_general(
        left, right, (((1,), (1,)), ((), ())), preferred_element_type=FLOAT
    )


def norm_scale(values):
    return lax.rsqrt(jnp.mean(values * values, axis=-1, keepdims=True) + EPS)


def norm_back(normal, row_scale, gain_row, upstream):
    weighted = upstream * gain_row
    return row_scale * (
        weighted - normal * jnp.mean(weighted * normal, axis=-1, keepdims=True)
    )


def row_index(rows, cols):
    return lax.broadcasted_iota(jnp.int32, (rows, cols), 0)


def conv_terms(mixed, halo):
    rows = row_index(TOK, mixed.shape[1])
    one = pltpu.roll(mixed, 1, 0)
    two = pltpu.roll(mixed, 2, 0)
    one = jnp.where(rows == 0, halo[1:2], one)
    two = jnp.where(rows == 0, halo[0:1], jnp.where(rows == 1, halo[1:2], two))
    return one, two


def follows_of(here):
    return jnp.minimum(here.seq, 1).astype(FLOAT)


def mixer_forward(here, tokens, halo, flags, mix, proj, normed, gated, resid, rows, two):
    small = jnp.transpose(mat(mix, slice(SMALL_AT, SMALL_AT + LANE)).astype(FLOAT))
    rows[...] = small[0:8]
    gain = rows[0:1]
    x = tokens[...].astype(FLOAT)
    normed[0:TOK] = (x * norm_scale(x) * gain).astype(HALF)
    before = halo[...].astype(FLOAT)
    normed[TOK:ALL] = (before * norm_scale(before) * gain).astype(HALF)
    follows = follows_of(here)
    first_ok, second_ok = flags[:, 0:1], flags[:, 1:2]

    @pl.loop(0, D // TILE)
    def _(tile):
        feats = cut(tile * TILE, TILE)
        parts = [dot(normed[...], mat(mix, mix_cols(tile, which))) for which in range(3)]
        for which in range(3):
            proj[which, :, feats] = parts[which]
        mixed = parts[0] * parts[2]
        own = mixed[0:TOK]
        one, second = conv_terms(own, mixed[TOK:ALL] * follows)
        conv = (
            rows[2:3, feats] * own
            + first_ok * rows[3:4, feats] * one
            + second_ok * rows[4:5, feats] * second
        )
        gated[:, feats] = (parts[1][0:TOK] * conv).astype(HALF)

    @pl.loop(0, D // TILE)
    def _(tile):
        feats = cut(tile * TILE, TILE)
        branch = dot(gated[...], mat(mix, mix_cols(tile, 3)))
        resid[:, feats] = tokens[:, feats].astype(FLOAT) + branch

    value = resid[...]
    two[...] = (value * norm_scale(value) * rows[1:2]).astype(HALF)


def reduce_rings(here, mail, ref, base, parts, orders, near, far, stage):
    rings = []
    for number, ((first, chunks), order) in enumerate(zip(parts, orders)):
        fixed = {"x": None, "y": None, "z": None}
        for axis in order[:stage]:
            fixed[axis] = here.at[axis]
        pick = column_pick(ref, fixed, order[stage], base + first * LANE, chunks)
        kind = RingReduce if stage <= 1 else DirectReduce
        rings.append(kind(here, mail, order[stage], pick, near[number][stage], far[number][stage]))
    return rings


def landing_shapes(parts, orders):
    shapes = []
    for (_, chunks), order in zip(parts, orders):
        split = (chunks + 1) // 2
        done = []
        for stage in range(len(order)):
            gone = order[: stage + 1]
            lead = ()
            if "z" not in gone:
                lead += (2,)
            if "y" not in gone:
                lead += (4,)
            if "x" not in gone:
                lead += (4,)
            if "z" not in gone:
                lead += (2,)
            done += [lead + (16, chunks * LANE)] * 2
            if stage <= 1:
                done += [lead + (16, split * LANE), lead + (16, (chunks - split) * LANE)]
            else:
                done += [lead + (16, chunks * LANE), (16, LANE)]
        shapes.append(done)
    return shapes


def landing_refs(orders, refs):
    near, far = [], []
    place = 0
    for order in orders:
        near.append([])
        far.append([])
        for _ in order:
            near[-1].append(refs[place : place + 2])
            far[-1].append(refs[place + 2 : place + 4])
            place += 4
    return near, far


def ffn_hidden(ffn, twos, backs, acts, start, width):
    value = twos[...].reshape(4 * TOK, D)
    gate = dot(value, mat(ffn, cut(start, width)))
    upper = dot(value, mat(ffn, cut(SLAB + start, width)))
    d_active = dot(backs[...].reshape(4 * TOK, D), mat(ffn, cut(2 * SLAB + start, width)))
    sig = jax.nn.sigmoid(gate)
    swish = gate * sig
    acts[:, cut(start, width)] = (d_active * upper * (sig * (1.0 + gate * (1.0 - sig)))).astype(HALF)
    acts[:, cut(SLAB + start, width)] = (d_active * swish).astype(HALF)
    acts[:, cut(2 * SLAB + start, width)] = (swish * upper).astype(HALF)


def ffn_tokens(ffn, acts, target, kinds):
    @pl.loop(0, D // TILE)
    def _(tile):
        total = 0.0
        for kind in kinds:
            cols = slice(kind * SLAB, (kind + 1) * SLAB)
            total += dot_nt(acts[:, cols], mat_rows(ffn, tile, cols))
        target[:, :, cut(tile * TILE, TILE)] = total.astype(HALF).reshape(4, TOK, TILE)


def ffn_weight_grads(ffn, acts, acts_in, turned, half, part):
    first, chunks = part

    @pl.loop(first * LANE // TILE, (first + chunks) * LANE // TILE)
    def _(tile):
        cols = cut(half * FFN_HALF + tile * TILE, TILE)
        side = half * jnp.minimum(lax.div(tile, 2), 1)
        value = dot(turned[0, side], acts[:, cols])
        value += dot(turned[1, side], acts_in[:, cut(tile * TILE, TILE)])
        ffn[:, :, :, :, :, cols] = value.astype(HALF).reshape(GRID + (16, TILE))


def turn(target, value):
    target[...] = jnp.transpose(value.astype(FLOAT)).astype(HALF)


def mixer_backward(here, flags, mix, proj, rows, branch, grads, small):
    follows = follows_of(here)
    first_ok, second_ok = flags[:, 0:1], flags[:, 1:2]

    @pl.loop(0, D // TILE)
    def _(tile):
        feats = cut(tile * TILE, TILE)
        gated = dot_nt(branch[0], mat_rows(mix, tile, slice(OUT_AT, OUT_AT + HALF_D)))
        gated += dot_nt(
            branch[1], mat_rows(mix, tile, slice(MIX_HALF + OUT_AT, MIX_HALF + OUT_AT + HALF_D))
        )
        b_all, c_all, v_all = (proj[which, :, feats] for which in range(3))
        mixed = b_all * v_all
        own = mixed[0:TOK]
        one, second = conv_terms(own, mixed[TOK:ALL] * follows)
        tap_one, tap_two = rows[3:4, feats], rows[4:5, feats]
        conv = rows[2:3, feats] * own + first_ok * tap_one * one + second_ok * tap_two * second
        d_c = gated * conv
        d_conv = gated * c_all[0:TOK]
        small[2:3, feats] = jnp.sum(d_conv * own, axis=0, keepdims=True)
        small[3:4, feats] = jnp.sum(d_conv * first_ok * one, axis=0, keepdims=True)
        small[4:5, feats] = jnp.sum(d_conv * second_ok * second, axis=0, keepdims=True)
        term_one = first_ok * tap_one * d_conv
        term_two = second_ok * tap_two * d_conv
        lines = row_index(TOK, TILE)
        zero = jnp.zeros((TOK, TILE), FLOAT)
        d_mixed = (
            rows[2:3, feats] * d_conv
            + jnp.where(lines < TOK - 1, pltpu.roll(term_one, TOK - 1, 0), zero)
            + jnp.where(lines < TOK - 2, pltpu.roll(term_two, TOK - 2, 0), zero)
        )
        lines = row_index(16, TILE)
        zero = jnp.zeros((16, TILE), FLOAT)
        d_halo = follows * (
            jnp.where(lines < 2, term_two[0:16], zero)
            + jnp.where(lines == 1, pltpu.roll(term_one[0:16], 1, 0), zero)
        )
        half, place = lax.div(tile, 2), lax.rem(tile, 2) * TILE
        for which, (main, edge) in enumerate(
            (
                (d_mixed * v_all[0:TOK], d_halo * v_all[TOK:ALL]),
                (d_c, zero),
                (d_mixed * b_all[0:TOK], d_halo * b_all[TOK:ALL]),
            )
        ):
            cols = cut(which * HALF_D + place, TILE)
            grads[half, 0:TOK, cols] = main.astype(HALF)
            grads[half, TOK:ALL, cols] = edge.astype(HALF)


def projection_back(mix, grads, normed_grad):
    @pl.loop(0, D // TILE)
    def _(tile):
        total = dot_nt(grads[0], mat_rows(mix, tile, slice(0, OUT_AT)))
        total += dot_nt(grads[1], mat_rows(mix, tile, slice(MIX_HALF, MIX_HALF + OUT_AT)))
        normed_grad[:, cut(tile * TILE, TILE)] = total


def mixer_weight_grads(here, grads, branch, turned, grads_in, branch_in, total, rings):
    def put(cols, value):
        total[:, :, :, :, :, cols] = value.astype(HALF).reshape(GRID + (16, TILE))

    for ring, (first, chunks) in zip(rings[:2], MIX_PARTS):

        @pl.loop(first * LANE // TILE, (first + chunks) * LANE // TILE)
        def _(tile):
            cols = cut(tile * TILE, TILE)
            put(cols, dot(turned[0], grads[here.core, :, cols]) + dot(turned[1], grads_in[:, cols]))

        ring.start()

    @pl.loop(0, HALF_D // TILE)
    def _(tile):
        cols = cut(tile * TILE, TILE)
        value = dot(turned[2, :, 0:TOK], branch[here.core, :, cols])
        value += dot(turned[3, :, 0:TOK], branch_in[:, cols])
        put(cut(OUT_AT + tile * TILE, TILE), value)


def twice(value):
    value = value.astype(FLOAT)
    return jnp.concatenate([value, value], axis=0).astype(HALF)


def lay_out(own, in_rows, out_rows, gate_rows, up_rows, down_rows, small_rows):
    for half in range(2):
        for which in range(3):
            start = which * D + half * HALF_D
            own[half, :, which * HALF_D : (which + 1) * HALF_D] = twice(
                in_rows[:, start : start + HALF_D]
            )
        own[half, :, OUT_AT:SMALL_AT] = twice(out_rows[:, half * HALF_D : (half + 1) * HALF_D])
        own[half, :, SMALL_AT:MIX_HALF] = twice(small_rows[...])
    early = FFN_HALF - SLAB
    rest = SLAB - early
    for place in range(4):
        at, start = MIX_HALF + place * FFN_HALF, place * SLAB
        own[0, :, at : at + SLAB] = twice(gate_rows[:, start : start + SLAB])
        own[0, :, at + SLAB : at + FFN_HALF] = twice(up_rows[:, start : start + early])
        own[1, :, at : at + rest] = twice(up_rows[:, start + early : start + SLAB])
        own[1, :, at + rest : at + rest + SLAB] = twice(down_rows[:, start : start + SLAB])
        own[1, :, at + rest + SLAB : at + FFN_HALF] = jnp.zeros((16, LANE), HALF)


def lay_flags(board, flags, tail, tokens, positions, counts):
    slots = lax.broadcasted_iota(jnp.int32, (1, LANE), 1)
    place, count = positions[...], jnp.broadcast_to(counts[...], (1, LANE))

    def bit(condition):
        return jnp.where(condition, jnp.ones((1, LANE), FLOAT), jnp.zeros((1, LANE), FLOAT))

    board[...] = jnp.zeros_like(board)
    board[0:1] = bit(place >= 1)
    board[1:2] = bit(place >= 2)
    board[2:3] = bit(slots < count)
    for row in (3, 16):
        board[row : row + 1] = bit(slots == count - 2)
        board[row + 1 : row + 2] = bit(slots == count - 1)
    flags[...] = jnp.transpose(board[...])
    tail[...] = dot(board[16:32].astype(HALF), tokens[...]).astype(HALF)


def lay_small(board, small_rows, vectors):
    board[...] = jnp.zeros_like(board)
    board[0:5, 0:8] = vectors[...].astype(FLOAT)
    small_rows[...] = jnp.transpose(board[...])[0:8].astype(HALF)


def block_kernel(
    in_rows, out_rows, gate_rows, up_rows, down_rows, vectors, tokens, positions, counts, cotangent,
    mixed_out, grad_tokens, grad_in, grad_out, grad_small, grad_gate, grad_up, grad_down,
    own, mix_owned, ffn_owned, board, small_rows, flags, tail,
    mate, full, halo, mix, ffn, twos, backs, proj, normed, gated, resid, rows, acts, turned_ffn,
    total, mix_mate, acts_in, ffn_rest, ffn_mate, work, ffn_work,
    branch, grads, d_normed, small, turned, normed_in, gated_in, branch_in, grads_in, small_in,
    edge_in, d_resid, *scratch,
):
    two_near, two_far = scratch[0:2], scratch[2:4]
    out_near, out_far = scratch[4:6], scratch[6:8]
    *landing, send, recv, local_sem = scratch[8:]
    mix_near, mix_far = landing_refs(MIX_REDUCE, landing[:MIX_LANDING])
    ffn_near, ffn_far = landing_refs(FFN_REDUCE, landing[MIX_LANDING:])
    here = Here()
    mail = Mail(send, recv)
    x, core = here.at["x"], here.core
    twin = here.twin()
    barrier, count = greet(
        near_list(here, ("x", "y", "z"))
        + [here.beside(axis, 2) for axis in ("x", "y", "z")]
        + [twin, here.along(1), here.along(-1)]
    )
    lay_flags(board, flags, tail, tokens, positions, counts)
    lay_small(board, small_rows, vectors)
    lay_out(own, in_rows, out_rows, gate_rows, up_rows, down_rows, small_rows)
    pl.semaphore_wait(barrier, count)
    rows_in = mail.post(own.at[1 - core], mate, twin)
    halo_in = mail.post(tail, halo, here.along(1))
    backs[x] = (flags[:, 2:3] * cotangent[...].astype(FLOAT)).astype(HALF)
    acts[:, 3 * SLAB : FFN_COLS] = jnp.zeros((4 * TOK, FFN_COLS - 3 * SLAB), HALF)
    rows_in.wait_recv()
    mine = lax.broadcasted_iota(jnp.int32, (16, OWN_COLS), 0) // 8 == core
    full[...] = jnp.where(mine, own[core].astype(FLOAT), mate[...].astype(FLOAT)).astype(HALF)

    mix_base, ffn_base = core * MIX_HALF, core * FFN_HALF
    ffn_own = blocks(ffn, here.at, cut(ffn_base, FFN_HALF))

    def slab(place):
        return full.at[:, cut(MIX_HALF + place * FFN_HALF, FFN_HALF)]

    rings = gather_rings(here, mail, mix, mix_base, MIX_PARTS, MIX_GATHER, 0, DirectGather)
    for ring, (first, chunks) in zip(rings, MIX_PARTS):
        ring.start(full.at[:, first * LANE : (first + chunks) * LANE])
    slabs = [
        mail.post(slab(here.ring("x", step)), ffn_own, here.beside("x", step)) for step in (1, 3, 2)
    ]
    keep_mix = pltpu.make_async_copy(
        full.at[:, 0:MIX_HALF], blocks(mix, here.at, cut(mix_base, MIX_HALF)), local_sem.at[0]
    )
    keep_slab = pltpu.make_async_copy(slab(x), ffn_own, local_sem.at[1])
    keep_mix.start()
    keep_slab.start()
    keep_mix.wait()
    mix_rings = chain(
        rings,
        gather_rings(here, mail, mix, mix_base, MIX_PARTS, MIX_GATHER, 1, DirectGather),
    )
    keep_slab.wait()
    wait_all(slabs)
    ffn_rings = gather_rings(here, mail, ffn, ffn_base, FFN_PARTS, FFN_GATHER, 0)
    start_all(ffn_rings)
    mix_rings = chain(
        mix_rings, gather_rings(here, mail, mix, mix_base, MIX_PARTS, MIX_GATHER, 2)
    )
    swaps = swap_pieces(here, mail, mix_rings, (0,))
    relay_all(ffn_rings)
    relay_all(mix_rings)
    swaps += swap_pieces(here, mail, mix_rings, (1, -1))
    stream = RingGather(here, mail, "x", row_pick(backs))
    stream.start()
    finish_all(ffn_rings)
    ffn_rings = gather_rings(here, mail, ffn, ffn_base, FFN_PARTS, FFN_GATHER, 1)
    start_all(ffn_rings)
    for ring in mix_rings:
        ring.finish()
        swaps += swap_pieces(here, mail, [ring], (2,))
    stream.relay()
    ffn_swaps = swap_pieces(here, mail, ffn_rings, (0,))
    wait_all(swaps)
    halo_in.wait_recv()
    mixer_forward(here, tokens, halo, flags, mix, proj, normed, gated, resid, rows, twos.at[x])
    two_ring = RingGather(here, mail, "x", row_pick(twos))
    two_ring.start()
    relay_all(ffn_rings)
    ffn_swaps += swap_pieces(here, mail, ffn_rings, (1, -1))
    early = [mail.post(normed, normed_in, twin), mail.post(gated, gated_in, twin)]
    two_ring.relay()
    for step in (0, 1, -1):
        block = here.ring("x", step)
        turn(turned_ffn.at[0, 0, :, cut(block * TOK, TOK)], twos[block])
    turn(turned.at[0, :, 0:ALL], normed[...])
    turn(turned.at[2, :, 0:TOK], gated[...])
    finish_all(ffn_rings)
    ffn_swaps += swap_pieces(here, mail, ffn_rings, (2,))
    stream.finish()
    for block in range(4):
        turn(turned_ffn.at[0, 1, :, block * TOK : (block + 1) * TOK], backs[block])
    shared = [mail.post(turned_ffn.at[0, 1], turned_ffn.at[1, 1], twin)]
    wait_all(ffn_swaps)
    two_ring.finish()
    block = here.ring("x", 2)
    turn(turned_ffn.at[0, 0, :, cut(block * TOK, TOK)], twos[block])
    gathered = len(mail.posted)
    shared.append(mail.post(turned_ffn.at[0, 0], turned_ffn.at[1, 0], twin))

    @pl.loop(0, SLAB // TILE)
    def _(tile):
        ffn_hidden(ffn, twos, backs, acts, tile * TILE, TILE)

    ffn_hidden(ffn, twos, backs, acts, SLAB // TILE * TILE, SLAB % TILE)
    shared.append(
        mail.post(acts.at[:, cut((1 - core) * FFN_HALF, FFN_HALF)], acts_in, twin)
    )
    ffn_tokens(ffn, acts, work, (0, 1))
    two_ring = RingReduce(here, mail, "x", row_pick(work), two_near, two_far)
    two_ring.start()
    ffn_tokens(ffn, acts, ffn_work, (2,))
    two_ring.relay()
    mail.settle(gathered)
    wait_all(shared)
    ffn_rings = reduce_rings(here, mail, ffn, ffn_base, FFN_PARTS, FFN_REDUCE, ffn_near, ffn_far, 0)
    for part, ring in zip(FFN_PARTS, ffn_rings):
        ffn_weight_grads(ffn, acts, acts_in, turned_ffn, core, part)
        ring.start()
    two_ring.finish()
    value = resid[...]
    scale = norm_scale(value)
    unit = value * scale
    d_two = work[x].astype(FLOAT)
    small[...] = jnp.zeros_like(small)
    small[1:2] = jnp.sum(d_two * unit, axis=0, keepdims=True)
    d_value = flags[:, 2:3] * cotangent[...].astype(FLOAT) + norm_back(unit, scale, rows[1:2], d_two)
    d_resid[...] = d_value
    branch[0] = d_value[:, 0:HALF_D].astype(HALF)
    branch[1] = d_value[:, HALF_D:D].astype(HALF)
    late = [mail.post(branch.at[1 - core], branch_in, twin)]
    out_ring = RingReduce(here, mail, "x", row_pick(ffn_work), out_near, out_far)
    out_ring.start()
    mixer_backward(here, flags, mix, proj, rows, branch, grads, small)
    late.append(mail.post(grads.at[1 - core], grads_in, twin))
    relay_all(ffn_rings)
    out_ring.relay()
    projection_back(mix, grads, d_normed)
    x_own, x_edge = tokens[...].astype(FLOAT), halo[...].astype(FLOAT)
    scale = norm_scale(x_own)
    unit = x_own * scale
    small[0:1] = jnp.sum(d_normed[0:TOK] * unit, axis=0, keepdims=True) + jnp.sum(
        d_normed[TOK:ALL] * x_edge * norm_scale(x_edge), axis=0, keepdims=True
    )
    late.append(mail.post(small, small_in, twin))
    edge = mail.post(d_normed.at[pl.ds(TOK, 8)], edge_in, here.along(-1))
    wait_all(early)
    turn(turned.at[1, :, 0:ALL], normed_in[...])
    turn(turned.at[3, :, 0:TOK], gated_in[...])
    wait_all(late)
    mix_rings = reduce_rings(here, mail, total, 0, MIX_PARTS, MIX_REDUCE, mix_near, mix_far, 0)
    mixer_weight_grads(here, grads, branch, turned, grads_in, branch_in, total, mix_rings)
    small_sum = small[...] + small_in[...]
    total[:, :, :, :, :, SMALL_AT:MIX_HALF] = (
        jnp.transpose(small_sum).astype(HALF).reshape(GRID + (16, LANE))
    )
    mix_rings[2].start()
    ffn_rings = chain(
        ffn_rings,
        reduce_rings(here, mail, ffn, ffn_base, FFN_PARTS, FFN_REDUCE, ffn_near, ffn_far, 1),
    )
    relay_all(mix_rings)
    relay_all(ffn_rings)
    edge.wait_recv()
    d_first = (
        d_normed[0:TOK] + flags[:, 3:4] * edge_in[0:1] + flags[:, 4:5] * edge_in[1:2]
    )
    grad_tokens[...] = (d_resid[...] + norm_back(unit, scale, rows[0:1], d_first)).astype(HALF)
    mix_rings = chain(
        mix_rings,
        reduce_rings(here, mail, total, 0, MIX_PARTS, MIX_REDUCE, mix_near, mix_far, 1),
    )
    finish_all(ffn_rings)
    copies = []
    for step in (1, 3, 2):
        there = here.ring("x", step)
        copies.append(
            mail.post(
                blocks(ffn, {**here.at, "x": there}, cut(ffn_base, FFN_HALF)),
                ffn_rest.at[x],
                here.beside("x", step),
            )
        )
    ffn_rest[x] = ffn_own[...]
    relay_all(mix_rings)
    out_ring.finish()
    mixed_out[...] = (flags[:, 2:3] * (resid[...] + ffn_work[x].astype(FLOAT))).astype(HALF)
    mix_rings = chain(
        mix_rings,
        reduce_rings(here, mail, total, 0, MIX_PARTS, MIX_REDUCE, mix_near, mix_far, 2),
    )
    wait_all(copies)
    ffn_swap = mail.post(ffn_rest, ffn_mate, twin)
    ffn_owned[:, :, cut(core * FFN_HALF, FFN_HALF)] = ffn_rest[...].astype(FLOAT)
    relay_all(mix_rings)
    ffn_swap.wait_recv()
    ffn_owned[:, :, cut((1 - core) * FFN_HALF, FFN_HALF)] = ffn_mate[...].astype(FLOAT)
    lines = pl.ds(pl.multiple_of(8 * core, 8), 8)
    for place in range(4):
        cols = slice(place * SLAB, (place + 1) * SLAB)
        for kind, target in enumerate((grad_gate, grad_up, grad_down)):
            target[:, cols] = ffn_owned[place, lines, kind * SLAB : (kind + 1) * SLAB]
    finish_all(mix_rings)
    own_sum = blocks(total, here.at, slice(None))
    mix_swap = mail.post(own_sum, mix_mate, twin)
    mix_owned[:, cut(core * MIX_HALF, MIX_HALF)] = own_sum[...].astype(FLOAT)
    mix_swap.wait_recv()
    mix_owned[:, cut((1 - core) * MIX_HALF, MIX_HALF)] = mix_mate[...].astype(FLOAT)
    for half in range(2):
        at = half * MIX_HALF
        for which in range(3):
            start = which * D + half * HALF_D
            grad_in[:, start : start + HALF_D] = mix_owned[
                lines, at + which * HALF_D : at + (which + 1) * HALF_D
            ]
        grad_out[:, half * HALF_D : (half + 1) * HALF_D] = mix_owned[lines, at + OUT_AT : at + SMALL_AT]
    grad_small[...] = mix_owned[lines, SMALL_AT:MIX_HALF]
    mail.settle(len(mail.posted))


def write_kernel(*refs):
    count = (len(refs) - 2) // 2
    ins, outs = refs[:count], refs[count:]
    for source, target in zip(ins[:-1], outs):
        target[...] = source[...]
    small = jnp.transpose(ins[-1][...])
    outs[-3][...] = small[0:1, 0:8]
    outs[-2][...] = small[1:2, 0:8]
    outs[-1][...] = small[2:5, 0:8]


def vmem():
    return pl.BlockSpec(memory_space=pltpu.VMEM)


def sems(count):
    return pltpu.SemaphoreType.DMA((count,))


def params(number):
    return pltpu.CompilerParams(
        collective_id=number, has_side_effects=True, vmem_limit_bytes=VMEM_LIMIT
    )


def shape(dims, dtype):
    return jax.ShapeDtypeStruct(dims, dtype)


def whole_block(*operands):
    landing = [
        pltpu.VMEM(dims, HALF)
        for part in landing_shapes(MIX_PARTS, MIX_REDUCE) + landing_shapes(FFN_PARTS, FFN_REDUCE)
        for dims in part
    ]
    stream_landing = [pltpu.VMEM((TOK, D), HALF)] * 2 + [pltpu.VMEM((TOK // 2, D), HALF)] * 2
    return pl.pallas_call(
        block_kernel,
        out_shape=(
            shape((TOK, D), HALF),
            shape((TOK, D), HALF),
            shape((8, 3 * D), FLOAT),
            shape((8, D), FLOAT),
            shape((8, LANE), FLOAT),
            shape((8, 4 * SLAB), FLOAT),
            shape((8, 4 * SLAB), FLOAT),
            shape((8, 4 * SLAB), FLOAT),
        ),
        in_specs=[vmem()] * 10,
        out_specs=(vmem(),) * 8,
        scratch_shapes=[
            pltpu.VMEM((2, 16, OWN_COLS), HALF),
            pltpu.VMEM((16, MIX_COLS), FLOAT),
            pltpu.VMEM((4, 16, FFN_COLS), FLOAT),
            pltpu.VMEM((LANE, LANE), FLOAT),
            pltpu.VMEM((8, LANE), HALF),
            pltpu.VMEM((TOK, LANE), FLOAT),
            pltpu.VMEM((16, D), HALF),
            pltpu.VMEM((16, OWN_COLS), HALF),
            pltpu.VMEM((16, OWN_COLS), HALF),
            pltpu.VMEM((16, D), HALF),
            pltpu.VMEM(GRID + (16, MIX_COLS), HALF),
            pltpu.VMEM(GRID + (16, FFN_COLS), HALF),
            pltpu.VMEM((4, TOK, D), HALF),
            pltpu.VMEM((4, TOK, D), HALF),
            pltpu.VMEM((3, ALL, D), FLOAT),
            pltpu.VMEM((ALL, D), HALF),
            pltpu.VMEM((TOK, D), HALF),
            pltpu.VMEM((TOK, D), FLOAT),
            pltpu.VMEM((8, D), FLOAT),
            pltpu.VMEM((4 * TOK, FFN_COLS), HALF),
            pltpu.VMEM((2, 2, D, 4 * TOK), HALF),
            pltpu.VMEM(GRID + (16, MIX_HALF), HALF),
            pltpu.VMEM((16, MIX_HALF), HALF),
            pltpu.VMEM((4 * TOK, FFN_HALF), HALF),
            pltpu.VMEM((4, 16, FFN_HALF), HALF),
            pltpu.VMEM((4, 16, FFN_HALF), HALF),
            pltpu.VMEM((4, TOK, D), HALF),
            pltpu.VMEM((4, TOK, D), HALF),
            pltpu.VMEM((2, TOK, HALF_D), HALF),
            pltpu.VMEM((2, ALL, OUT_AT), HALF),
            pltpu.VMEM((ALL, D), FLOAT),
            pltpu.VMEM((LANE, D), FLOAT),
            pltpu.VMEM((4, D, ALL), HALF),
            pltpu.VMEM((ALL, D), HALF),
            pltpu.VMEM((TOK, D), HALF),
            pltpu.VMEM((TOK, HALF_D), HALF),
            pltpu.VMEM((ALL, OUT_AT), HALF),
            pltpu.VMEM((LANE, D), FLOAT),
            pltpu.VMEM((8, D), FLOAT),
            pltpu.VMEM((TOK, D), FLOAT),
        ]
        + stream_landing * 2
        + landing
        + [sems(176), sems(176), sems(2)],
        compiler_params=params(0),
        name="whole_block",
    )(*operands)


def local(
    tokens,
    gain_mix,
    in_weight,
    conv_weight,
    out_weight,
    gain_ffn,
    gate_weight,
    up_weight,
    down_weight,
    live_counts,
    positions,
    cotangent,
):
    vectors = jnp.concatenate([gain_mix[None], gain_ffn[None], conv_weight], axis=0)
    mixed_out, grad_tokens, grad_in, grad_out, grad_small, grad_gate, grad_up, grad_down = whole_block(
        in_weight, out_weight, gate_weight, up_weight, jnp.transpose(down_weight), vectors,
        tokens, positions.reshape(1, TOK), live_counts, cotangent,
    )
    plain = (mixed_out, grad_tokens, grad_in, grad_out, grad_gate, grad_up, grad_down)
    mixed_out, grad_tokens, grad_in, grad_out, grad_gate, grad_up, grad_down, one, two, taps = (
        pl.pallas_call(
            write_kernel,
            out_shape=tuple(shape(value.shape, value.dtype) for value in plain)
            + (
                shape((1, 8), FLOAT),
                shape((1, 8), FLOAT),
                shape((3, 8), FLOAT),
            ),
            in_specs=[vmem()] * 8,
            out_specs=(vmem(),) * 10,
            name="write",
            compiler_params=pltpu.CompilerParams(vmem_limit_bytes=VMEM_LIMIT),
        )(*plain, grad_small)
    )
    return (
        mixed_out,
        grad_tokens,
        one.reshape(8),
        grad_in,
        taps,
        grad_out,
        two.reshape(8),
        grad_gate,
        grad_up,
        jnp.transpose(grad_down),
    )


def solution(mesh):
    rows = P(("fsdp", "seq"), None)
    flat = P(("fsdp", "seq"))
    cols = P(None, ("fsdp", "seq"))
    return jax.shard_map(
        local,
        mesh=mesh,
        in_specs=(rows, flat, rows, cols, rows, flat, rows, rows, cols, P("fsdp", "seq"), flat, rows),
        out_specs=(rows, rows, flat, rows, cols, rows, flat, rows, rows, cols),
        check_vma=False,
    )
```
